256 devices in a mesh: section: 4 (over z_lo), seq: 64 (over z_hi, x, y, core).
Axes of the slice: x: 4, y: 4, z: 8 (z_hi: 2, z_lo: 4; z = z_hi * 4 + z_lo), core: 2. Of those that a mesh axis runs over, the one named last changes fastest.
Arguments:
- features: bfloat16 [1536, 32, 256], P('seq'), may hold values from -6 to 6
- conv_kernels: bfloat16 [4, 3, 3, 256, 256], P('section'), may hold values from -0.125 to 0.125
- patch_weights: bfloat16 [4, 4096, 1024], P('section'), may hold values from -0.1875 to 0.1875
- positions: int32 [48], replicated, may hold values from 0 to 3840
- out_cotangent: bfloat16 [1536, 32, 256], P('seq'), may hold values from -6 to 6
Outputs:
- weight_grads: float32 [4, 4096, 1024], P('section', 'seq')
The draws below stay inside these ranges and needn't reach their ends.
All inputs are finite; a program needn't handle non-finite values.
Results may differ from the reference program's by a relative error of at most 0.027.
Values may be sent and summed in bfloat16 or wider, within the bound.
No kernel may reach another device: no remote copies, remote signals or barrier semaphores. Data moves between devices by JAX's collectives and lax.ppermute only.
A program may use at most 128 MiB of HBM per device.

```python
import math
import jax
import jax.numpy as jnp
from jax import lax

D = 4096
C = 256
SIDE = 32
SEQ_LEN = 4096
P_SIZE = 1024
ROWS = 1536
IMAGES = 48
N_SECTION = 4


def place_ends(values, rng, smallest, top_value):
    index_at = [jax.random.randint(jax.random.fold_in(rng, axis), (), 0, length) for axis, length in enumerate(values.shape)]
    longest = values.shape.index(max(values.shape))
    beside = index_at[:longest] + [(index_at[longest] + 1) % values.shape[longest]] + index_at[longest + 1:]
    return values.at[tuple(index_at)].set(smallest).at[tuple(beside)].set(top_value)


def steps_of(rng, dims, split, low, largest):
    gain, own = 1.0, jax.random.fold_in(rng, 6)
    for position, shards_of in split:
        steps = jnp.exp(jax.random.uniform(jax.random.fold_in(own, position), (shards_of,), jnp.float32, low / len(split), largest / len(split)))
        gain = gain * jnp.repeat(steps, dims[position] // shards_of).reshape([-1 if axis == position else 1 for axis in range(len(dims))])
    return gain


def scatter_about(key, shape, spread, bound, cuts=(), kind=jnp.bfloat16):
    values = spread * jax.random.normal(key, shape, jnp.float32)
    if cuts:
        values = values * steps_of(key, shape, cuts, -0.22, 0.18)
    return jnp.clip(values, -bound, bound).astype(kind)


def setup_inputs(seed: int = 0) -> dict:
    arg_keys = jax.random.split(jax.random.key(seed), 6)
    features = scatter_about(arg_keys[0], (ROWS, SIDE, C), 1.0, 6.0, ((0, 64),))
    conv_kernels = scatter_about(arg_keys[1], (N_SECTION, 3, 3, C, C), (9 * C) ** -0.5, 0.125, ((0, 4),))
    patch_weights = scatter_about(arg_keys[2], (N_SECTION, D, P_SIZE), P_SIZE ** -0.5, 0.1875, ((0, 4),))
    positions = place_ends(jax.random.randint(arg_keys[3], (IMAGES,), 0, SEQ_LEN - SIDE * SIDE // 4 + 1), jax.random.fold_in(arg_keys[3], 1), 0, (SEQ_LEN - SIDE * SIDE // 4 + 1) - 1).astype(jnp.int32)
    out_cotangent = scatter_about(arg_keys[4], (ROWS, SIDE, C), 1.0, 6.0, ((0, 64),))
    return {"features": features, "conv_kernels": conv_kernels, "patch_weights": patch_weights, "positions": positions, "out_cotangent": out_cotangent}


NORM_EPS = 1e-05

def patchify(field):
    count, side, channels = field.shape
    blocks = field.reshape(count // 2, 2, side // 2, 2, channels).transpose(0, 2, 1, 3, 4)
    return blocks.reshape(count // 2 * (side // 2), 4 * channels)

def unpatchify(tokens, count, side):
    channels = tokens.shape[1] // 4
    blocks = tokens.reshape(count // 2, side // 2, 2, 2, channels).transpose(0, 2, 1, 3, 4)
    return blocks.reshape(count, side, channels)

def normed(tokens):
    scale = lax.rsqrt(lax.optimization_barrier(jnp.mean(tokens * tokens, axis=-1, keepdims=True)) + NORM_EPS)
    return (tokens * scale, scale)

def silu_slope(value):
    sigma = jax.nn.sigmoid(value)
    return sigma * (1.0 + value * (1.0 - sigma))

def norm_back(grad_out, tokens):
    normal, scale = normed(tokens)
    inner = grad_out * silu_slope(normal)
    return scale * (inner - normal * lax.optimization_barrier(jnp.mean(inner * normal, axis=-1, keepdims=True)))

def position_code(places, width):
    half = width // 2
    rates = jnp.exp(jnp.arange(half, dtype=jnp.float32) * (-math.log(10000.0) / half))
    angle = places.astype(jnp.float32)[:, None] * rates[None, :]
    return jnp.concatenate([jnp.sin(angle), jnp.cos(angle)], axis=1)

def stacked_taps(upper, middle, lower):
    pieces = []
    side = middle.shape[1]
    for part in (upper, middle, lower):
        wide = jnp.pad(part, ((0, 0), (1, 1), (0, 0)))
        pieces += [wide[:, 0:side], wide[:, 1:side + 1], wide[:, 2:side + 2]]
    return jnp.concatenate(pieces, axis=2)

def apply_taps(taps, kernel):
    count, side, depth = taps.shape
    result = jnp.dot(taps.reshape(count * side, depth), kernel, preferred_element_type=jnp.float32)
    return result.reshape(count, side, kernel.shape[1])

def conv_image(field, kernel):
    count = field.shape[0]
    padded = jnp.pad(field, ((1, 1), (0, 0), (0, 0)))
    return apply_taps(stacked_taps(padded[0:count], field, padded[2:count + 2]), kernel)

def image_grads(image, cotangent, start, weights, ahead, behind):
    side = image.shape[0]
    width = weights.shape[1]
    count = side // 2 * (side // 2)
    skip_field = conv_image(image, ahead[0]).astype(jnp.bfloat16)
    skip_patch = patchify(skip_field)
    places = start + jnp.arange(count, dtype=jnp.int32)
    embedded = jnp.dot(skip_patch, weights[0].T, preferred_element_type=jnp.float32)
    first_tokens = (embedded + position_code(places, width)).astype(jnp.bfloat16)
    first_normal, _ = normed(first_tokens.astype(jnp.float32))
    first_act = jax.nn.silu(first_normal).astype(jnp.bfloat16)
    first_lift = unpatchify(jnp.dot(first_act, weights[1], preferred_element_type=jnp.float32), side, side)
    first_input = jax.nn.silu(first_lift).astype(jnp.bfloat16)
    second_field = conv_image(first_input, ahead[1]).astype(jnp.bfloat16)
    second_input = jax.nn.silu(second_field.astype(jnp.float32)).astype(jnp.bfloat16)
    third_field = conv_image(second_input, ahead[2]).astype(jnp.bfloat16)
    third_patch = patchify(third_field)
    third_tokens = jnp.dot(third_patch, weights[2].T, preferred_element_type=jnp.float32).astype(jnp.bfloat16)
    last_normal, _ = normed(third_tokens.astype(jnp.float32))
    last_act = jax.nn.silu(last_normal).astype(jnp.bfloat16)
    last_lift = unpatchify(jnp.dot(last_act, weights[3], preferred_element_type=jnp.float32), side, side)
    last_lift = last_lift + skip_field.astype(jnp.float32)
    last_grad = (conv_image(cotangent, behind[3]) * silu_slope(last_lift)).astype(jnp.bfloat16)
    last_patch = patchify(last_grad)
    third_back = norm_back(jnp.dot(last_patch, weights[3].T, preferred_element_type=jnp.float32), third_tokens.astype(jnp.float32)).astype(jnp.bfloat16)
    third_lift = unpatchify(jnp.dot(third_back, weights[2], preferred_element_type=jnp.float32), side, side)
    third_lift = third_lift.astype(jnp.bfloat16)
    second_back = (conv_image(third_lift, behind[2]) * silu_slope(second_field.astype(jnp.float32))).astype(jnp.bfloat16)
    first_grad = (conv_image(second_back, behind[1]) * silu_slope(first_lift)).astype(jnp.bfloat16)
    first_patch = patchify(first_grad)
    first_back = norm_back(jnp.dot(first_patch, weights[1].T, preferred_element_type=jnp.float32), first_tokens.astype(jnp.float32)).astype(jnp.bfloat16)
    grads = [jnp.dot(first_back.T, skip_patch, preferred_element_type=jnp.float32), jnp.dot(first_act.T, first_patch, preferred_element_type=jnp.float32), jnp.dot(third_back.T, third_patch, preferred_element_type=jnp.float32), jnp.dot(last_act.T, last_patch, preferred_element_type=jnp.float32)]
    return jnp.stack(grads)

def reference(features, conv_kernels, patch_weights, positions, out_cotangent):
    side = features.shape[1]
    channels = features.shape[2]
    sections = conv_kernels.shape[0]
    images = features.shape[0] // side
    ahead = conv_kernels.reshape(sections, 9 * channels, channels)
    behind = jnp.transpose(conv_kernels[:, ::-1, ::-1], (0, 1, 2, 4, 3)).reshape(sections, 9 * channels, channels)
    image_stack = jnp.roll(features, side // 2, axis=0).reshape(images, side, side, channels)
    cot_stack = jnp.roll(out_cotangent, side // 2, axis=0).reshape(images, side, side, channels)

    def step(total, item):
        image, cotangent, start = item
        return (total + image_grads(image, cotangent, start, patch_weights, ahead, behind), None)
    total0 = jnp.zeros(patch_weights.shape, jnp.float32)
    total, _ = lax.scan(step, total0, (image_stack, cot_stack, positions))
    count = side // 2 * (side // 2)
    return total * (1.0 / math.sqrt(images * count))
```

```python
import math

import jax
import jax.numpy as jnp
from jax import lax
from jax.experimental import pallas as pl
from jax.experimental.pallas import tpu as pltpu
from jax.sharding import PartitionSpec as P

NORM_EPS = 1e-05
BF16 = jnp.bfloat16
F32 = jnp.float32
SIDE = 32
HALF = SIDE // 2
C = 256
N_SEQ = 64
SEQ = "seq"

X1, X3, Y1, Y3, CORE, ZH = (1 << 3, 3 << 3, 1 << 1, 3 << 1, 1, 1 << 5)


def flip(value, mask):
    return lax.ppermute(value, SEQ, [(i, i ^ mask) for i in range(N_SEQ)])


def partner(value):
    return lax.ppermute(value, "section", [(0, 1), (1, 0), (2, 3), (3, 2)])


HOPS = [(1 * N_SEQ + q, 2 * N_SEQ + q) for q in range(N_SEQ)] + [
    (q, 3 * N_SEQ + (q ^ ZH)) for q in range(N_SEQ)
]


def hop_on(value):
    return lax.ppermute(value, ("section", SEQ), HOPS)


def hop_back(value):
    return lax.ppermute(value, ("section", SEQ), [(j, i) for i, j in HOPS])


def dot(left, right):
    return jnp.dot(left, right, preferred_element_type=F32)


def dot_nt(left, right):
    return lax.dot_general(left, right, (((1,), (1,)), ((), ())), preferred_element_type=F32)


def dot_tn(left, right):
    return lax.dot_general(left, right, (((0,), (0,)), ((), ())), preferred_element_type=F32)


def patchify(field):
    pairs = field.reshape(HALF, 2, HALF, 2 * C)
    return jnp.concatenate([pairs[:, 0], pairs[:, 1]], axis=-1).reshape(HALF * HALF, 4 * C)


def unpatchify(tokens):
    pairs = tokens.reshape(HALF, HALF, 4 * C)
    return jnp.stack([pairs[..., : 2 * C], pairs[..., 2 * C :]], axis=1).reshape(SIDE, HALF, 2 * C)


def silu_slope(value):
    sigma = jax.nn.sigmoid(value)
    return sigma * (1.0 + value * (1.0 - sigma))


CHUNKS = 8
VMEM = pl.BlockSpec(memory_space=pltpu.VMEM)
SMEM = pl.BlockSpec(memory_space=pltpu.SMEM)
ANY = pl.BlockSpec(memory_space=pl.ANY)


def conv_in_kernel(field, kernel_ref, left_ref, right_ref, turned=False):
    even, odd = field[..., :C], field[..., C:]
    column = lax.broadcasted_iota(jnp.int32, (SIDE, HALF, C), 1)
    before = jnp.where(column == 0, 0.0, pltpu.roll(odd, 1, 1))
    after = jnp.where(column == HALF - 1, 0.0, pltpu.roll(even, HALF - 1, 1))
    middle = field.astype(BF16)
    left_ref[1 : SIDE + 1, :, C:] = middle
    left_ref[1 : SIDE + 1, :, :C] = before.astype(BF16)
    right_ref[1 : SIDE + 1, :, : 2 * C] = middle
    right_ref[1 : SIDE + 1, :, 2 * C :] = after.astype(BF16)
    out = []
    for ref in (left_ref, right_ref):
        edge = jnp.zeros((HALF, 3 * C), BF16)
        ref[0] = edge
        ref[SIDE + 1] = edge
        total = None
        for row in range(3):
            taps = ref[row : row + SIDE].reshape(SIDE * HALF, 3 * C)
            if turned:
                for column in range(3):
                    tap = (2 - row) * 3 + 2 - column
                    weight = kernel_ref[tap * C : (tap + 1) * C]
                    term = dot_nt(taps[:, column * C : (column + 1) * C], weight)
                    total = term if total is None else total + term
            else:
                term = dot(taps, kernel_ref[row * 3 * C : (row + 1) * 3 * C])
                total = term if total is None else total + term
        out.append(total.reshape(SIDE, HALF, C))
    return jnp.concatenate(out, axis=-1)


def choose(to_ref, mine, own_ref, other_ref):
    @pl.when(mine)
    def _():
        to_ref[...] = own_ref[...]

    @pl.when(jnp.logical_not(mine))
    def _():
        to_ref[...] = other_ref[...]


def rounded(value):
    return value.astype(BF16).astype(F32)


def silu(value):
    return value * jax.nn.sigmoid(value)


class Weights:
    def __init__(self, index_ref, own_ref, near_ref, far_ref, parity):
        self.args = (index_ref, own_ref, near_ref, far_ref, parity)
        self.rows = own_ref.shape[0] // CHUNKS
        self.share = own_ref.shape[0] // N_SEQ

    def own_chunk(self, chunk):
        index_ref, own_ref = self.args[:2]
        per = N_SEQ // CHUNKS
        starts = [
            pl.multiple_of(index_ref[chunk * per + i] * self.share, self.share) for i in range(per)
        ]
        return jnp.concatenate([own_ref[pl.ds(start, self.share)] for start in starts], axis=0)

    def sweep(self, slot, step):
        _, _, near_ref, far_ref, parity = self.args

        @pl.when(parity == slot)
        def _():
            @pl.loop(0, CHUNKS)
            def _(chunk):
                step(chunk, self.own_chunk(chunk))

        @pl.when(parity != slot)
        def _():
            sweep_other(near_ref, far_ref, step)


def sweep_other(near_ref, far_ref, step):
    half = CHUNKS // 2
    rows = near_ref.shape[0] // half
    for first, ref in ((0, near_ref), (half, far_ref)):

        @pl.loop(0, half)
        def _(i, first=first, ref=ref):
            step(first + i, ref[pl.ds(pl.multiple_of(i * rows, rows), rows)])


def lanes(chunk, count):
    return pl.ds(pl.multiple_of(chunk * count, count), count)


TAPS = [pltpu.VMEM((SIDE + 2, HALF, 3 * C), BF16)] * 2
TOKENS = HALF * HALF
KERNEL = [pltpu.VMEM((9 * C, C), BF16)]
PARAMS = pltpu.CompilerParams(vmem_limit_bytes=40 * 1024 * 1024)


def call(body, outs, args):
    return pl.pallas_call(
        body,
        out_shape=[jax.ShapeDtypeStruct(shape, kind) for shape, kind in outs],
        in_specs=[VMEM] * len(args),
        out_specs=[VMEM] * len(outs),
        compiler_params=PARAMS,
    )(*args)


def run_start(section, phase, rows, late, near, kernels):
    def body(
        section_ref, phase_ref, rows_ref, late_ref, near_ref, own_kernel_ref, other_kernel_ref,
        skip_ref, start_ref, image_ref, left_ref, right_ref, kernel_ref,
    ):
        where, kind = section_ref[0], phase_ref[0]
        choose(kernel_ref, (where == 0) | (where == 3), own_kernel_ref, other_kernel_ref)

        @pl.when(kind == 0)
        def _():
            image_ref[:16] = late_ref[...]
            image_ref[16:] = rows_ref[:16]

        @pl.when(kind == 1)
        def _():
            image_ref[:8] = near_ref[...]
            image_ref[8:] = rows_ref[...]

        @pl.when(kind == 2)
        def _():
            image_ref[:24] = rows_ref[...]
            image_ref[24:] = near_ref[...]

        @pl.when(kind == 3)
        def _():
            image_ref[...] = jnp.zeros_like(image_ref)

        @pl.when(where < 2)
        def _():
            field = conv_in_kernel(image_ref[...], kernel_ref, left_ref, right_ref)
            skip_ref[...] = field.astype(BF16)

        @pl.when(where >= 2)
        def _():
            field = conv_in_kernel(image_ref[...], kernel_ref, left_ref, right_ref, turned=True)
            start_ref[...] = field

    shape = (SIDE, HALF, 2 * C)
    return pl.pallas_call(
        body,
        out_shape=[jax.ShapeDtypeStruct(shape, BF16), jax.ShapeDtypeStruct(shape, F32)],
        in_specs=[SMEM, SMEM] + [VMEM] * 5,
        out_specs=[VMEM] * 2,
        scratch_shapes=[pltpu.VMEM(shape, F32)] + TAPS + KERNEL,
        compiler_params=PARAMS,
        name="start",
    )(section, phase, rows, late, near, *kernels)


def run_piece(blocks, weight):
    share, depth = weight.shape[0] // N_SEQ, weight.shape[1]

    def body(index_ref, weight_ref, out_ref):
        out_ref[...] = weight_ref[...]

    return pl.pallas_call(
        body,
        grid_spec=pltpu.PrefetchScalarGridSpec(
            num_scalar_prefetch=1,
            grid=(2,),
            in_specs=[pl.BlockSpec((share, depth), lambda i, index: (index[i], 0))],
            out_specs=pl.BlockSpec((share, depth), lambda i, index: (i, 0)),
        ),
        out_shape=jax.ShapeDtypeStruct((2 * share, depth), weight.dtype),
    )(blocks, weight)


def gather_partner(piece):
    rows, depth = piece.shape
    half, part = depth // 2, depth // 4

    def split(piece_ref, first_ref, second_ref):
        first_ref[...] = piece_ref[:, :half]
        second_ref[...] = piece_ref[:, half:]

    shape = (rows, half)
    first, second = call(split, [(shape, BF16)] * 2, (piece,))
    got = [flip(first, m) for m in (X1, X1 ^ X3, X3)] + [flip(second, m) for m in (Y1, Y1 ^ Y3, Y3)]

    def stack(*refs):
        for side in range(2):
            for far in range(4):
                source = refs[side] if far == 0 else refs[2 + 3 * side + far - 1]
                refs[8 + side][far * rows : (far + 1) * rows] = source[...]

    shape = (4 * rows, half)
    wide = call(stack, [(shape, BF16)] * 2, (first, second, *got))
    rings = ((Y1, Y3), (X1, X3))
    near = [flip(value, ring[0]) for value, ring in zip(wide, rings)]
    far = [flip(value, ring[1]) for value, ring in zip(wide, rings)]

    def cut(*refs):
        for side in range(2):
            refs[4 + 2 * side][...] = refs[side][:, :part]
            refs[5 + 2 * side][...] = refs[2 + side][:, part:]

    shape = (4 * rows, part)
    parts = call(cut, [(shape, BF16)] * 4, (*far, *near))
    low = [flip(parts[2 * side], ring[0]) for side, ring in enumerate(rings)]
    high = [flip(parts[2 * side + 1], ring[1]) for side, ring in enumerate(rings)]

    def join(*refs):
        out_ref = refs[10]
        for side in range(2):
            base = side * half
            mine, one, three = refs[side], refs[2 + side], refs[4 + side]
            for outer in range(4):
                sources = {0: [mine], 1: [one], 3: [three], 2: [refs[6 + side], refs[8 + side]]}[outer]
                for j, source in enumerate(sources):
                    count = source.shape[1]
                    at = slice(base + j * count, base + (j + 1) * count)
                    for inner in range(4):
                        block = source[inner * rows : (inner + 1) * rows]
                        x, y = (inner, outer) if side == 0 else (outer, inner)
                        start = (4 * x + y) * rows
                        out_ref[start : start + rows, at] = block

    args = (*wide, *near, *far, *low, *high)
    return call(join, [((16 * rows, depth), BF16)], args)[0]


def run_forward(section, blocks, skip, own, near, far, codes, kernels):
    width, depth = own.shape
    cols = width // CHUNKS

    def body(
        section_ref, index_ref, skip_ref, own_ref, near_ref, far_ref, one_ref, two_ref, cos_ref,
        sin_ref, own_kernel_ref, other_kernel_ref, tokens_ref, act_ref, lift_ref, field_ref, sum_ref,
        left_ref, right_ref, kernel_ref,
    ):
        parity = section_ref[0] % 2

        @pl.when(section_ref[0] < 2)
        def _():
            weights = Weights(index_ref, own_ref, near_ref, far_ref, parity)
            choose(kernel_ref, parity == 1, own_kernel_ref, other_kernel_ref)
            patch = patchify(skip_ref[...])
            sum_ref[...] = jnp.zeros_like(sum_ref)

            def embed(chunk, rows):
                at = lanes(chunk, cols)
                code = one_ref[:, at][:, None] * cos_ref[:, at][None]
                code += two_ref[:, at][:, None] * sin_ref[:, at][None]
                value = dot_nt(patch, rows) + code.reshape(TOKENS, cols)
                value = value.astype(BF16)
                tokens_ref[:, at] = value
                value = value.astype(F32)
                sum_ref[...] += jnp.sum(value * value, axis=-1, keepdims=True)

            weights.sweep(0, embed)
            scale = lax.rsqrt(sum_ref[...] * (1.0 / width) + NORM_EPS)
            lift_ref[...] = jnp.zeros_like(lift_ref)

            def raise_up(chunk, rows):
                at = lanes(chunk, cols)
                active = silu(tokens_ref[:, at].astype(F32) * scale).astype(BF16)
                act_ref[:, at] = active
                lift_ref[...] += dot(active, rows)

            weights.sweep(1, raise_up)

            field = unpatchify(rounded(silu(lift_ref[...])))
            field_ref[...] = conv_in_kernel(field, kernel_ref, left_ref, right_ref).astype(BF16)

    return pl.pallas_call(
        body,
        out_shape=[
            jax.ShapeDtypeStruct((TOKENS, width), BF16),
            jax.ShapeDtypeStruct((TOKENS, width), BF16),
            jax.ShapeDtypeStruct((TOKENS, depth), F32),
            jax.ShapeDtypeStruct((SIDE, HALF, 2 * C), BF16),
        ],
        in_specs=[SMEM, SMEM] + [VMEM] * 10,
        out_specs=[VMEM] * 4,
        scratch_shapes=[pltpu.VMEM((TOKENS, 1), F32)] + TAPS + KERNEL,
        compiler_params=PARAMS,
        name="forward_first_pair",
    )(section, blocks, skip, own, near, far, *codes, *kernels)


def run_second_pair(section, blocks, second, skip, start, own, near, far, kernels):
    width, depth = own.shape
    cols = width // CHUNKS

    def body(
        section_ref, index_ref, second_ref, skip_ref, start_ref, own_ref, near_ref, far_ref,
        own_kernel_ref, other_kernel_ref, back_ref, side_ref, patch_ref, sum_ref, left_ref,
        right_ref, kernel_ref, tokens_ref, inner_ref, lift_ref,
    ):
        parity = section_ref[0] % 2

        @pl.when(section_ref[0] >= 2)
        def _():
            weights = Weights(index_ref, own_ref, near_ref, far_ref, parity)
            choose(kernel_ref, parity == 0, own_kernel_ref, other_kernel_ref)
            field = rounded(silu(second_ref[...].astype(F32)))
            field = conv_in_kernel(field, kernel_ref, left_ref, right_ref).astype(BF16)
            patch_ref[...] = patchify(field)
            sum_ref[...] = jnp.zeros_like(sum_ref)

            def embed(chunk, rows):
                value = dot_nt(patch_ref[...], rows).astype(BF16)
                tokens_ref[:, lanes(chunk, cols)] = value
                value = value.astype(F32)
                sum_ref[...] += jnp.sum(value * value, axis=-1, keepdims=True)

            weights.sweep(0, embed)
            scale = lax.rsqrt(sum_ref[...] * (1.0 / width) + NORM_EPS)
            lift_ref[...] = patchify(skip_ref[...]).astype(F32)

            def raise_up(chunk, rows):
                at = lanes(chunk, cols)
                active = silu(tokens_ref[:, at].astype(F32) * scale).astype(BF16)
                side_ref[:, at] = active
                lift_ref[...] += dot(active, rows)

            weights.sweep(1, raise_up)
            last_patch = (patchify(start_ref[...]) * silu_slope(lift_ref[...])).astype(BF16)

            @pl.when(parity == 1)
            def _():
                patch_ref[...] = last_patch

            sum_ref[...] = jnp.zeros_like(sum_ref)

            def descend(chunk, rows):
                at = lanes(chunk, cols)
                normal = tokens_ref[:, at].astype(F32) * scale
                inner = dot_nt(last_patch, rows) * silu_slope(normal)
                inner_ref[:, at] = inner
                sum_ref[...] += jnp.sum(inner * normal, axis=-1, keepdims=True)

            weights.sweep(1, descend)
            mean = sum_ref[...] * (1.0 / width)
            lift_ref[...] = jnp.zeros_like(lift_ref)

            def lower(chunk, rows):
                at = lanes(chunk, cols)
                normal = tokens_ref[:, at].astype(F32) * scale
                back = (scale * (inner_ref[:, at] - normal * mean)).astype(BF16)

                @pl.when(parity == 0)
                def _():
                    side_ref[:, at] = back

                lift_ref[...] += dot(back, rows)

            weights.sweep(0, lower)
            field = unpatchify(rounded(lift_ref[...]))
            field = conv_in_kernel(field, kernel_ref, left_ref, right_ref, turned=True)
            back_ref[...] = (field * silu_slope(second_ref[...].astype(F32))).astype(BF16)

    return pl.pallas_call(
        body,
        out_shape=[
            jax.ShapeDtypeStruct((SIDE, HALF, 2 * C), BF16),
            jax.ShapeDtypeStruct((TOKENS, width), BF16),
            jax.ShapeDtypeStruct((TOKENS, depth), BF16),
        ],
        in_specs=[SMEM, SMEM] + [VMEM] * 8,
        out_specs=[VMEM] * 3,
        scratch_shapes=[pltpu.VMEM((TOKENS, 1), F32)]
        + TAPS
        + KERNEL
        + [
            pltpu.VMEM((TOKENS, width), BF16),
            pltpu.VMEM((TOKENS, width), F32),
            pltpu.VMEM((TOKENS, depth), F32),
        ],
        compiler_params=PARAMS,
        name="second_pair",
    )(section, blocks, second, skip, start, own, near, far, *kernels)


def run_back(section, given, skip, lift, tokens, prior, patch, near, far, kernels):
    width, depth = tokens.shape[1], lift.shape[1]
    cols = width // CHUNKS

    def body(
        section_ref, given_ref, skip_ref, lift_ref, tokens_ref, prior_ref, known_ref, near_ref,
        far_ref, own_kernel_ref, other_kernel_ref, keep_ref, send_ref, patch_ref, sum_ref, left_ref,
        right_ref, kernel_ref, inner_ref,
    ):
        where = section_ref[0]

        @pl.when(where >= 1)
        def _():
            keep_ref[...] = prior_ref[:, : width // 2]
            send_ref[...] = prior_ref[:, width // 2 :]

        @pl.when(where >= 2)
        def _():
            patch_ref[...] = known_ref[...]

        @pl.when(where < 2)
        def _():
            choose(kernel_ref, where == 1, own_kernel_ref, other_kernel_ref)
            field = given_ref[...].astype(F32)
            field = conv_in_kernel(field, kernel_ref, left_ref, right_ref, turned=True)
            patch_ref[...] = (patchify(field) * silu_slope(lift_ref[...])).astype(BF16)

        @pl.when(where == 0)
        def _():
            sum_ref[...] = jnp.zeros_like(sum_ref)

            @pl.loop(0, CHUNKS)
            def _(chunk):
                value = tokens_ref[:, lanes(chunk, cols)].astype(F32)
                sum_ref[...] += jnp.sum(value * value, axis=-1, keepdims=True)

            scale = lax.rsqrt(sum_ref[...] * (1.0 / width) + NORM_EPS)
            sum_ref[...] = jnp.zeros_like(sum_ref)

            def descend(chunk, rows):
                at = lanes(chunk, cols)
                normal = tokens_ref[:, at].astype(F32) * scale
                inner = dot_nt(patch_ref[...], rows) * silu_slope(normal)
                inner_ref[:, at] = inner
                sum_ref[...] += jnp.sum(inner * normal, axis=-1, keepdims=True)

            sweep_other(near_ref, far_ref, descend)
            mean = sum_ref[...] * (1.0 / width)

            for first, ref in ((0, keep_ref), (CHUNKS // 2, send_ref)):

                @pl.loop(0, CHUNKS // 2)
                def _(i, first=first, ref=ref):
                    at = lanes(first + i, cols)
                    normal = tokens_ref[:, at].astype(F32) * scale
                    back = scale * (inner_ref[:, at] - normal * mean)
                    ref[:, lanes(i, cols)] = back.astype(BF16)

            patch_ref[...] = patchify(skip_ref[...])

    return pl.pallas_call(
        body,
        out_shape=[
            jax.ShapeDtypeStruct((TOKENS, width // 2), BF16),
            jax.ShapeDtypeStruct((TOKENS, width // 2), BF16),
            jax.ShapeDtypeStruct((TOKENS, depth), BF16),
        ],
        in_specs=[SMEM] + [VMEM] * 10,
        out_specs=[VMEM] * 3,
        scratch_shapes=[pltpu.VMEM((TOKENS, 1), F32)] + TAPS + KERNEL + [pltpu.VMEM((TOKENS, width), F32)],
        compiler_params=PARAMS,
        name="back_first_pair",
    )(section, given, skip, lift, tokens, prior, patch, near, far, *kernels)


SENT = {"a": (1, 2), "b": (3, 2)}
KEPT = {"a": (0, 3), "b": (0, 1)}


def run_partial(keep, recv, patch, patch_recv):
    half, depth = keep.shape[1], patch.shape[1]
    part, block = depth // 4, half // 16

    def body(keep_ref, recv_ref, patch_ref, other_ref, *out_refs):
        tokens = jnp.concatenate([keep_ref[...], recv_ref[...]], axis=0)
        patches = jnp.concatenate([patch_ref[...], other_ref[...]], axis=0)
        for column in range(4):
            name = "ab"[column % 2]
            sent_ref, kept_ref = out_refs[column], out_refs[4 + column]
            right = patches[:, column * part : (column + 1) * part]
            for i in range(2):
                for ref, far in ((sent_ref, SENT[name][i]), (kept_ref, KEPT[name][i])):
                    if column < 2:
                        left = tokens[:, far * 4 * block : (far + 1) * 4 * block]
                    else:
                        left = jnp.concatenate(
                            [tokens[:, (4 * j + far) * block :][:, :block] for j in range(4)], axis=1
                        )
                    ref[i] = dot_tn(left, right).astype(ref.dtype)

    shape = (2, 4 * block, part)
    outs = call(body, [(shape, BF16)] * 4 + [(shape, F32)] * 4, (keep, recv, patch, patch_recv))
    return outs[:4], outs[4:]


FIRST_RINGS = ((X1, X3), (X3, X1), (Y1, Y3), (Y3, Y1))


def run_sum(partial):
    sent, kept = partial
    got = [flip(value, ring[0]) for value, ring in zip(sent, FIRST_RINGS)]
    rows, part = kept[0].shape[1:]
    block = rows // 4

    def add_once(*refs):
        kept_refs, got_refs, sent_refs, out_refs = refs[:4], refs[4:8], refs[8:12], refs[12:]
        for kept_ref, got_ref, sent_ref, out_ref in zip(kept_refs, got_refs, sent_refs, out_refs):
            total = kept_ref[...] + got_ref[...].astype(F32)
            out_ref[...] = total[0]
            sent_ref[...] = total[1].astype(BF16)

    shape = (rows, part)
    outs = call(add_once, [(shape, BF16)] * 4 + [(shape, F32)] * 4, (*kept, *got))
    got = [flip(value, ring[1]) for value, ring in zip(outs[:4], FIRST_RINGS)]

    def add_twice(*refs):
        kept_refs, got_refs, out_refs = refs[:4], refs[4:8], refs[8:]
        for half in range(2):
            a, b = 2 * half, 2 * half + 1
            total = [kept_refs[i][...] + got_refs[i][...].astype(F32) for i in (a, b)]
            total = jnp.concatenate(total, axis=1)
            for far in range(4):
                ref = out_refs[4 * half + far]
                ref[...] = total[far * block : (far + 1) * block].astype(ref.dtype)

    shape = (block, 2 * part)
    kinds = [F32, BF16, BF16, BF16] * 2
    outs = call(add_twice, [(shape, kind) for kind in kinds], (*outs[4:], *got))
    got = [flip(v, m) for v, m in zip(outs[1:4], (Y1, Y1 ^ Y3, Y3))]
    got += [flip(v, m) for v, m in zip(outs[5:8], (X1, X1 ^ X3, X3))]

    def add_last(*refs):
        for half in range(2):
            total = refs[half][...]
            for ref in refs[2 + 3 * half : 5 + 3 * half]:
                total += ref[...].astype(F32)
            at = slice(half * 2 * part, (half + 1) * 2 * part)
            refs[8][:, at] = total[: block // 2]
            refs[9][:, at] = total[block // 2 :].astype(BF16)

    shape = (block // 2, 4 * part)
    mine, away = call(add_last, [(shape, F32), (shape, BF16)], (outs[0], outs[4], *got))
    return mine + flip(away, ZH).astype(F32)


def on_device(features, conv_kernels, patch_weights, positions, out_cotangent):
    weight = patch_weights[0]
    width, depth = weight.shape
    kernel = conv_kernels[0].reshape(9 * C, C)
    section = lax.axis_index("section")
    place = lax.axis_index(SEQ)
    first_pair = section < 2

    order = jnp.arange(N_SEQ, dtype=jnp.int32)
    away = ((order & 1) << 5) | (((order >> 3) & 3) << 3) | (((order >> 1) & 3) << 1) | (order >> 5)
    blocks = away ^ place

    here, phase = section.reshape(1), (place % 4).reshape(1)
    near = gather_partner(partner(run_piece(blocks, weight)))
    far = flip(near, CORE)
    kernels = (kernel, partner(kernel))

    across = lax.ppermute(
        out_cotangent, ("section", SEQ), [(q, 3 * N_SEQ + (q ^ ZH)) for q in range(N_SEQ)]
    )
    rows = jnp.where(first_pair, features, jnp.where(section == 3, across, out_cotangent))
    rows = rows.astype(F32).reshape(rows.shape[0], HALF, 2 * C)
    late = lax.ppermute(rows[8:], SEQ, [(4 * k + 3, (4 * k + 4) % N_SEQ) for k in range(N_SEQ // 4)])
    some = jnp.where(phase[0] == 0, rows[16:], rows[:8])
    pairs = [(4 * k, 4 * k + 1) for k in range(N_SEQ // 4)]
    pairs += [(4 * k + 3, 4 * k + 2) for k in range(N_SEQ // 4)]
    beside = lax.ppermute(some, SEQ, pairs)
    skip_field, start = run_start(here, phase, rows, late, beside, kernels)
    skip_recv = hop_on(skip_field)

    image_id = jnp.minimum(3 * (place // 4) + place % 4, positions.shape[0] - 1)
    begin = positions[image_id]
    half = width // 2
    feature = (blocks[:, None] * (width // N_SEQ) + jnp.arange(width // N_SEQ)[None, :]).reshape(-1)
    rates = jnp.exp((feature % half).astype(F32) * (-math.log(10000.0) / half))
    is_sin = (feature < half)[None, :]
    steps = jnp.arange(HALF, dtype=jnp.int32)
    row_angle = (begin + HALF * steps).astype(F32)[:, None] * rates[None, :]
    col_angle = steps.astype(F32)[:, None] * rates[None, :]
    row_sin, row_cos = jnp.sin(row_angle), jnp.cos(row_angle)
    row_one = jnp.where(is_sin, row_sin, row_cos)
    row_two = jnp.where(is_sin, row_cos, -row_sin)
    col_cos, col_sin = jnp.cos(col_angle), jnp.sin(col_angle)

    codes = (row_one, row_two, col_cos, col_sin)
    tokens, active, first_lift, second_field = run_forward(
        here, blocks, skip_field, weight, near, far, codes, kernels
    )
    second_back, side, patch = run_second_pair(
        here, blocks, hop_on(second_field), skip_recv, start, weight, near, far, kernels
    )
    prior = jnp.where(first_pair, active, side)
    keep, send, patch = run_back(
        here, hop_back(second_back), skip_field, first_lift, tokens, prior, patch, near, far,
        kernels,
    )

    summed = run_sum(run_partial(keep, flip(send, CORE), patch, flip(patch, CORE)))
    tokens_in_all = positions.shape[0] * HALF * HALF
    return (summed * (1.0 / math.sqrt(tokens_in_all)))[None]


def solution(mesh):
    in_specs = (
        P("seq", None, None),
        P("section", None, None, None, None),
        P("section", None, None),
        P(),
        P("seq", None, None),
    )
    out_specs = P("section", "seq", None)
    return jax.shard_map(
        on_device, mesh=mesh, in_specs=in_specs, out_specs=out_specs, check_vma=False
    )
```

```python
import math

import jax
import jax.numpy as jnp
from jax import lax
from jax.experimental import pallas as pl
from jax.experimental.pallas import tpu as pltpu
from jax.sharding import PartitionSpec as P

NORM_EPS = 1e-05
BF16 = jnp.bfloat16
F32 = jnp.float32
SIDE = 32
HALF = SIDE // 2
C = 256
N_SEQ = 64
SEQ = "seq"

X1, X3, Y1, Y3, CORE, ZH = (1 << 3, 3 << 3, 1 << 1, 3 << 1, 1, 1 << 5)


def flip(value, mask):
    return lax.ppermute(value, SEQ, [(i, i ^ mask) for i in range(N_SEQ)])


def partner(value):
    return lax.ppermute(value, "section", [(0, 1), (1, 0), (2, 3), (3, 2)])


HOPS = [(1 * N_SEQ + q, 2 * N_SEQ + q) for q in range(N_SEQ)] + [
    (q, 3 * N_SEQ + (q ^ ZH)) for q in range(N_SEQ)
]


def hop_on(value):
    return lax.ppermute(value, ("section", SEQ), HOPS)


def hop_back(value):
    return lax.ppermute(value, ("section", SEQ), [(j, i) for i, j in HOPS])


def dot(left, right):
    return jnp.dot(left, right, preferred_element_type=F32)


def dot_nt(left, right):
    return lax.dot_general(left, right, (((1,), (1,)), ((), ())), preferred_element_type=F32)


def dot_tn(left, right):
    return lax.dot_general(left, right, (((0,), (0,)), ((), ())), preferred_element_type=F32)


def patchify(field):
    pairs = field.reshape(HALF, 2, HALF, 2 * C)
    return jnp.concatenate([pairs[:, 0], pairs[:, 1]], axis=-1).reshape(HALF * HALF, 4 * C)


def unpatchify(tokens):
    pairs = tokens.reshape(HALF, HALF, 4 * C)
    return jnp.stack([pairs[..., : 2 * C], pairs[..., 2 * C :]], axis=1).reshape(SIDE, HALF, 2 * C)


def silu(value):
    half = 0.5 * value
    return half + half * jnp.tanh(half)


def silu_slope(value):
    half = 0.5 * value
    t = jnp.tanh(half)
    return (0.5 + 0.5 * t) * (1.0 + half * (1.0 - t))


CHUNKS = 4
UNROLL = 4
VMEM = pl.BlockSpec(memory_space=pltpu.VMEM)
SMEM = pl.BlockSpec(memory_space=pltpu.SMEM)
ANY = pl.BlockSpec(memory_space=pl.ANY)


def conv_in_kernel(field, kernel_ref, left_ref, right_ref, turned=False):
    even, odd = field[..., :C], field[..., C:]
    column = lax.broadcasted_iota(jnp.int32, (SIDE, HALF, C), 1)
    before = jnp.where(column == 0, 0.0, pltpu.roll(odd, 1, 1))
    after = jnp.where(column == HALF - 1, 0.0, pltpu.roll(even, HALF - 1, 1))
    middle = field.astype(BF16)
    left_ref[1 : SIDE + 1, :, C:] = middle
    left_ref[1 : SIDE + 1, :, :C] = before.astype(BF16)
    right_ref[1 : SIDE + 1, :, : 2 * C] = middle
    right_ref[1 : SIDE + 1, :, 2 * C :] = after.astype(BF16)
    out = []
    for ref in (left_ref, right_ref):
        edge = jnp.zeros((HALF, 3 * C), BF16)
        ref[0] = edge
        ref[SIDE + 1] = edge
        total = None
        for row in range(3):
            taps = ref[row : row + SIDE].reshape(SIDE * HALF, 3 * C)
            if turned:
                for column in range(3):
                    tap = (2 - row) * 3 + 2 - column
                    weight = kernel_ref[tap * C : (tap + 1) * C]
                    term = dot_nt(taps[:, column * C : (column + 1) * C], weight)
                    total = term if total is None else total + term
            else:
                term = dot(taps, kernel_ref[row * 3 * C : (row + 1) * 3 * C])
                total = term if total is None else total + term
        out.append(total.reshape(SIDE, HALF, C))
    return jnp.concatenate(out, axis=-1)


def choose(to_ref, mine, own_ref, top_ref, low_ref):
    @pl.when(mine)
    def _():
        to_ref[...] = own_ref[...]

    @pl.when(jnp.logical_not(mine))
    def _():
        to_ref[: top_ref.shape[0]] = top_ref[...]
        to_ref[top_ref.shape[0] :] = low_ref[...]


def rounded(value):
    return value.astype(BF16).astype(F32)


class Weights:
    def __init__(self, index_ref, own_ref, near_ref, far_ref, both_ref, sems, parity):
        self.args = (index_ref, own_ref, near_ref, far_ref, both_ref, sems, parity)
        self.rows = both_ref.shape[1] // CHUNKS
        self.share = both_ref.shape[1] // N_SEQ

    def start(self, own=True):
        index_ref, own_ref, near_ref, far_ref, both_ref, sems, parity = self.args
        per = N_SEQ // CHUNKS
        for block in range(N_SEQ if own else 0):
            source = pl.multiple_of(index_ref[block] * self.share, self.share)
            pltpu.make_async_copy(
                own_ref.at[pl.ds(source, self.share)],
                both_ref.at[parity, pl.ds(block * self.share, self.share)],
                sems.at[parity, block // per],
            ).start()
        for chunk in range(CHUNKS):
            source = near_ref if chunk < CHUNKS // 2 else far_ref
            pltpu.make_async_copy(
                source.at[pl.ds(chunk % (CHUNKS // 2) * self.rows, self.rows)],
                both_ref.at[1 - parity, pl.ds(chunk * self.rows, self.rows)],
                sems.at[1 - parity, chunk],
            ).start()

    def sweep(self, slot, step, wait=False):
        _, _, near_ref, _, both_ref, sems, _ = self.args

        @pl.loop(0, CHUNKS, unroll=UNROLL)
        def _(chunk):
            rows = pl.ds(pl.multiple_of(chunk * self.rows, self.rows), self.rows)
            if wait:
                pltpu.make_async_copy(
                    near_ref.at[pl.ds(0, self.rows)], both_ref.at[slot, rows], sems.at[slot, chunk]
                ).wait()
            step(chunk, both_ref[slot, rows])


def weight_scratch(width, depth):
    return [pltpu.VMEM((2, width, depth), BF16), pltpu.SemaphoreType.DMA((2, CHUNKS))]


def lanes(chunk, count):
    return pl.ds(pl.multiple_of(chunk * count, count), count)


TAPS = [pltpu.VMEM((SIDE + 2, HALF, 3 * C), BF16)] * 2
TOKENS = HALF * HALF
KERNEL = [pltpu.VMEM((9 * C, C), BF16)]
PARAMS = pltpu.CompilerParams(vmem_limit_bytes=40 * 1024 * 1024)


def call(body, outs, args, after=()):
    count = len(args)

    def with_after(*refs):
        body(*refs[:count], *refs[count + len(after) :])

    return pl.pallas_call(
        with_after,
        out_shape=[jax.ShapeDtypeStruct(shape, kind) for shape, kind in outs],
        in_specs=[VMEM] * count + [ANY] * len(after),
        out_specs=[VMEM] * len(outs),
        compiler_params=PARAMS,
    )(*args, *after)


def run_start(section, phase, rows, late, near, kernels):
    def body(
        section_ref, phase_ref, rows_ref, late_ref, near_ref, own_kernel_ref, top_ref, low_ref,
        skip_ref, start_ref, image_ref, left_ref, right_ref, kernel_ref,
    ):
        where, kind = section_ref[0], phase_ref[0]
        choose(kernel_ref, (where == 0) | (where == 3), own_kernel_ref, top_ref, low_ref)

        @pl.when(kind == 0)
        def _():
            image_ref[:16] = late_ref[...]
            image_ref[16:] = rows_ref[:16]

        @pl.when(kind == 1)
        def _():
            image_ref[:8] = near_ref[...]
            image_ref[8:] = rows_ref[...]

        @pl.when(kind == 2)
        def _():
            image_ref[:24] = rows_ref[...]
            image_ref[24:] = near_ref[...]

        @pl.when(kind == 3)
        def _():
            image_ref[...] = jnp.zeros_like(image_ref)

        @pl.when(where < 2)
        def _():
            field = conv_in_kernel(image_ref[...], kernel_ref, left_ref, right_ref)
            skip_ref[...] = field.astype(BF16)

        @pl.when(where >= 2)
        def _():
            field = conv_in_kernel(image_ref[...], kernel_ref, left_ref, right_ref, turned=True)
            start_ref[...] = field

    shape = (SIDE, HALF, 2 * C)
    return pl.pallas_call(
        body,
        out_shape=[jax.ShapeDtypeStruct(shape, BF16), jax.ShapeDtypeStruct(shape, F32)],
        in_specs=[SMEM, SMEM] + [VMEM] * 6,
        out_specs=[VMEM] * 2,
        scratch_shapes=[pltpu.VMEM(shape, F32)] + TAPS + KERNEL,
        compiler_params=PARAMS,
        name="start",
    )(section, phase, rows, late, near, *kernels)


def run_piece(blocks, weight):
    share, depth = weight.shape[0] // N_SEQ, weight.shape[1]

    def body(index_ref, weight_ref, out_ref):
        out_ref[...] = weight_ref[...]

    return pl.pallas_call(
        body,
        grid_spec=pltpu.PrefetchScalarGridSpec(
            num_scalar_prefetch=1,
            grid=(2,),
            in_specs=[pl.BlockSpec((share, depth), lambda i, index: (index[i], 0))],
            out_specs=pl.BlockSpec((share, depth), lambda i, index: (i, 0)),
        ),
        out_shape=jax.ShapeDtypeStruct((2 * share, depth), weight.dtype),
    )(blocks, weight)


def gather_first(piece, after):
    rows, depth = piece.shape
    half = depth // 2

    def split(piece_ref, first_ref, second_ref):
        first_ref[...] = piece_ref[:, :half]
        second_ref[...] = piece_ref[:, half:]

    shape = (rows, half)
    first, second = call(split, [(shape, BF16)] * 2, (piece,), after)
    got = [flip(first, m) for m in (X1, X1 ^ X3, X3)] + [flip(second, m) for m in (Y1, Y1 ^ Y3, Y3)]
    return (first, second, *got)


def gather_second(held, kernel, after):
    rows, half = held[0].shape
    depth, part = 2 * half, half // 2

    def stack(*refs):
        for side in range(2):
            for far in range(4):
                source = refs[side] if far == 0 else refs[2 + 3 * side + far - 1]
                refs[9 + side][far * rows : (far + 1) * rows] = source[...]
        refs[11][...] = refs[8][:kernel_rows]

    shape = (4 * rows, half)
    kernel_rows = kernel.shape[0] // 2
    kernel_part = ((kernel_rows, kernel.shape[1]), BF16)
    *wide, top = call(stack, [(shape, BF16)] * 2 + [kernel_part], (*held, kernel), after)
    top = partner(top)
    rings = ((Y1, Y3), (X1, X3))
    near = [flip(value, ring[0]) for value, ring in zip(wide, rings)]
    far = [flip(value, ring[1]) for value, ring in zip(wide, rings)]

    def cut(*refs):
        for side in range(2):
            refs[5 + 2 * side][...] = refs[side][:, :part]
            refs[6 + 2 * side][...] = refs[2 + side][:, part:]
        refs[9][...] = refs[4][kernel_rows:]

    shape = (4 * rows, part)
    *parts, low_rows = call(cut, [(shape, BF16)] * 4 + [kernel_part], (*far, *near, kernel), (top,))
    low_rows = partner(low_rows)
    low = [flip(parts[2 * side], ring[0]) for side, ring in enumerate(rings)]
    high = [flip(parts[2 * side + 1], ring[1]) for side, ring in enumerate(rings)]

    def join(*refs):
        out_ref = refs[10]
        for side in range(2):
            base = side * half
            mine, one, three = refs[side], refs[2 + side], refs[4 + side]
            for outer in range(4):
                sources = {0: [mine], 1: [one], 3: [three], 2: [refs[6 + side], refs[8 + side]]}[outer]
                for j, source in enumerate(sources):
                    count = source.shape[1]
                    at = slice(base + j * count, base + (j + 1) * count)
                    for inner in range(4):
                        block = source[inner * rows : (inner + 1) * rows]
                        x, y = (inner, outer) if side == 0 else (outer, inner)
                        start = (4 * x + y) * rows
                        out_ref[start : start + rows, at] = block

    args = (*wide, *near, *far, *low, *high)
    return call(join, [((16 * rows, depth), BF16)], args, (low_rows,))[0], (top, low_rows)


def run_forward(section, blocks, skip, own, near, far, codes, kernels):
    width, depth = own.shape
    cols = width // CHUNKS

    def body(
        section_ref, index_ref, skip_ref, own_ref, near_ref, far_ref, one_ref, two_ref, cos_ref,
        sin_ref, own_kernel_ref, top_ref, low_ref, tokens_ref, act_ref, lift_ref, field_ref, sum_ref,
        left_ref, right_ref, kernel_ref, both_ref, sems,
    ):
        parity = section_ref[0] % 2

        @pl.when(section_ref[0] < 2)
        def _():
            weights = Weights(index_ref, own_ref, near_ref, far_ref, both_ref, sems, parity)
            weights.start()
            choose(kernel_ref, parity == 1, own_kernel_ref, top_ref, low_ref)
            patch = patchify(skip_ref[...])
            sum_ref[...] = jnp.zeros_like(sum_ref)

            def embed(chunk, rows):
                at = lanes(chunk, cols)
                code = one_ref[:, at][:, None] * cos_ref[:, at][None]
                code += two_ref[:, at][:, None] * sin_ref[:, at][None]
                value = dot_nt(patch, rows) + code.reshape(TOKENS, cols)
                value = value.astype(BF16)
                tokens_ref[:, at] = value
                value = value.astype(F32)
                sum_ref[...] += jnp.sum(value * value, axis=-1, keepdims=True)

            weights.sweep(0, embed, wait=True)
            scale = lax.rsqrt(sum_ref[...] * (1.0 / width) + NORM_EPS)
            lift_ref[...] = jnp.zeros_like(lift_ref)

            def raise_up(chunk, rows):
                at = lanes(chunk, cols)
                active = silu(tokens_ref[:, at].astype(F32) * scale).astype(BF16)
                act_ref[:, at] = active
                lift_ref[...] += dot(active, rows)

            weights.sweep(1, raise_up, wait=True)

            field = unpatchify(rounded(silu(lift_ref[...])))
            field_ref[...] = conv_in_kernel(field, kernel_ref, left_ref, right_ref).astype(BF16)

    return pl.pallas_call(
        body,
        out_shape=[
            jax.ShapeDtypeStruct((TOKENS, width), BF16),
            jax.ShapeDtypeStruct((TOKENS, width), BF16),
            jax.ShapeDtypeStruct((TOKENS, depth), F32),
            jax.ShapeDtypeStruct((SIDE, HALF, 2 * C), BF16),
        ],
        in_specs=[SMEM, SMEM, VMEM] + [ANY] * 3 + [VMEM] * 7,
        out_specs=[VMEM] * 4,
        scratch_shapes=[pltpu.VMEM((TOKENS, 1), F32)]
        + TAPS
        + KERNEL
        + weight_scratch(width, depth),
        compiler_params=PARAMS,
        name="forward_first_pair",
    )(section, blocks, skip, own, near, far, *codes, *kernels)


def run_second_pair(section, blocks, second, skip, start, own, near, far, kernels):
    width, depth = own.shape
    cols = width // CHUNKS

    def body(
        section_ref, index_ref, second_ref, skip_ref, start_ref, own_ref, near_ref, far_ref,
        own_kernel_ref, top_ref, low_ref, back_ref, side_ref, patch_ref, sum_ref, left_ref,
        right_ref, kernel_ref, tokens_ref, inner_ref, lift_ref, both_ref, sems,
    ):
        parity = section_ref[0] % 2

        @pl.when(section_ref[0] >= 2)
        def _():
            weights = Weights(index_ref, own_ref, near_ref, far_ref, both_ref, sems, parity)
            weights.start()
            choose(kernel_ref, parity == 0, own_kernel_ref, top_ref, low_ref)
            field = rounded(silu(second_ref[...].astype(F32)))
            field = conv_in_kernel(field, kernel_ref, left_ref, right_ref).astype(BF16)
            patch_ref[...] = patchify(field)
            sum_ref[...] = jnp.zeros_like(sum_ref)

            def embed(chunk, rows):
                value = dot_nt(patch_ref[...], rows).astype(BF16)
                tokens_ref[:, lanes(chunk, cols)] = value
                value = value.astype(F32)
                sum_ref[...] += jnp.sum(value * value, axis=-1, keepdims=True)

            weights.sweep(0, embed, wait=True)
            scale = lax.rsqrt(sum_ref[...] * (1.0 / width) + NORM_EPS)
            lift_ref[...] = patchify(skip_ref[...]).astype(F32)

            def raise_up(chunk, rows):
                at = lanes(chunk, cols)
                active = silu(tokens_ref[:, at].astype(F32) * scale).astype(BF16)
                side_ref[:, at] = active
                lift_ref[...] += dot(active, rows)

            weights.sweep(1, raise_up, wait=True)
            last_patch = (patchify(start_ref[...]) * silu_slope(lift_ref[...])).astype(BF16)

            @pl.when(parity == 1)
            def _():
                patch_ref[...] = last_patch

            sum_ref[...] = jnp.zeros_like(sum_ref)

            def descend(chunk, rows):
                at = lanes(chunk, cols)
                normal = tokens_ref[:, at].astype(F32) * scale
                inner = dot_nt(last_patch, rows) * silu_slope(normal)
                inner_ref[:, at] = inner
                sum_ref[...] += jnp.sum(inner * normal, axis=-1, keepdims=True)

            weights.sweep(1, descend)
            mean = sum_ref[...] * (1.0 / width)
            lift_ref[...] = jnp.zeros_like(lift_ref)

            def lower(chunk, rows):
                at = lanes(chunk, cols)
                normal = tokens_ref[:, at].astype(F32) * scale
                back = (scale * (inner_ref[:, at] - normal * mean)).astype(BF16)

                @pl.when(parity == 0)
                def _():
                    side_ref[:, at] = back

                lift_ref[...] += dot(back, rows)

            weights.sweep(0, lower)
            field = unpatchify(rounded(lift_ref[...]))
            field = conv_in_kernel(field, kernel_ref, left_ref, right_ref, turned=True)
            back_ref[...] = (field * silu_slope(second_ref[...].astype(F32))).astype(BF16)

    return pl.pallas_call(
        body,
        out_shape=[
            jax.ShapeDtypeStruct((SIDE, HALF, 2 * C), BF16),
            jax.ShapeDtypeStruct((TOKENS, width), BF16),
            jax.ShapeDtypeStruct((TOKENS, depth), BF16),
        ],
        in_specs=[SMEM, SMEM] + [VMEM] * 3 + [ANY] * 3 + [VMEM] * 3,
        out_specs=[VMEM] * 3,
        scratch_shapes=[pltpu.VMEM((TOKENS, 1), F32)]
        + TAPS
        + KERNEL
        + [
            pltpu.VMEM((TOKENS, width), BF16),
            pltpu.VMEM((TOKENS, width), F32),
            pltpu.VMEM((TOKENS, depth), F32),
        ]
        + weight_scratch(width, depth),
        compiler_params=PARAMS,
        name="second_pair",
    )(section, blocks, second, skip, start, own, near, far, *kernels)


def run_back(section, given, skip, lift, tokens, prior, patch, near, far, kernels):
    width, depth = tokens.shape[1], lift.shape[1]
    cols = width // CHUNKS

    def body(
        section_ref, given_ref, skip_ref, lift_ref, tokens_ref, prior_ref, known_ref, near_ref,
        far_ref, own_kernel_ref, top_ref, low_ref, keep_ref, send_ref, patch_ref, sum_ref, left_ref,
        right_ref, kernel_ref, inner_ref, both_ref, sems,
    ):
        where = section_ref[0]
        weights = Weights(None, None, near_ref, far_ref, both_ref, sems, 1)

        @pl.when(where == 0)
        def _():
            weights.start(own=False)

        @pl.when(where >= 1)
        def _():
            keep_ref[...] = prior_ref[:, : width // 2]
            send_ref[...] = prior_ref[:, width // 2 :]

        @pl.when(where >= 2)
        def _():
            patch_ref[...] = known_ref[...]

        @pl.when(where < 2)
        def _():
            choose(kernel_ref, where == 1, own_kernel_ref, top_ref, low_ref)
            field = given_ref[...].astype(F32)
            field = conv_in_kernel(field, kernel_ref, left_ref, right_ref, turned=True)
            patch_ref[...] = (patchify(field) * silu_slope(lift_ref[...])).astype(BF16)

        @pl.when(where == 0)
        def _():
            sum_ref[...] = jnp.zeros_like(sum_ref)

            @pl.loop(0, CHUNKS, unroll=UNROLL)
            def _(chunk):
                value = tokens_ref[:, lanes(chunk, cols)].astype(F32)
                sum_ref[...] += jnp.sum(value * value, axis=-1, keepdims=True)

            scale = lax.rsqrt(sum_ref[...] * (1.0 / width) + NORM_EPS)
            sum_ref[...] = jnp.zeros_like(sum_ref)

            def descend(chunk, rows):
                at = lanes(chunk, cols)
                normal = tokens_ref[:, at].astype(F32) * scale
                inner = dot_nt(patch_ref[...], rows) * silu_slope(normal)
                inner_ref[:, at] = inner
                sum_ref[...] += jnp.sum(inner * normal, axis=-1, keepdims=True)

            weights.sweep(0, descend, wait=True)
            mean = sum_ref[...] * (1.0 / width)

            for first, ref in ((0, keep_ref), (CHUNKS // 2, send_ref)):

                @pl.loop(0, CHUNKS // 2, unroll=UNROLL)
                def _(i, first=first, ref=ref):
                    at = lanes(first + i, cols)
                    normal = tokens_ref[:, at].astype(F32) * scale
                    back = scale * (inner_ref[:, at] - normal * mean)
                    ref[:, lanes(i, cols)] = back.astype(BF16)

            patch_ref[...] = patchify(skip_ref[...])

    return pl.pallas_call(
        body,
        out_shape=[
            jax.ShapeDtypeStruct((TOKENS, width // 2), BF16),
            jax.ShapeDtypeStruct((TOKENS, width // 2), BF16),
            jax.ShapeDtypeStruct((TOKENS, depth), BF16),
        ],
        in_specs=[SMEM] + [VMEM] * 6 + [ANY] * 2 + [VMEM] * 3,
        out_specs=[VMEM] * 3,
        scratch_shapes=[pltpu.VMEM((TOKENS, 1), F32)]
        + TAPS
        + KERNEL
        + [
            pltpu.VMEM((TOKENS, width), F32),
            pltpu.VMEM((1, width, depth), BF16),
            pltpu.SemaphoreType.DMA((1, CHUNKS)),
        ],
        compiler_params=PARAMS,
        name="back_first_pair",
    )(section, given, skip, lift, tokens, prior, patch, near, far, *kernels)


SENT = {"a": (1, 2), "b": (3, 2)}
KEPT = {"a": (0, 3), "b": (0, 1)}


def run_partial(keep, recv, patch, patch_recv):
    half, depth = keep.shape[1], patch.shape[1]
    part, block = depth // 4, half // 16

    def body(keep_ref, recv_ref, patch_ref, other_ref, *out_refs):
        tokens = jnp.concatenate([keep_ref[...], recv_ref[...]], axis=0)
        patches = jnp.concatenate([patch_ref[...], other_ref[...]], axis=0)
        for column in range(4):
            name = "ab"[column % 2]
            sent_ref, kept_ref = out_refs[column], out_refs[4 + column]
            right = patches[:, column * part : (column + 1) * part]
            for i in range(2):
                for ref, far in ((sent_ref, SENT[name][i]), (kept_ref, KEPT[name][i])):
                    if column < 2:
                        left = tokens[:, far * 4 * block : (far + 1) * 4 * block]
                    else:
                        left = jnp.concatenate(
                            [tokens[:, (4 * j + far) * block :][:, :block] for j in range(4)], axis=1
                        )
                    ref[i] = dot_tn(left, right).astype(ref.dtype)

    shape = (2, 4 * block, part)
    outs = call(body, [(shape, BF16)] * 4 + [(shape, F32)] * 4, (keep, recv, patch, patch_recv))
    return outs[:4], outs[4:]


FIRST_RINGS = ((X1, X3), (X3, X1), (Y1, Y3), (Y3, Y1))


def run_sum(partial):
    sent, kept = partial
    got = [flip(value, ring[0]) for value, ring in zip(sent, FIRST_RINGS)]
    rows, part = kept[0].shape[1:]
    block = rows // 4

    def add_once(*refs):
        kept_refs, got_refs, sent_refs, out_refs = refs[:4], refs[4:8], refs[8:12], refs[12:]
        for kept_ref, got_ref, sent_ref, out_ref in zip(kept_refs, got_refs, sent_refs, out_refs):
            total = kept_ref[...] + got_ref[...].astype(F32)
            out_ref[...] = total[0]
            sent_ref[...] = total[1].astype(BF16)

    shape = (rows, part)
    outs = call(add_once, [(shape, BF16)] * 4 + [(shape, F32)] * 4, (*kept, *got))
    got = [flip(value, ring[1]) for value, ring in zip(outs[:4], FIRST_RINGS)]

    def add_twice(*refs):
        kept_refs, got_refs, out_refs = refs[:4], refs[4:8], refs[8:]
        for half in range(2):
            a, b = 2 * half, 2 * half + 1
            total = [kept_refs[i][...] + got_refs[i][...].astype(F32) for i in (a, b)]
            total = jnp.concatenate(total, axis=1)
            for far in range(4):
                ref = out_refs[4 * half + far]
                ref[...] = total[far * block : (far + 1) * block].astype(ref.dtype)

    shape = (block, 2 * part)
    kinds = [F32, BF16, BF16, BF16] * 2
    outs = call(add_twice, [(shape, kind) for kind in kinds], (*outs[4:], *got))
    got = [flip(v, m) for v, m in zip(outs[1:4], (Y1, Y1 ^ Y3, Y3))]
    got += [flip(v, m) for v, m in zip(outs[5:8], (X1, X1 ^ X3, X3))]

    def add_last(*refs):
        for half in range(2):
            total = refs[half][...]
            for ref in refs[2 + 3 * half : 5 + 3 * half]:
                total += ref[...].astype(F32)
            at = slice(half * 2 * part, (half + 1) * 2 * part)
            refs[8][:, at] = total[: block // 2]
            refs[9][:, at] = total[block // 2 :].astype(BF16)

    shape = (block // 2, 4 * part)
    mine, away = call(add_last, [(shape, F32), (shape, BF16)], (outs[0], outs[4], *got))
    return mine + flip(away, ZH).astype(F32)


def on_device(features, conv_kernels, patch_weights, positions, out_cotangent):
    weight = patch_weights[0]
    width, depth = weight.shape
    kernel = conv_kernels[0].reshape(9 * C, C)
    section = lax.axis_index("section")
    place = lax.axis_index(SEQ)
    first_pair = section < 2

    order = jnp.arange(N_SEQ, dtype=jnp.int32)
    away = ((order & 1) << 5) | (((order >> 3) & 3) << 3) | (((order >> 1) & 3) << 1) | (order >> 5)
    blocks = away ^ place

    here, phase = section.reshape(1), (place % 4).reshape(1)
    piece = partner(run_piece(blocks, weight))

    across = lax.ppermute(
        out_cotangent, ("section", SEQ), [(q, 3 * N_SEQ + (q ^ ZH)) for q in range(N_SEQ)]
    )
    rows = jnp.where(first_pair, features, jnp.where(section == 3, across, out_cotangent))
    rows = rows.astype(F32).reshape(rows.shape[0], HALF, 2 * C)
    late = lax.ppermute(rows[8:], SEQ, [(4 * k + 3, (4 * k + 4) % N_SEQ) for k in range(N_SEQ // 4)])
    some = jnp.where(phase[0] == 0, rows[16:], rows[:8])
    pairs = [(4 * k, 4 * k + 1) for k in range(N_SEQ // 4)]
    pairs += [(4 * k + 3, 4 * k + 2) for k in range(N_SEQ // 4)]
    beside = lax.ppermute(some, SEQ, pairs)

    image_id = jnp.minimum(3 * (place // 4) + place % 4, positions.shape[0] - 1)
    begin = positions[image_id]
    half = width // 2
    feature = (blocks[:, None] * (width // N_SEQ) + jnp.arange(width // N_SEQ)[None, :]).reshape(-1)
    rates = jnp.exp((feature % half).astype(F32) * (-math.log(10000.0) / half))
    is_sin = (feature < half)[None, :]
    steps = jnp.arange(HALF, dtype=jnp.int32)
    row_angle = (begin + HALF * steps).astype(F32)[:, None] * rates[None, :]
    col_angle = steps.astype(F32)[:, None] * rates[None, :]
    row_sin, row_cos = jnp.sin(row_angle), jnp.cos(row_angle)
    row_one = jnp.where(is_sin, row_sin, row_cos)
    row_two = jnp.where(is_sin, row_cos, -row_sin)
    col_cos, col_sin = jnp.cos(col_angle), jnp.sin(col_angle)

    codes = (row_one, row_two, col_cos, col_sin)

    held = gather_first(piece, (rows, *codes))
    near, kernel_other = gather_second(held, kernel, (late, beside))
    far = flip(near, CORE)
    kernels = (kernel, *kernel_other)
    skip_field, start = run_start(here, phase, rows, late, beside, kernels)
    skip_recv = hop_on(skip_field)

    tokens, active, first_lift, second_field = run_forward(
        here, blocks, skip_field, weight, near, far, codes, kernels
    )
    second_back, side, patch = run_second_pair(
        here, blocks, hop_on(second_field), skip_recv, start, weight, near, far, kernels
    )
    prior = jnp.where(first_pair, active, side)
    keep, send, patch = run_back(
        here, hop_back(second_back), skip_field, first_lift, tokens, prior, patch, near, far,
        kernels,
    )

    summed = run_sum(run_partial(keep, flip(send, CORE), patch, flip(patch, CORE)))
    tokens_in_all = positions.shape[0] * HALF * HALF
    return (summed * (1.0 / math.sqrt(tokens_in_all)))[None]


def solution(mesh):
    in_specs = (
        P("seq", None, None),
        P("section", None, None, None, None),
        P("section", None, None),
        P(),
        P("seq", None, None),
    )
    out_specs = P("section", "seq", None)
    return jax.shard_map(
        on_device, mesh=mesh, in_specs=in_specs, out_specs=out_specs, check_vma=False
    )
```

```python
import math

import jax
import jax.numpy as jnp
from jax import lax
from jax.experimental import pallas as pl
from jax.experimental.pallas import tpu as pltpu
from jax.sharding import PartitionSpec as P

NORM_EPS = 1e-05
BF16 = jnp.bfloat16
F32 = jnp.float32
SIDE = 32
HALF = SIDE // 2
C = 256
N_SEQ = 64
SEQ = "seq"

X1, X3, Y1, Y3, CORE, ZH = (1 << 3, 3 << 3, 1 << 1, 3 << 1, 1, 1 << 5)


def flip(value, mask):
    return lax.ppermute(value, SEQ, [(i, i ^ mask) for i in range(N_SEQ)])


def partner(value):
    return lax.ppermute(value, "section", [(0, 1), (1, 0), (2, 3), (3, 2)])


HOPS = [(1 * N_SEQ + q, 2 * N_SEQ + q) for q in range(N_SEQ)] + [
    (q, 3 * N_SEQ + (q ^ ZH)) for q in range(N_SEQ)
]


def hop_on(value):
    return lax.ppermute(value, ("section", SEQ), HOPS)


def hop_back(value):
    return lax.ppermute(value, ("section", SEQ), [(j, i) for i, j in HOPS])


def dot(left, right):
    return jnp.dot(left, right, preferred_element_type=F32)


def dot_nt(left, right):
    return lax.dot_general(left, right, (((1,), (1,)), ((), ())), preferred_element_type=F32)


def dot_tn(left, right):
    return lax.dot_general(left, right, (((0,), (0,)), ((), ())), preferred_element_type=F32)


def patchify(field):
    pairs = field.reshape(HALF, 2, HALF, 2 * C)
    return jnp.concatenate([pairs[:, 0], pairs[:, 1]], axis=-1).reshape(HALF * HALF, 4 * C)


def unpatchify(tokens):
    pairs = tokens.reshape(HALF, HALF, 4 * C)
    return jnp.stack([pairs[..., : 2 * C], pairs[..., 2 * C :]], axis=1).reshape(SIDE, HALF, 2 * C)


def silu(value):
    half = 0.5 * value
    return half + half * jnp.tanh(half)


def silu_slope(value):
    half = 0.5 * value
    t = jnp.tanh(half)
    return (0.5 + 0.5 * t) * (1.0 + half * (1.0 - t))


CHUNKS = 4
UNROLL = 4
VMEM = pl.BlockSpec(memory_space=pltpu.VMEM)
SMEM = pl.BlockSpec(memory_space=pltpu.SMEM)
ANY = pl.BlockSpec(memory_space=pl.ANY)


def conv_in_kernel(field, kernel_ref, left_ref, right_ref, turned=False):
    even, odd = field[..., :C], field[..., C:]
    column = lax.broadcasted_iota(jnp.int32, (SIDE, HALF, C), 1)
    before = jnp.where(column == 0, 0.0, pltpu.roll(odd, 1, 1))
    after = jnp.where(column == HALF - 1, 0.0, pltpu.roll(even, HALF - 1, 1))
    middle = field.astype(BF16)
    left_ref[1 : SIDE + 1, :, C:] = middle
    left_ref[1 : SIDE + 1, :, :C] = before.astype(BF16)
    right_ref[1 : SIDE + 1, :, : 2 * C] = middle
    right_ref[1 : SIDE + 1, :, 2 * C :] = after.astype(BF16)
    out = []
    for ref in (left_ref, right_ref):
        edge = jnp.zeros((HALF, 3 * C), BF16)
        ref[0] = edge
        ref[SIDE + 1] = edge
        total = None
        for row in range(3):
            taps = ref[row : row + SIDE].reshape(SIDE * HALF, 3 * C)
            if turned:
                for column in range(3):
                    tap = (2 - row) * 3 + 2 - column
                    weight = kernel_ref[tap * C : (tap + 1) * C]
                    term = dot_nt(taps[:, column * C : (column + 1) * C], weight)
                    total = term if total is None else total + term
            else:
                term = dot(taps, kernel_ref[row * 3 * C : (row + 1) * 3 * C])
                total = term if total is None else total + term
        out.append(total.reshape(SIDE, HALF, C))
    return jnp.concatenate(out, axis=-1)


def choose(to_ref, mine, own_ref, top_ref, low_ref):
    @pl.when(mine)
    def _():
        to_ref[...] = own_ref[...]

    @pl.when(jnp.logical_not(mine))
    def _():
        to_ref[: top_ref.shape[0]] = top_ref[...]
        to_ref[top_ref.shape[0] :] = low_ref[...]


def rounded(value):
    return value.astype(BF16).astype(F32)


class Weights:
    def __init__(self, index_ref, own_ref, near_ref, far_ref, both_ref, sems, parity):
        self.args = (index_ref, own_ref, near_ref, far_ref, both_ref, sems, parity)
        self.rows = both_ref.shape[1] // CHUNKS
        self.share = both_ref.shape[1] // N_SEQ

    def start(self, own=True):
        index_ref, own_ref, near_ref, far_ref, both_ref, sems, parity = self.args
        per = N_SEQ // CHUNKS
        for block in range(N_SEQ if own else 0):
            source = pl.multiple_of(index_ref[block] * self.share, self.share)
            pltpu.make_async_copy(
                own_ref.at[pl.ds(source, self.share)],
                both_ref.at[parity, pl.ds(block * self.share, self.share)],
                sems.at[parity, block // per],
            ).start()
        for chunk in range(CHUNKS):
            source = near_ref if chunk < CHUNKS // 2 else far_ref
            pltpu.make_async_copy(
                source.at[pl.ds(chunk % (CHUNKS // 2) * self.rows, self.rows)],
                both_ref.at[1 - parity, pl.ds(chunk * self.rows, self.rows)],
                sems.at[1 - parity, chunk],
            ).start()

    def sweep(self, slot, step, wait=False):
        _, _, near_ref, _, both_ref, sems, _ = self.args

        @pl.loop(0, CHUNKS, unroll=UNROLL)
        def _(chunk):
            rows = pl.ds(pl.multiple_of(chunk * self.rows, self.rows), self.rows)
            if wait:
                pltpu.make_async_copy(
                    near_ref.at[pl.ds(0, self.rows)], both_ref.at[slot, rows], sems.at[slot, chunk]
                ).wait()
            step(chunk, both_ref[slot, rows])


def weight_scratch(width, depth):
    return [pltpu.VMEM((2, width, depth), BF16), pltpu.SemaphoreType.DMA((2, CHUNKS))]


def lanes(chunk, count):
    return pl.ds(pl.multiple_of(chunk * count, count), count)


TAPS = [pltpu.VMEM((SIDE + 2, HALF, 3 * C), BF16)] * 2
TOKENS = HALF * HALF
KERNEL = [pltpu.VMEM((9 * C, C), BF16)]
PARAMS = pltpu.CompilerParams(vmem_limit_bytes=40 * 1024 * 1024)


def call(body, outs, args, after=()):
    count = len(args)

    def with_after(*refs):
        body(*refs[:count], *refs[count + len(after) :])

    return pl.pallas_call(
        with_after,
        out_shape=[jax.ShapeDtypeStruct(shape, kind) for shape, kind in outs],
        in_specs=[VMEM] * count + [ANY] * len(after),
        out_specs=[VMEM] * len(outs),
        compiler_params=PARAMS,
    )(*args, *after)


def run_rows(phase, features, cotangent):
    count = features.shape[0]
    wide = 2 * C

    def body(phase_ref, features_ref, cotangent_ref, *refs):
        late_ref, beside_ref, value_ref = refs[2:]
        for side, ref in enumerate((features_ref, cotangent_ref)):
            for part in range(2):
                value_ref[part] = ref[:, :, part * 128 : (part + 1) * 128].astype(F32)
            quarters = [
                value_ref[part, :, pl.ds(column, HALF, stride=2), :]
                for column in range(2)
                for part in range(2)
            ]
            rows = jnp.concatenate(quarters, axis=-1).astype(BF16)
            refs[side][...] = rows
            at = slice(side * wide, (side + 1) * wide)
            late_ref[:, :, at] = rows[8:]

            @pl.when(phase_ref[0] == 0)
            def _(rows=rows, at=at):
                beside_ref[:, :, at] = rows[16:]

            @pl.when(phase_ref[0] != 0)
            def _(rows=rows, at=at):
                beside_ref[:, :, at] = rows[:8]

    shapes = [(count, HALF, wide)] * 2 + [(16, HALF, 2 * wide), (8, HALF, 2 * wide)]
    return pl.pallas_call(
        body,
        out_shape=[jax.ShapeDtypeStruct(shape, BF16) for shape in shapes],
        in_specs=[SMEM, VMEM, VMEM],
        out_specs=[VMEM] * 4,
        scratch_shapes=[pltpu.VMEM((2, count, SIDE, 128), F32)],
        compiler_params=PARAMS,
        name="rows",
    )(phase, features, cotangent)


def run_image(phase, rows, late, beside):
    def body(phase_ref, *refs):
        late_ref, beside_ref = refs[2:4]
        kind = phase_ref[0]
        for side in range(2):
            rows_ref, out_ref = refs[side], refs[4 + side]
            at = slice(side * 2 * C, (side + 1) * 2 * C)

            @pl.when(kind == 0)
            def _(rows_ref=rows_ref, out_ref=out_ref, at=at):
                out_ref[:16] = late_ref[:, :, at]
                out_ref[16:] = rows_ref[:16]

            @pl.when(kind == 1)
            def _(rows_ref=rows_ref, out_ref=out_ref, at=at):
                out_ref[:8] = beside_ref[:, :, at]
                out_ref[8:] = rows_ref[...]

            @pl.when(kind == 2)
            def _(rows_ref=rows_ref, out_ref=out_ref, at=at):
                out_ref[:24] = rows_ref[...]
                out_ref[24:] = beside_ref[:, :, at]

            @pl.when(kind == 3)
            def _(out_ref=out_ref):
                out_ref[...] = jnp.zeros_like(out_ref)

    return pl.pallas_call(
        body,
        out_shape=[jax.ShapeDtypeStruct((SIDE, HALF, 2 * C), BF16)] * 2,
        in_specs=[SMEM] + [VMEM] * 4,
        out_specs=[VMEM] * 2,
        compiler_params=PARAMS,
        name="image",
    )(phase, *rows, late, beside)


def run_start(section, image, kernels, turned):
    def body(section_ref, image_ref, own_ref, top_ref, low_ref, out_ref, left_ref, right_ref, kernel_ref):
        where = section_ref[0]

        @pl.when((where >= 2) if turned else (where < 2))
        def _():
            choose(kernel_ref, where == (3 if turned else 0), own_ref, top_ref, low_ref)
            field = image_ref[...].astype(F32)
            field = conv_in_kernel(field, kernel_ref, left_ref, right_ref, turned=turned)
            out_ref[...] = field.astype(out_ref.dtype)

    return pl.pallas_call(
        body,
        out_shape=jax.ShapeDtypeStruct((SIDE, HALF, 2 * C), F32 if turned else BF16),
        in_specs=[SMEM] + [VMEM] * 4,
        out_specs=VMEM,
        scratch_shapes=TAPS + KERNEL,
        compiler_params=PARAMS,
        name="start_turned" if turned else "start",
    )(section, image, *kernels)


def run_piece(blocks, weight):
    share, depth = weight.shape[0] // N_SEQ, weight.shape[1]

    def body(index_ref, weight_ref, out_ref):
        out_ref[...] = weight_ref[...]

    return pl.pallas_call(
        body,
        grid_spec=pltpu.PrefetchScalarGridSpec(
            num_scalar_prefetch=1,
            grid=(2,),
            in_specs=[pl.BlockSpec((share, depth), lambda i, index: (index[i], 0))],
            out_specs=pl.BlockSpec((share, depth), lambda i, index: (i, 0)),
        ),
        out_shape=jax.ShapeDtypeStruct((2 * share, depth), weight.dtype),
    )(blocks, weight)


def gather_partner(piece, kernel, images, before):
    rows, depth = piece.shape
    half, part = depth // 2, depth // 4
    kernel_rows = kernel.shape[0] // 2
    kernel_part = ((kernel_rows, kernel.shape[1]), BF16)

    def split(piece_ref, kernel_ref, first_ref, second_ref, top_ref):
        first_ref[...] = piece_ref[:, :half]
        second_ref[...] = piece_ref[:, half:]
        top_ref[...] = kernel_ref[:kernel_rows]

    outs = [((rows, half), BF16)] * 2 + [kernel_part]
    first, second, top = call(split, outs, (piece, kernel), before)
    got = [flip(first, m) for m in (X1, X1 ^ X3, X3)] + [flip(second, m) for m in (Y1, Y1 ^ Y3, Y3)]
    top = partner(top)
    image, cotangent = images()
    cotangent = hop_on(cotangent)

    def stack(*refs):
        for side in range(2):
            for far in range(4):
                source = refs[side] if far == 0 else refs[2 + 3 * side + far - 1]
                refs[9 + side][far * rows : (far + 1) * rows] = source[...]
        refs[11][...] = refs[8][kernel_rows:]

    outs = [((4 * rows, half), BF16)] * 2 + [kernel_part]
    *wide, low_rows = call(stack, outs, (first, second, *got, kernel), (top, image))
    rings = ((Y1, Y3), (X1, X3))
    near = [flip(value, ring[0]) for value, ring in zip(wide, rings)]
    far = [flip(value, ring[1]) for value, ring in zip(wide, rings)]
    low_rows = partner(low_rows)
    kernels = (kernel, top, low_rows)
    section = lax.axis_index("section").reshape(1)
    skip_field = run_start(section, image, kernels, turned=False)

    def cut(*refs):
        for side in range(2):
            refs[4 + 2 * side][...] = refs[side][:, :part]
            refs[5 + 2 * side][...] = refs[2 + side][:, part:]

    outs = [((4 * rows, part), BF16)] * 4
    parts = call(cut, outs, (*far, *near), (low_rows, cotangent))
    low = [flip(parts[2 * side], ring[0]) for side, ring in enumerate(rings)]
    high = [flip(parts[2 * side + 1], ring[1]) for side, ring in enumerate(rings)]

    def join(*refs):
        out_ref = refs[10]
        for side in range(2):
            base = side * half
            mine, one, three = refs[side], refs[2 + side], refs[4 + side]
            for outer in range(4):
                sources = {0: [mine], 1: [one], 3: [three], 2: [refs[6 + side], refs[8 + side]]}[outer]
                for j, source in enumerate(sources):
                    count = source.shape[1]
                    at = slice(base + j * count, base + (j + 1) * count)
                    for inner in range(4):
                        block = source[inner * rows : (inner + 1) * rows]
                        x, y = (inner, outer) if side == 0 else (outer, inner)
                        start = (4 * x + y) * rows
                        out_ref[start : start + rows, at] = block

    args = (*wide, *near, *far, *low, *high)
    held = call(join, [((16 * rows, depth), BF16)], args, (skip_field,))[0]
    return held, kernels, skip_field, cotangent


def run_forward(section, blocks, skip, own, near, far, codes, kernels):
    width, depth = own.shape
    cols = width // CHUNKS

    def body(
        section_ref, index_ref, skip_ref, own_ref, near_ref, far_ref, one_ref, two_ref, cos_ref,
        sin_ref, own_kernel_ref, top_ref, low_ref, tokens_ref, act_ref, lift_ref, field_ref, sum_ref,
        left_ref, right_ref, kernel_ref, both_ref, sems,
    ):
        parity = section_ref[0] % 2

        @pl.when(section_ref[0] < 2)
        def _():
            weights = Weights(index_ref, own_ref, near_ref, far_ref, both_ref, sems, parity)
            weights.start()
            choose(kernel_ref, parity == 1, own_kernel_ref, top_ref, low_ref)
            patch = patchify(skip_ref[...])
            sum_ref[...] = jnp.zeros_like(sum_ref)

            def embed(chunk, rows):
                at = lanes(chunk, cols)
                code = one_ref[:, at][:, None] * cos_ref[:, at][None]
                code += two_ref[:, at][:, None] * sin_ref[:, at][None]
                value = dot_nt(patch, rows) + code.reshape(TOKENS, cols)
                value = value.astype(BF16)
                tokens_ref[:, at] = value
                value = value.astype(F32)
                sum_ref[...] += jnp.sum(value * value, axis=-1, keepdims=True)

            weights.sweep(0, embed, wait=True)
            scale = lax.rsqrt(sum_ref[...] * (1.0 / width) + NORM_EPS)
            lift_ref[...] = jnp.zeros_like(lift_ref)

            def raise_up(chunk, rows):
                at = lanes(chunk, cols)
                active = silu(tokens_ref[:, at].astype(F32) * scale).astype(BF16)
                act_ref[:, at] = active
                lift_ref[...] += dot(active, rows)

            weights.sweep(1, raise_up, wait=True)

            field = unpatchify(rounded(silu(lift_ref[...])))
            field_ref[...] = conv_in_kernel(field, kernel_ref, left_ref, right_ref).astype(BF16)

    return pl.pallas_call(
        body,
        out_shape=[
            jax.ShapeDtypeStruct((TOKENS, width), BF16),
            jax.ShapeDtypeStruct((TOKENS, width), BF16),
            jax.ShapeDtypeStruct((TOKENS, depth), F32),
            jax.ShapeDtypeStruct((SIDE, HALF, 2 * C), BF16),
        ],
        in_specs=[SMEM, SMEM, VMEM] + [ANY] * 3 + [VMEM] * 7,
        out_specs=[VMEM] * 4,
        scratch_shapes=[pltpu.VMEM((TOKENS, 1), F32)]
        + TAPS
        + KERNEL
        + weight_scratch(width, depth),
        compiler_params=PARAMS,
        name="forward_first_pair",
    )(section, blocks, skip, own, near, far, *codes, *kernels)


def run_second_pair(section, blocks, second, skip, start, own, near, far, kernels):
    width, depth = own.shape
    cols = width // CHUNKS

    def body(
        section_ref, index_ref, second_ref, skip_ref, start_ref, own_ref, near_ref, far_ref,
        own_kernel_ref, top_ref, low_ref, back_ref, side_ref, patch_ref, sum_ref, left_ref,
        right_ref, kernel_ref, tokens_ref, inner_ref, lift_ref, both_ref, sems,
    ):
        parity = section_ref[0] % 2

        @pl.when(section_ref[0] >= 2)
        def _():
            weights = Weights(index_ref, own_ref, near_ref, far_ref, both_ref, sems, parity)
            weights.start()
            choose(kernel_ref, parity == 0, own_kernel_ref, top_ref, low_ref)
            field = rounded(silu(second_ref[...].astype(F32)))
            field = conv_in_kernel(field, kernel_ref, left_ref, right_ref).astype(BF16)
            patch_ref[...] = patchify(field)
            sum_ref[...] = jnp.zeros_like(sum_ref)

            def embed(chunk, rows):
                value = dot_nt(patch_ref[...], rows).astype(BF16)
                tokens_ref[:, lanes(chunk, cols)] = value
                value = value.astype(F32)
                sum_ref[...] += jnp.sum(value * value, axis=-1, keepdims=True)

            weights.sweep(0, embed, wait=True)
            scale = lax.rsqrt(sum_ref[...] * (1.0 / width) + NORM_EPS)
            lift_ref[...] = patchify(skip_ref[...]).astype(F32)

            def raise_up(chunk, rows):
                at = lanes(chunk, cols)
                active = silu(tokens_ref[:, at].astype(F32) * scale).astype(BF16)
                side_ref[:, at] = active
                lift_ref[...] += dot(active, rows)

            weights.sweep(1, raise_up, wait=True)
            last_patch = (patchify(start_ref[...]) * silu_slope(lift_ref[...])).astype(BF16)

            @pl.when(parity == 1)
            def _():
                patch_ref[...] = last_patch

            sum_ref[...] = jnp.zeros_like(sum_ref)

            def descend(chunk, rows):
                at = lanes(chunk, cols)
                normal = tokens_ref[:, at].astype(F32) * scale
                inner = dot_nt(last_patch, rows) * silu_slope(normal)
                inner_ref[:, at] = inner
                sum_ref[...] += jnp.sum(inner * normal, axis=-1, keepdims=True)

            weights.sweep(1, descend)
            mean = sum_ref[...] * (1.0 / width)
            lift_ref[...] = jnp.zeros_like(lift_ref)

            def lower(chunk, rows):
                at = lanes(chunk, cols)
                normal = tokens_ref[:, at].astype(F32) * scale
                back = (scale * (inner_ref[:, at] - normal * mean)).astype(BF16)

                @pl.when(parity == 0)
                def _():
                    side_ref[:, at] = back

                lift_ref[...] += dot(back, rows)

            weights.sweep(0, lower)
            field = unpatchify(rounded(lift_ref[...]))
            field = conv_in_kernel(field, kernel_ref, left_ref, right_ref, turned=True)
            back_ref[...] = (field * silu_slope(second_ref[...].astype(F32))).astype(BF16)

    return pl.pallas_call(
        body,
        out_shape=[
            jax.ShapeDtypeStruct((SIDE, HALF, 2 * C), BF16),
            jax.ShapeDtypeStruct((TOKENS, width), BF16),
            jax.ShapeDtypeStruct((TOKENS, depth), BF16),
        ],
        in_specs=[SMEM, SMEM] + [VMEM] * 3 + [ANY] * 3 + [VMEM] * 3,
        out_specs=[VMEM] * 3,
        scratch_shapes=[pltpu.VMEM((TOKENS, 1), F32)]
        + TAPS
        + KERNEL
        + [
            pltpu.VMEM((TOKENS, width), BF16),
            pltpu.VMEM((TOKENS, width), F32),
            pltpu.VMEM((TOKENS, depth), F32),
        ]
        + weight_scratch(width, depth),
        compiler_params=PARAMS,
        name="second_pair",
    )(section, blocks, second, skip, start, own, near, far, *kernels)


def run_back(section, given, skip, lift, tokens, prior, patch, near, far, kernels):
    width, depth = tokens.shape[1], lift.shape[1]
    cols = width // CHUNKS

    def body(
        section_ref, given_ref, skip_ref, lift_ref, tokens_ref, prior_ref, known_ref, near_ref,
        far_ref, own_kernel_ref, top_ref, low_ref, keep_ref, send_ref, patch_ref, sum_ref, left_ref,
        right_ref, kernel_ref, inner_ref, both_ref, sems,
    ):
        where = section_ref[0]
        weights = Weights(None, None, near_ref, far_ref, both_ref, sems, 1)

        @pl.when(where == 0)
        def _():
            weights.start(own=False)

        @pl.when(where >= 1)
        def _():
            keep_ref[...] = prior_ref[:, : width // 2]
            send_ref[...] = prior_ref[:, width // 2 :]

        @pl.when(where >= 2)
        def _():
            patch_ref[...] = known_ref[...]

        @pl.when(where < 2)
        def _():
            choose(kernel_ref, where == 1, own_kernel_ref, top_ref, low_ref)
            field = given_ref[...].astype(F32)
            field = conv_in_kernel(field, kernel_ref, left_ref, right_ref, turned=True)
            patch_ref[...] = (patchify(field) * silu_slope(lift_ref[...])).astype(BF16)

        @pl.when(where == 0)
        def _():
            sum_ref[...] = jnp.zeros_like(sum_ref)

            @pl.loop(0, CHUNKS, unroll=UNROLL)
            def _(chunk):
                value = tokens_ref[:, lanes(chunk, cols)].astype(F32)
                sum_ref[...] += jnp.sum(value * value, axis=-1, keepdims=True)

            scale = lax.rsqrt(sum_ref[...] * (1.0 / width) + NORM_EPS)
            sum_ref[...] = jnp.zeros_like(sum_ref)

            def descend(chunk, rows):
                at = lanes(chunk, cols)
                normal = tokens_ref[:, at].astype(F32) * scale
                inner = dot_nt(patch_ref[...], rows) * silu_slope(normal)
                inner_ref[:, at] = inner
                sum_ref[...] += jnp.sum(inner * normal, axis=-1, keepdims=True)

            weights.sweep(0, descend, wait=True)
            mean = sum_ref[...] * (1.0 / width)

            for first, ref in ((0, keep_ref), (CHUNKS // 2, send_ref)):

                @pl.loop(0, CHUNKS // 2, unroll=UNROLL)
                def _(i, first=first, ref=ref):
                    at = lanes(first + i, cols)
                    normal = tokens_ref[:, at].astype(F32) * scale
                    back = scale * (inner_ref[:, at] - normal * mean)
                    ref[:, lanes(i, cols)] = back.astype(BF16)

            patch_ref[...] = patchify(skip_ref[...])

    return pl.pallas_call(
        body,
        out_shape=[
            jax.ShapeDtypeStruct((TOKENS, width // 2), BF16),
            jax.ShapeDtypeStruct((TOKENS, width // 2), BF16),
            jax.ShapeDtypeStruct((TOKENS, depth), BF16),
        ],
        in_specs=[SMEM] + [VMEM] * 6 + [ANY] * 2 + [VMEM] * 3,
        out_specs=[VMEM] * 3,
        scratch_shapes=[pltpu.VMEM((TOKENS, 1), F32)]
        + TAPS
        + KERNEL
        + [
            pltpu.VMEM((TOKENS, width), F32),
            pltpu.VMEM((1, width, depth), BF16),
            pltpu.SemaphoreType.DMA((1, CHUNKS)),
        ],
        compiler_params=PARAMS,
        name="back_first_pair",
    )(section, given, skip, lift, tokens, prior, patch, near, far, *kernels)


SENT = {"a": (1, 2), "b": (3, 2)}
KEPT = {"a": (0, 3), "b": (0, 1)}


def run_partial(keep, recv, patch, patch_recv):
    half, depth = keep.shape[1], patch.shape[1]
    part, block = depth // 4, half // 16

    def body(keep_ref, recv_ref, patch_ref, other_ref, *out_refs):
        tokens = jnp.concatenate([keep_ref[...], recv_ref[...]], axis=0)
        patches = jnp.concatenate([patch_ref[...], other_ref[...]], axis=0)
        for column in range(4):
            name = "ab"[column % 2]
            sent_ref, kept_ref = out_refs[column], out_refs[4 + column]
            right = patches[:, column * part : (column + 1) * part]
            for i in range(2):
                for ref, far in ((sent_ref, SENT[name][i]), (kept_ref, KEPT[name][i])):
                    if column < 2:
                        left = tokens[:, far * 4 * block : (far + 1) * 4 * block]
                    else:
                        left = jnp.concatenate(
                            [tokens[:, (4 * j + far) * block :][:, :block] for j in range(4)], axis=1
                        )
                    ref[i] = dot_tn(left, right).astype(ref.dtype)

    shape = (2, 4 * block, part)
    outs = call(body, [(shape, BF16)] * 4 + [(shape, F32)] * 4, (keep, recv, patch, patch_recv))
    return outs[:4], outs[4:]


FIRST_RINGS = ((X1, X3), (X3, X1), (Y1, Y3), (Y3, Y1))


def run_sum(partial):
    sent, kept = partial
    got = [flip(value, ring[0]) for value, ring in zip(sent, FIRST_RINGS)]
    rows, part = kept[0].shape[1:]
    block = rows // 4

    def add_once(*refs):
        kept_refs, got_refs, sent_refs, out_refs = refs[:4], refs[4:8], refs[8:12], refs[12:]
        for kept_ref, got_ref, sent_ref, out_ref in zip(kept_refs, got_refs, sent_refs, out_refs):
            total = kept_ref[...] + got_ref[...].astype(F32)
            out_ref[...] = total[0]
            sent_ref[...] = total[1].astype(BF16)

    shape = (rows, part)
    outs = call(add_once, [(shape, BF16)] * 4 + [(shape, F32)] * 4, (*kept, *got))
    got = [flip(value, ring[1]) for value, ring in zip(outs[:4], FIRST_RINGS)]

    def add_twice(*refs):
        kept_refs, got_refs, out_refs = refs[:4], refs[4:8], refs[8:]
        for half in range(2):
            a, b = 2 * half, 2 * half + 1
            total = [kept_refs[i][...] + got_refs[i][...].astype(F32) for i in (a, b)]
            total = jnp.concatenate(total, axis=1)
            for far in range(4):
                ref = out_refs[4 * half + far]
                ref[...] = total[far * block : (far + 1) * block].astype(ref.dtype)

    shape = (block, 2 * part)
    kinds = [F32, BF16, BF16, BF16] * 2
    outs = call(add_twice, [(shape, kind) for kind in kinds], (*outs[4:], *got))
    got = [flip(v, m) for v, m in zip(outs[1:4], (Y1, Y1 ^ Y3, Y3))]
    got += [flip(v, m) for v, m in zip(outs[5:8], (X1, X1 ^ X3, X3))]

    def add_last(*refs):
        for half in range(2):
            total = refs[half][...]
            for ref in refs[2 + 3 * half : 5 + 3 * half]:
                total += ref[...].astype(F32)
            at = slice(half * 2 * part, (half + 1) * 2 * part)
            refs[8][:, at] = total[: block // 2]
            refs[9][:, at] = total[block // 2 :].astype(BF16)

    shape = (block // 2, 4 * part)
    mine, away = call(add_last, [(shape, F32), (shape, BF16)], (outs[0], outs[4], *got))
    return mine + flip(away, ZH).astype(F32)


def on_device(features, conv_kernels, patch_weights, positions, out_cotangent):
    weight = patch_weights[0]
    width, depth = weight.shape
    kernel = conv_kernels[0].reshape(9 * C, C)
    section = lax.axis_index("section")
    place = lax.axis_index(SEQ)
    first_pair = section < 2

    order = jnp.arange(N_SEQ, dtype=jnp.int32)
    away = ((order & 1) << 5) | (((order >> 3) & 3) << 3) | (((order >> 1) & 3) << 1) | (order >> 5)
    blocks = away ^ place

    here, phase = section.reshape(1), (place % 4).reshape(1)
    piece = partner(run_piece(blocks, weight))
    *rows, late, beside = run_rows(phase, features, out_cotangent)
    late = lax.ppermute(late, SEQ, [(4 * k + 3, (4 * k + 4) % N_SEQ) for k in range(N_SEQ // 4)])
    pairs = [(4 * k, 4 * k + 1) for k in range(N_SEQ // 4)]
    pairs += [(4 * k + 3, 4 * k + 2) for k in range(N_SEQ // 4)]
    beside = lax.ppermute(beside, SEQ, pairs)

    image_id = jnp.minimum(3 * (place // 4) + place % 4, positions.shape[0] - 1)
    begin = positions[image_id]
    half = width // 2
    feature = (blocks[:, None] * (width // N_SEQ) + jnp.arange(width // N_SEQ)[None, :]).reshape(-1)
    rates = jnp.exp((feature % half).astype(F32) * (-math.log(10000.0) / half))
    is_sin = (feature < half)[None, :]
    steps = jnp.arange(HALF, dtype=jnp.int32)
    row_angle = (begin + HALF * steps).astype(F32)[:, None] * rates[None, :]
    col_angle = steps.astype(F32)[:, None] * rates[None, :]
    row_sin, row_cos = jnp.sin(row_angle), jnp.cos(row_angle)
    row_one = jnp.where(is_sin, row_sin, row_cos)
    row_two = jnp.where(is_sin, row_cos, -row_sin)
    col_cos, col_sin = jnp.cos(col_angle), jnp.sin(col_angle)

    codes = (row_one, row_two, col_cos, col_sin)

    near, kernels, skip_field, cotangent = gather_partner(
        piece, kernel, lambda: run_image(phase, rows, late, beside), (late, beside, *codes)
    )
    far = flip(near, CORE)
    skip_recv = hop_on(skip_field)
    start = run_start(here, cotangent, kernels, turned=True)

    tokens, active, first_lift, second_field = run_forward(
        here, blocks, skip_field, weight, near, far, codes, kernels
    )
    second_back, side, patch = run_second_pair(
        here, blocks, hop_on(second_field), skip_recv, start, weight, near, far, kernels
    )
    prior = jnp.where(first_pair, active, side)
    keep, send, patch = run_back(
        here, hop_back(second_back), skip_field, first_lift, tokens, prior, patch, near, far,
        kernels,
    )

    summed = run_sum(run_partial(keep, flip(send, CORE), patch, flip(patch, CORE)))
    tokens_in_all = positions.shape[0] * HALF * HALF
    return (summed * (1.0 / math.sqrt(tokens_in_all)))[None]


def solution(mesh):
    in_specs = (
        P("seq", None, None),
        P("section", None, None, None, None),
        P("section", None, None),
        P(),
        P("seq", None, None),
    )
    out_specs = P("section", "seq", None)
    return jax.shard_map(
        on_device, mesh=mesh, in_specs=in_specs, out_specs=out_specs, check_vma=False
    )
```

```python
import math

import jax
import jax.numpy as jnp
from jax import lax
from jax.experimental import pallas as pl
from jax.experimental.pallas import tpu as pltpu
from jax.sharding import PartitionSpec as P

NORM_EPS = 1e-05
BF16 = jnp.bfloat16
F32 = jnp.float32
SIDE = 32
HALF = SIDE // 2
C = 256
N_SEQ = 64
SEQ = "seq"

X1, X3, Y1, Y3, CORE, ZH = (1 << 3, 3 << 3, 1 << 1, 3 << 1, 1, 1 << 5)


def flip(value, mask):
    return lax.ppermute(value, SEQ, [(i, i ^ mask) for i in range(N_SEQ)])


def partner(value):
    return lax.ppermute(value, "section", [(0, 1), (1, 0), (2, 3), (3, 2)])


HOPS = [(1 * N_SEQ + q, 2 * N_SEQ + q) for q in range(N_SEQ)]
HOPS += [(q, 3 * N_SEQ + (q ^ ZH)) for q in range(N_SEQ)]
HOPS += [(j, i) for i, j in HOPS]


def hop(value):
    return lax.ppermute(value, ("section", SEQ), HOPS)


def beside_swap(value):
    pairs = [((2 * k - 1) % N_SEQ, 2 * k) for k in range(N_SEQ // 2)]
    return lax.ppermute(value, SEQ, pairs + [(j, i) for i, j in pairs])


def dot(left, right):
    return jnp.dot(left, right, preferred_element_type=F32)


def dot_nt(left, right):
    return lax.dot_general(left, right, (((1,), (1,)), ((), ())), preferred_element_type=F32)


def dot_tn(left, right):
    return lax.dot_general(left, right, (((0,), (0,)), ((), ())), preferred_element_type=F32)


def patchify(field):
    pairs = field.reshape(HALF, 2, HALF, 2 * C)
    return jnp.concatenate([pairs[:, 0], pairs[:, 1]], axis=-1).reshape(HALF * HALF, 4 * C)


def unpatchify(tokens):
    pairs = tokens.reshape(HALF, HALF, 4 * C)
    return jnp.stack([pairs[..., : 2 * C], pairs[..., 2 * C :]], axis=1).reshape(SIDE, HALF, 2 * C)


def silu(value):
    half = 0.5 * value
    return half + half * jnp.tanh(half)


def silu_slope(value):
    half = 0.5 * value
    t = jnp.tanh(half)
    return (0.5 + 0.5 * t) * (1.0 + half * (1.0 - t))


CHUNKS = 4
UNROLL = 4
VMEM = pl.BlockSpec(memory_space=pltpu.VMEM)
SMEM = pl.BlockSpec(memory_space=pltpu.SMEM)
ANY = pl.BlockSpec(memory_space=pl.ANY)


def conv_in_kernel(field, kernel_ref, left_ref, right_ref, turned=False):
    even, odd = field[..., :C], field[..., C:]
    column = lax.broadcasted_iota(jnp.int32, (SIDE, HALF, C), 1)
    before = jnp.where(column == 0, 0.0, pltpu.roll(odd, 1, 1))
    after = jnp.where(column == HALF - 1, 0.0, pltpu.roll(even, HALF - 1, 1))
    middle = field.astype(BF16)
    left_ref[1 : SIDE + 1, :, C:] = middle
    left_ref[1 : SIDE + 1, :, :C] = before.astype(BF16)
    right_ref[1 : SIDE + 1, :, : 2 * C] = middle
    right_ref[1 : SIDE + 1, :, 2 * C :] = after.astype(BF16)
    out = []
    for ref in (left_ref, right_ref):
        edge = jnp.zeros((HALF, 3 * C), BF16)
        ref[0] = edge
        ref[SIDE + 1] = edge
        total = None
        for row in range(3):
            taps = ref[row : row + SIDE].reshape(SIDE * HALF, 3 * C)
            if turned:
                for column in range(3):
                    tap = (2 - row) * 3 + 2 - column
                    weight = kernel_ref[tap * C : (tap + 1) * C]
                    term = dot_nt(taps[:, column * C : (column + 1) * C], weight)
                    total = term if total is None else total + term
            else:
                term = dot(taps, kernel_ref[row * 3 * C : (row + 1) * 3 * C])
                total = term if total is None else total + term
        out.append(total.reshape(SIDE, HALF, C))
    return jnp.concatenate(out, axis=-1)


def choose(to_ref, mine, own_ref, top_ref, low_ref):
    @pl.when(mine)
    def _():
        to_ref[...] = own_ref[...]

    @pl.when(jnp.logical_not(mine))
    def _():
        to_ref[: top_ref.shape[0]] = top_ref[...]
        to_ref[top_ref.shape[0] :] = low_ref[...]


def rounded(value):
    return value.astype(BF16).astype(F32)


class Weights:
    def __init__(self, index_ref, own_ref, near_ref, far_ref, both_ref, sems, parity):
        self.args = (index_ref, own_ref, near_ref, far_ref, both_ref, sems, parity)
        self.rows = both_ref.shape[1] // CHUNKS
        self.share = both_ref.shape[1] // N_SEQ

    def start(self, own=True):
        index_ref, own_ref, near_ref, far_ref, both_ref, sems, parity = self.args
        per = N_SEQ // CHUNKS
        for block in range(N_SEQ if own else 0):
            source = pl.multiple_of(index_ref[block] * self.share, self.share)
            pltpu.make_async_copy(
                own_ref.at[pl.ds(source, self.share)],
                both_ref.at[parity, pl.ds(block * self.share, self.share)],
                sems.at[parity, block // per],
            ).start()
        for chunk in range(CHUNKS):
            source = near_ref if chunk < CHUNKS // 2 else far_ref
            pltpu.make_async_copy(
                source.at[pl.ds(chunk % (CHUNKS // 2) * self.rows, self.rows)],
                both_ref.at[1 - parity, pl.ds(chunk * self.rows, self.rows)],
                sems.at[1 - parity, chunk],
            ).start()

    def sweep(self, slot, step, wait=False):
        _, _, near_ref, _, both_ref, sems, _ = self.args

        @pl.loop(0, CHUNKS, unroll=UNROLL)
        def _(chunk):
            rows = pl.ds(pl.multiple_of(chunk * self.rows, self.rows), self.rows)
            if wait:
                pltpu.make_async_copy(
                    near_ref.at[pl.ds(0, self.rows)], both_ref.at[slot, rows], sems.at[slot, chunk]
                ).wait()
            step(chunk, both_ref[slot, rows])


def weight_scratch(width, depth):
    return [pltpu.VMEM((2, width, depth), BF16), pltpu.SemaphoreType.DMA((2, CHUNKS))]


def lanes(chunk, count):
    return pl.ds(pl.multiple_of(chunk * count, count), count)


TAPS = [pltpu.VMEM((SIDE + 2, HALF, 3 * C), BF16)] * 2
TOKENS = HALF * HALF
KERNEL = [pltpu.VMEM((9 * C, C), BF16)]


def params(mib):
    return pltpu.CompilerParams(vmem_limit_bytes=mib * 1024 * 1024)


def call(body, outs, args, after=()):
    count = len(args)

    def with_after(*refs):
        body(*refs[:count], *refs[count + len(after) :])

    return pl.pallas_call(
        with_after,
        out_shape=[jax.ShapeDtypeStruct(shape, kind) for shape, kind in outs],
        in_specs=[VMEM] * count + [ANY] * len(after),
        out_specs=[VMEM] * len(outs),
        compiler_params=params(20),
    )(*args, *after)


def run_rows(phase, features, cotangent):
    count = features.shape[0]
    wide = 2 * C

    def body(phase_ref, features_ref, cotangent_ref, *refs):
        late_ref, beside_ref, value_ref = refs[2:]
        for side, ref in enumerate((features_ref, cotangent_ref)):
            for part in range(2):
                value_ref[part] = ref[:, :, part * 128 : (part + 1) * 128].astype(F32)
            quarters = [
                value_ref[part, :, pl.ds(column, HALF, stride=2), :]
                for column in range(2)
                for part in range(2)
            ]
            rows = jnp.concatenate(quarters, axis=-1).astype(BF16)
            refs[side][...] = rows
            at = slice(side * wide, (side + 1) * wide)
            late_ref[:, :, at] = rows[8:]

            @pl.when(phase_ref[0] == 0)
            def _(rows=rows, at=at):
                beside_ref[:, :, at] = rows[16:]

            @pl.when(phase_ref[0] != 0)
            def _(rows=rows, at=at):
                beside_ref[:, :, at] = rows[:8]

    shapes = [(count, HALF, wide)] * 2 + [(16, HALF, 2 * wide), (8, HALF, 2 * wide)]
    return pl.pallas_call(
        body,
        out_shape=[jax.ShapeDtypeStruct(shape, BF16) for shape in shapes],
        in_specs=[SMEM, VMEM, VMEM],
        out_specs=[VMEM] * 4,
        scratch_shapes=[pltpu.VMEM((2, count, SIDE, 128), F32)],
        compiler_params=params(12),
        name="rows",
    )(phase, features, cotangent)


def run_image(phase, rows, late, beside):
    def body(phase_ref, *refs):
        late_ref, beside_ref = refs[2:4]
        kind = phase_ref[0]
        for side in range(2):
            rows_ref, out_ref = refs[side], refs[4 + side]
            at = slice(side * 2 * C, (side + 1) * 2 * C)

            @pl.when(kind == 0)
            def _(rows_ref=rows_ref, out_ref=out_ref, at=at):
                out_ref[:16] = late_ref[:, :, at]
                out_ref[16:] = rows_ref[:16]

            @pl.when(kind == 1)
            def _(rows_ref=rows_ref, out_ref=out_ref, at=at):
                out_ref[:8] = beside_ref[:, :, at]
                out_ref[8:] = rows_ref[...]

            @pl.when(kind == 2)
            def _(rows_ref=rows_ref, out_ref=out_ref, at=at):
                out_ref[:24] = rows_ref[...]
                out_ref[24:] = beside_ref[:, :, at]

            @pl.when(kind == 3)
            def _(out_ref=out_ref):
                out_ref[...] = jnp.zeros_like(out_ref)

    return pl.pallas_call(
        body,
        out_shape=[jax.ShapeDtypeStruct((SIDE, HALF, 2 * C), BF16)] * 2,
        in_specs=[SMEM] + [VMEM] * 4,
        out_specs=[VMEM] * 2,
        compiler_params=params(12),
        name="image",
    )(phase, *rows, late, beside)


def run_start(section, image, kernels, turned):
    def body(section_ref, image_ref, own_ref, top_ref, low_ref, out_ref, left_ref, right_ref, kernel_ref):
        where = section_ref[0]

        @pl.when((where >= 2) if turned else (where < 2))
        def _():
            choose(kernel_ref, where == (3 if turned else 0), own_ref, top_ref, low_ref)
            field = image_ref[...].astype(F32)
            field = conv_in_kernel(field, kernel_ref, left_ref, right_ref, turned=turned)
            out_ref[...] = field.astype(out_ref.dtype)

    return pl.pallas_call(
        body,
        out_shape=jax.ShapeDtypeStruct((SIDE, HALF, 2 * C), F32 if turned else BF16),
        in_specs=[SMEM] + [VMEM] * 4,
        out_specs=VMEM,
        scratch_shapes=TAPS + KERNEL,
        compiler_params=params(16),
        name="start_turned" if turned else "start",
    )(section, image, *kernels)


def run_piece(blocks, weight):
    share, depth = weight.shape[0] // N_SEQ, weight.shape[1]

    def body(index_ref, weight_ref, out_ref):
        out_ref[...] = weight_ref[...]

    return pl.pallas_call(
        body,
        grid_spec=pltpu.PrefetchScalarGridSpec(
            num_scalar_prefetch=1,
            grid=(2,),
            in_specs=[pl.BlockSpec((share, depth), lambda i, index: (index[i], 0))],
            out_specs=pl.BlockSpec((share, depth), lambda i, index: (i, 0)),
        ),
        out_shape=jax.ShapeDtypeStruct((2 * share, depth), weight.dtype),
    )(blocks, weight)


def gather_partner(piece, kernel, images, before):
    rows, depth = piece.shape
    half, part = depth // 2, depth // 4
    kernel_rows = kernel.shape[0] // 2
    kernel_part = ((kernel_rows, kernel.shape[1]), BF16)

    def split(piece_ref, kernel_ref, first_ref, second_ref, top_ref):
        first_ref[...] = piece_ref[:, :half]
        second_ref[...] = piece_ref[:, half:]
        top_ref[...] = kernel_ref[:kernel_rows]

    outs = [((rows, half), BF16)] * 2 + [kernel_part]
    first, second, top = call(split, outs, (piece, kernel), before)
    got = [flip(first, m) for m in (X1, X1 ^ X3, X3)] + [flip(second, m) for m in (Y1, Y1 ^ Y3, Y3)]
    top = partner(top)
    image, cotangent = images()
    cotangent = hop(cotangent)

    def stack(*refs):
        for side in range(2):
            for far in range(4):
                source = refs[side] if far == 0 else refs[2 + 3 * side + far - 1]
                refs[9 + side][far * rows : (far + 1) * rows] = source[...]
        refs[11][...] = refs[8][kernel_rows:]

    outs = [((4 * rows, half), BF16)] * 2 + [kernel_part]
    *wide, low_rows = call(stack, outs, (first, second, *got, kernel), (top, image))
    rings = ((Y1, Y3), (X1, X3))
    near = [flip(value, ring[0]) for value, ring in zip(wide, rings)]
    far = [flip(value, ring[1]) for value, ring in zip(wide, rings)]
    low_rows = partner(low_rows)
    kernels = (kernel, top, low_rows)
    section = lax.axis_index("section").reshape(1)
    skip_field = run_start(section, image, kernels, turned=False)

    def cut(*refs):
        for side in range(2):
            refs[4 + 2 * side][...] = refs[side][:, :part]
            refs[5 + 2 * side][...] = refs[2 + side][:, part:]

    outs = [((4 * rows, part), BF16)] * 4
    parts = call(cut, outs, (*far, *near), (low_rows, cotangent))
    low = [flip(parts[2 * side], ring[0]) for side, ring in enumerate(rings)]
    high = [flip(parts[2 * side + 1], ring[1]) for side, ring in enumerate(rings)]

    def join(*refs):
        out_ref = refs[10]
        for side in range(2):
            base = side * half
            mine, one, three = refs[side], refs[2 + side], refs[4 + side]
            for outer in range(4):
                sources = {0: [mine], 1: [one], 3: [three], 2: [refs[6 + side], refs[8 + side]]}[outer]
                for j, source in enumerate(sources):
                    count = source.shape[1]
                    at = slice(base + j * count, base + (j + 1) * count)
                    for inner in range(4):
                        block = source[inner * rows : (inner + 1) * rows]
                        x, y = (inner, outer) if side == 0 else (outer, inner)
                        start = (4 * x + y) * rows
                        out_ref[start : start + rows, at] = block

    args = (*wide, *near, *far, *low, *high)
    held = call(join, [((16 * rows, depth), BF16)], args, (skip_field,))[0]
    return held, kernels, skip_field, cotangent


def run_forward(section, blocks, skip, own, near, far, codes, kernels):
    width, depth = own.shape
    cols = width // CHUNKS

    def body(
        section_ref, index_ref, skip_ref, own_ref, near_ref, far_ref, one_ref, two_ref, cos_ref,
        sin_ref, own_kernel_ref, top_ref, low_ref, tokens_ref, act_ref, lift_ref, field_ref, sum_ref,
        left_ref, right_ref, kernel_ref, both_ref, sems,
    ):
        parity = section_ref[0] % 2

        @pl.when(section_ref[0] < 2)
        def _():
            weights = Weights(index_ref, own_ref, near_ref, far_ref, both_ref, sems, parity)
            weights.start()
            choose(kernel_ref, parity == 1, own_kernel_ref, top_ref, low_ref)
            patch = patchify(skip_ref[...])
            sum_ref[...] = jnp.zeros_like(sum_ref)

            def embed(chunk, rows):
                at = lanes(chunk, cols)
                code = one_ref[:, at][:, None] * cos_ref[:, at][None]
                code += two_ref[:, at][:, None] * sin_ref[:, at][None]
                value = dot_nt(patch, rows) + code.reshape(TOKENS, cols)
                value = value.astype(BF16)
                tokens_ref[:, at] = value
                value = value.astype(F32)
                sum_ref[...] += jnp.sum(value * value, axis=-1, keepdims=True)

            weights.sweep(0, embed, wait=True)
            scale = lax.rsqrt(sum_ref[...] * (1.0 / width) + NORM_EPS)
            lift_ref[...] = jnp.zeros_like(lift_ref)

            def raise_up(chunk, rows):
                at = lanes(chunk, cols)
                active = silu(tokens_ref[:, at].astype(F32) * scale).astype(BF16)
                act_ref[:, at] = active
                lift_ref[...] += dot(active, rows)

            weights.sweep(1, raise_up, wait=True)

            field = unpatchify(rounded(silu(lift_ref[...])))
            field_ref[...] = conv_in_kernel(field, kernel_ref, left_ref, right_ref).astype(BF16)

    return pl.pallas_call(
        body,
        out_shape=[
            jax.ShapeDtypeStruct((TOKENS, width), BF16),
            jax.ShapeDtypeStruct((TOKENS, width), BF16),
            jax.ShapeDtypeStruct((TOKENS, depth), F32),
            jax.ShapeDtypeStruct((SIDE, HALF, 2 * C), BF16),
        ],
        in_specs=[SMEM, SMEM, VMEM] + [ANY] * 3 + [VMEM] * 7,
        out_specs=[VMEM] * 4,
        scratch_shapes=[pltpu.VMEM((TOKENS, 1), F32)]
        + TAPS
        + KERNEL
        + weight_scratch(width, depth),
        compiler_params=params(32),
        name="forward_first_pair",
    )(section, blocks, skip, own, near, far, *codes, *kernels)


def run_second_pair(section, blocks, second, skip, start, own, near, far, kernels):
    width, depth = own.shape
    cols = width // CHUNKS

    def body(
        section_ref, index_ref, second_ref, skip_ref, start_ref, own_ref, near_ref, far_ref,
        own_kernel_ref, top_ref, low_ref, back_ref, side_ref, patch_ref, sum_ref, left_ref,
        right_ref, kernel_ref, tokens_ref, inner_ref, lift_ref, both_ref, sems,
    ):
        parity = section_ref[0] % 2

        @pl.when(section_ref[0] >= 2)
        def _():
            weights = Weights(index_ref, own_ref, near_ref, far_ref, both_ref, sems, parity)
            weights.start()
            choose(kernel_ref, parity == 0, own_kernel_ref, top_ref, low_ref)
            field = rounded(silu(second_ref[...].astype(F32)))
            field = conv_in_kernel(field, kernel_ref, left_ref, right_ref).astype(BF16)
            patch_ref[...] = patchify(field)
            sum_ref[...] = jnp.zeros_like(sum_ref)

            def embed(chunk, rows):
                value = dot_nt(patch_ref[...], rows).astype(BF16)
                tokens_ref[:, lanes(chunk, cols)] = value
                value = value.astype(F32)
                sum_ref[...] += jnp.sum(value * value, axis=-1, keepdims=True)

            weights.sweep(0, embed, wait=True)
            scale = lax.rsqrt(sum_ref[...] * (1.0 / width) + NORM_EPS)
            lift_ref[...] = patchify(skip_ref[...]).astype(F32)

            def raise_up(chunk, rows):
                at = lanes(chunk, cols)
                active = silu(tokens_ref[:, at].astype(F32) * scale).astype(BF16)
                side_ref[:, at] = active
                lift_ref[...] += dot(active, rows)

            weights.sweep(1, raise_up, wait=True)
            last_patch = (patchify(start_ref[...]) * silu_slope(lift_ref[...])).astype(BF16)

            @pl.when(parity == 1)
            def _():
                patch_ref[...] = last_patch

            sum_ref[...] = jnp.zeros_like(sum_ref)

            def descend(chunk, rows):
                at = lanes(chunk, cols)
                normal = tokens_ref[:, at].astype(F32) * scale
                inner = dot_nt(last_patch, rows) * silu_slope(normal)
                inner_ref[:, at] = inner
                sum_ref[...] += jnp.sum(inner * normal, axis=-1, keepdims=True)

            weights.sweep(1, descend)
            mean = sum_ref[...] * (1.0 / width)
            lift_ref[...] = jnp.zeros_like(lift_ref)

            def lower(chunk, rows):
                at = lanes(chunk, cols)
                normal = tokens_ref[:, at].astype(F32) * scale
                back = (scale * (inner_ref[:, at] - normal * mean)).astype(BF16)

                @pl.when(parity == 0)
                def _():
                    side_ref[:, at] = back

                lift_ref[...] += dot(back, rows)

            weights.sweep(0, lower)
            field = unpatchify(rounded(lift_ref[...]))
            field = conv_in_kernel(field, kernel_ref, left_ref, right_ref, turned=True)
            back_ref[...] = (field * silu_slope(second_ref[...].astype(F32))).astype(BF16)

    return pl.pallas_call(
        body,
        out_shape=[
            jax.ShapeDtypeStruct((SIDE, HALF, 2 * C), BF16),
            jax.ShapeDtypeStruct((TOKENS, width), BF16),
            jax.ShapeDtypeStruct((TOKENS, depth), BF16),
        ],
        in_specs=[SMEM, SMEM] + [VMEM] * 3 + [ANY] * 3 + [VMEM] * 3,
        out_specs=[VMEM] * 3,
        scratch_shapes=[pltpu.VMEM((TOKENS, 1), F32)]
        + TAPS
        + KERNEL
        + [
            pltpu.VMEM((TOKENS, width), BF16),
            pltpu.VMEM((TOKENS, width), F32),
            pltpu.VMEM((TOKENS, depth), F32),
        ]
        + weight_scratch(width, depth),
        compiler_params=params(38),
        name="second_pair",
    )(section, blocks, second, skip, start, own, near, far, *kernels)


def run_back(section, given, skip, lift, tokens, prior, patch, near, far, kernels):
    width, depth = tokens.shape[1], lift.shape[1]
    cols = width // CHUNKS

    def body(
        section_ref, given_ref, skip_ref, lift_ref, tokens_ref, prior_ref, known_ref, near_ref,
        far_ref, own_kernel_ref, top_ref, low_ref, keep_ref, send_ref, patch_ref, sum_ref, left_ref,
        right_ref, kernel_ref, inner_ref, both_ref, sems,
    ):
        where = section_ref[0]
        weights = Weights(None, None, near_ref, far_ref, both_ref, sems, 1)

        @pl.when(where == 0)
        def _():
            weights.start(own=False)

        @pl.when(where >= 1)
        def _():
            keep_ref[...] = prior_ref[:, : width // 2]
            send_ref[...] = prior_ref[:, width // 2 :]

        @pl.when(where >= 2)
        def _():
            patch_ref[...] = known_ref[...]

        @pl.when(where < 2)
        def _():
            choose(kernel_ref, where == 1, own_kernel_ref, top_ref, low_ref)
            field = given_ref[...].astype(F32)
            field = conv_in_kernel(field, kernel_ref, left_ref, right_ref, turned=True)
            patch_ref[...] = (patchify(field) * silu_slope(lift_ref[...])).astype(BF16)

        @pl.when(where == 0)
        def _():
            sum_ref[...] = jnp.zeros_like(sum_ref)

            @pl.loop(0, CHUNKS, unroll=UNROLL)
            def _(chunk):
                value = tokens_ref[:, lanes(chunk, cols)].astype(F32)
                sum_ref[...] += jnp.sum(value * value, axis=-1, keepdims=True)

            scale = lax.rsqrt(sum_ref[...] * (1.0 / width) + NORM_EPS)
            sum_ref[...] = jnp.zeros_like(sum_ref)

            def descend(chunk, rows):
                at = lanes(chunk, cols)
                normal = tokens_ref[:, at].astype(F32) * scale
                inner = dot_nt(patch_ref[...], rows) * silu_slope(normal)
                inner_ref[:, at] = inner
                sum_ref[...] += jnp.sum(inner * normal, axis=-1, keepdims=True)

            weights.sweep(0, descend, wait=True)
            mean = sum_ref[...] * (1.0 / width)

            for first, ref in ((0, keep_ref), (CHUNKS // 2, send_ref)):

                @pl.loop(0, CHUNKS // 2, unroll=UNROLL)
                def _(i, first=first, ref=ref):
                    at = lanes(first + i, cols)
                    normal = tokens_ref[:, at].astype(F32) * scale
                    back = scale * (inner_ref[:, at] - normal * mean)
                    ref[:, lanes(i, cols)] = back.astype(BF16)

            patch_ref[...] = patchify(skip_ref[...])

    return pl.pallas_call(
        body,
        out_shape=[
            jax.ShapeDtypeStruct((TOKENS, width // 2), BF16),
            jax.ShapeDtypeStruct((TOKENS, width // 2), BF16),
            jax.ShapeDtypeStruct((TOKENS, depth), BF16),
        ],
        in_specs=[SMEM] + [VMEM] * 6 + [ANY] * 2 + [VMEM] * 3,
        out_specs=[VMEM] * 3,
        scratch_shapes=[pltpu.VMEM((TOKENS, 1), F32)]
        + TAPS
        + KERNEL
        + [
            pltpu.VMEM((TOKENS, width), F32),
            pltpu.VMEM((1, width, depth), BF16),
            pltpu.SemaphoreType.DMA((1, CHUNKS)),
        ],
        compiler_params=params(30),
        name="back_first_pair",
    )(section, given, skip, lift, tokens, prior, patch, near, far, *kernels)


SENT = {"a": (1, 2), "b": (3, 2)}
KEPT = {"a": (0, 3), "b": (0, 1)}


def run_partial(keep, recv, patch, patch_recv):
    half, depth = keep.shape[1], patch.shape[1]
    part, block = depth // 4, half // 16

    def body(keep_ref, recv_ref, patch_ref, other_ref, *out_refs):
        tokens = jnp.concatenate([keep_ref[...], recv_ref[...]], axis=0)
        patches = jnp.concatenate([patch_ref[...], other_ref[...]], axis=0)
        for column in range(4):
            name = "ab"[column % 2]
            sent_ref, kept_ref = out_refs[column], out_refs[4 + column]
            right = patches[:, column * part : (column + 1) * part]
            for i in range(2):
                for ref, far in ((sent_ref, SENT[name][i]), (kept_ref, KEPT[name][i])):
                    if column < 2:
                        left = tokens[:, far * 4 * block : (far + 1) * 4 * block]
                    else:
                        left = jnp.concatenate(
                            [tokens[:, (4 * j + far) * block :][:, :block] for j in range(4)], axis=1
                        )
                    ref[i] = dot_tn(left, right).astype(ref.dtype)

    shape = (2, 4 * block, part)
    outs = call(body, [(shape, BF16)] * 4 + [(shape, F32)] * 4, (keep, recv, patch, patch_recv))
    return outs[:4], outs[4:]


FIRST_RINGS = ((X1, X3), (X3, X1), (Y1, Y3), (Y3, Y1))


def run_sum(partial):
    sent, kept = partial
    got = [flip(value, ring[0]) for value, ring in zip(sent, FIRST_RINGS)]
    rows, part = kept[0].shape[1:]
    block = rows // 4

    def add_once(*refs):
        kept_refs, got_refs, sent_refs, out_refs = refs[:4], refs[4:8], refs[8:12], refs[12:]
        for kept_ref, got_ref, sent_ref, out_ref in zip(kept_refs, got_refs, sent_refs, out_refs):
            total = kept_ref[...] + got_ref[...].astype(F32)
            out_ref[...] = total[0]
            sent_ref[...] = total[1].astype(BF16)

    shape = (rows, part)
    outs = call(add_once, [(shape, BF16)] * 4 + [(shape, F32)] * 4, (*kept, *got))
    got = [flip(value, ring[1]) for value, ring in zip(outs[:4], FIRST_RINGS)]

    def add_twice(*refs):
        kept_refs, got_refs, out_refs = refs[:4], refs[4:8], refs[8:]
        for half in range(2):
            a, b = 2 * half, 2 * half + 1
            total = [kept_refs[i][...] + got_refs[i][...].astype(F32) for i in (a, b)]
            total = jnp.concatenate(total, axis=1)
            for far in range(4):
                ref = out_refs[4 * half + far]
                ref[...] = total[far * block : (far + 1) * block].astype(ref.dtype)

    shape = (block, 2 * part)
    kinds = [F32, BF16, BF16, BF16] * 2
    outs = call(add_twice, [(shape, kind) for kind in kinds], (*outs[4:], *got))
    got = [flip(v, m) for v, m in zip(outs[1:4], (Y1, Y1 ^ Y3, Y3))]
    got += [flip(v, m) for v, m in zip(outs[5:8], (X1, X1 ^ X3, X3))]

    def add_last(*refs):
        for half in range(2):
            total = refs[half][...]
            for ref in refs[2 + 3 * half : 5 + 3 * half]:
                total += ref[...].astype(F32)
            at = slice(half * 2 * part, (half + 1) * 2 * part)
            refs[8][:, at] = total[: block // 2]
            refs[9][:, at] = total[block // 2 :].astype(BF16)

    shape = (block // 2, 4 * part)
    mine, away = call(add_last, [(shape, F32), (shape, BF16)], (outs[0], outs[4], *got))
    return mine + flip(away, ZH).astype(F32)


def on_device(features, conv_kernels, patch_weights, positions, out_cotangent):
    weight = patch_weights[0]
    width, depth = weight.shape
    kernel = conv_kernels[0].reshape(9 * C, C)
    section = lax.axis_index("section")
    place = lax.axis_index(SEQ)
    first_pair = section < 2

    order = jnp.arange(N_SEQ, dtype=jnp.int32)
    away = ((order & 1) << 5) | (((order >> 3) & 3) << 3) | (((order >> 1) & 3) << 1) | (order >> 5)
    blocks = away ^ place

    here, phase = section.reshape(1), (place % 4).reshape(1)
    piece = partner(run_piece(blocks, weight))
    *rows, late, beside = run_rows(phase, features, out_cotangent)
    late, beside = beside_swap(late), flip(beside, CORE)

    image_id = jnp.minimum(3 * (place // 4) + place % 4, positions.shape[0] - 1)
    begin = positions[image_id]
    half = width // 2
    feature = (blocks[:, None] * (width // N_SEQ) + jnp.arange(width // N_SEQ)[None, :]).reshape(-1)
    rates = jnp.exp((feature % half).astype(F32) * (-math.log(10000.0) / half))
    is_sin = (feature < half)[None, :]
    steps = jnp.arange(HALF, dtype=jnp.int32)
    row_angle = (begin + HALF * steps).astype(F32)[:, None] * rates[None, :]
    col_angle = steps.astype(F32)[:, None] * rates[None, :]
    row_sin, row_cos = jnp.sin(row_angle), jnp.cos(row_angle)
    row_one = jnp.where(is_sin, row_sin, row_cos)
    row_two = jnp.where(is_sin, row_cos, -row_sin)
    col_cos, col_sin = jnp.cos(col_angle), jnp.sin(col_angle)

    codes = (row_one, row_two, col_cos, col_sin)

    near, kernels, skip_field, cotangent = gather_partner(
        piece, kernel, lambda: run_image(phase, rows, late, beside), (late, beside, *codes)
    )
    far = flip(near, CORE)
    skip_recv = hop(skip_field)
    start = run_start(here, cotangent, kernels, turned=True)

    tokens, active, first_lift, second_field = run_forward(
        here, blocks, skip_field, weight, near, far, codes, kernels
    )
    second_back, side, patch = run_second_pair(
        here, blocks, hop(second_field), skip_recv, start, weight, near, far, kernels
    )
    prior = jnp.where(first_pair, active, side)
    keep, send, patch = run_back(
        here, hop(second_back), skip_field, first_lift, tokens, prior, patch, near, far,
        kernels,
    )

    summed = run_sum(run_partial(keep, flip(send, CORE), patch, flip(patch, CORE)))
    tokens_in_all = positions.shape[0] * HALF * HALF
    return (summed * (1.0 / math.sqrt(tokens_in_all)))[None]


def solution(mesh):
    in_specs = (
        P("seq", None, None),
        P("section", None, None, None, None),
        P("section", None, None),
        P(),
        P("seq", None, None),
    )
    out_specs = P("section", "seq", None)
    return jax.shard_map(
        on_device, mesh=mesh, in_specs=in_specs, out_specs=out_specs, check_vma=False
    )
```

```python
import math

import jax
import jax.numpy as jnp
from jax import lax
from jax.experimental import pallas as pl
from jax.experimental.pallas import tpu as pltpu
from jax.sharding import PartitionSpec as P

NORM_EPS = 1e-05
BF16 = jnp.bfloat16
F32 = jnp.float32
SIDE = 32
HALF = SIDE // 2
C = 256
N_SEQ = 64
SEQ = "seq"

X1, X3, Y1, Y3, CORE, ZH = (1 << 3, 3 << 3, 1 << 1, 3 << 1, 1, 1 << 5)


def flip(value, mask):
    return lax.ppermute(value, SEQ, [(i, i ^ mask) for i in range(N_SEQ)])


def partner(value):
    return lax.ppermute(value, "section", [(0, 1), (1, 0), (2, 3), (3, 2)])


HOPS = [(1 * N_SEQ + q, 2 * N_SEQ + q) for q in range(N_SEQ)]
HOPS += [(q, 3 * N_SEQ + (q ^ ZH)) for q in range(N_SEQ)]
HOPS += [(j, i) for i, j in HOPS]


def hop(value):
    return lax.ppermute(value, ("section", SEQ), HOPS)


def beside_swap(value):
    pairs = [((2 * k - 1) % N_SEQ, 2 * k) for k in range(N_SEQ // 2)]
    return lax.ppermute(value, SEQ, pairs + [(j, i) for i, j in pairs])


def dot(left, right):
    return jnp.dot(left, right, preferred_element_type=F32)


def dot_nt(left, right):
    return lax.dot_general(left, right, (((1,), (1,)), ((), ())), preferred_element_type=F32)


def dot_tn(left, right):
    return lax.dot_general(left, right, (((0,), (0,)), ((), ())), preferred_element_type=F32)


def patchify(field):
    pairs = field.reshape(HALF, 2, HALF, 2 * C)
    return jnp.concatenate([pairs[:, 0], pairs[:, 1]], axis=-1).reshape(HALF * HALF, 4 * C)


def unpatchify(tokens):
    pairs = tokens.reshape(HALF, HALF, 4 * C)
    return jnp.stack([pairs[..., : 2 * C], pairs[..., 2 * C :]], axis=1).reshape(SIDE, HALF, 2 * C)


def silu(value):
    half = 0.5 * value
    return half + half * jnp.tanh(half)


def silu_slope(value):
    half = 0.5 * value
    t = jnp.tanh(half)
    return (0.5 + 0.5 * t) * (1.0 + half * (1.0 - t))


CHUNKS = 4
UNROLL = 4
VMEM = pl.BlockSpec(memory_space=pltpu.VMEM)
SMEM = pl.BlockSpec(memory_space=pltpu.SMEM)
ANY = pl.BlockSpec(memory_space=pl.ANY)
HBM = pl.BlockSpec(memory_space=pltpu.HBM)


def conv_in_kernel(field, kernel_ref, left_ref, right_ref, turned=False):
    even, odd = field[..., :C], field[..., C:]
    column = lax.broadcasted_iota(jnp.int32, (SIDE, HALF, C), 1)
    before = jnp.where(column == 0, 0.0, pltpu.roll(odd, 1, 1))
    after = jnp.where(column == HALF - 1, 0.0, pltpu.roll(even, HALF - 1, 1))
    middle = field.astype(BF16)
    left_ref[1 : SIDE + 1, :, C:] = middle
    left_ref[1 : SIDE + 1, :, :C] = before.astype(BF16)
    right_ref[1 : SIDE + 1, :, : 2 * C] = middle
    right_ref[1 : SIDE + 1, :, 2 * C :] = after.astype(BF16)
    out = []
    for ref in (left_ref, right_ref):
        edge = jnp.zeros((HALF, 3 * C), BF16)
        ref[0] = edge
        ref[SIDE + 1] = edge
        total = None
        for row in range(3):
            taps = ref[row : row + SIDE].reshape(SIDE * HALF, 3 * C)
            if turned:
                for column in range(3):
                    tap = (2 - row) * 3 + 2 - column
                    weight = kernel_ref[tap * C : (tap + 1) * C]
                    term = dot_nt(taps[:, column * C : (column + 1) * C], weight)
                    total = term if total is None else total + term
            else:
                term = dot(taps, kernel_ref[row * 3 * C : (row + 1) * 3 * C])
                total = term if total is None else total + term
        out.append(total.reshape(SIDE, HALF, C))
    return jnp.concatenate(out, axis=-1)


def choose(to_ref, mine, own_ref, other_ref):
    @pl.when(mine)
    def _():
        to_ref[...] = own_ref[...]

    @pl.when(jnp.logical_not(mine))
    def _():
        to_ref[...] = other_ref[...]


def rounded(value):
    return value.astype(BF16).astype(F32)


class Weights:
    def __init__(self, index_ref, own_ref, near_ref, far_ref, both_ref, sems, parity):
        self.args = (index_ref, own_ref, near_ref, far_ref, both_ref, sems, parity)
        self.rows = both_ref.shape[1] // CHUNKS
        self.share = both_ref.shape[1] // N_SEQ

    def start(self, own=True):
        index_ref, own_ref, near_ref, far_ref, both_ref, sems, parity = self.args
        per = N_SEQ // CHUNKS
        for block in range(N_SEQ if own else 0):
            source = pl.multiple_of(index_ref[block] * self.share, self.share)
            pltpu.make_async_copy(
                own_ref.at[pl.ds(source, self.share)],
                both_ref.at[parity, pl.ds(block * self.share, self.share)],
                sems.at[parity, block // per],
            ).start()
        for chunk in range(CHUNKS):
            source = near_ref if chunk < CHUNKS // 2 else far_ref
            pltpu.make_async_copy(
                source.at[pl.ds(chunk % (CHUNKS // 2) * self.rows, self.rows)],
                both_ref.at[1 - parity, pl.ds(chunk * self.rows, self.rows)],
                sems.at[1 - parity, chunk],
            ).start()

    def sweep(self, slot, step, wait=False):
        _, _, near_ref, _, both_ref, sems, _ = self.args

        @pl.loop(0, CHUNKS, unroll=UNROLL)
        def _(chunk):
            rows = pl.ds(pl.multiple_of(chunk * self.rows, self.rows), self.rows)
            if wait:
                pltpu.make_async_copy(
                    near_ref.at[pl.ds(0, self.rows)], both_ref.at[slot, rows], sems.at[slot, chunk]
                ).wait()
            step(chunk, both_ref[slot, rows])


def weight_scratch(width, depth):
    return [pltpu.VMEM((2, width, depth), BF16), pltpu.SemaphoreType.DMA((2, CHUNKS))]


def lanes(chunk, count):
    return pl.ds(pl.multiple_of(chunk * count, count), count)


TAPS = [pltpu.VMEM((SIDE + 2, HALF, 3 * C), BF16)] * 2
TOKENS = HALF * HALF
KERNEL = [pltpu.VMEM((9 * C, C), BF16)]


def params(mib):
    return pltpu.CompilerParams(vmem_limit_bytes=mib * 1024 * 1024)


def call(body, outs, args, after=()):
    count = len(args)

    def with_after(*refs):
        body(*refs[:count], *refs[count + len(after) :])

    return pl.pallas_call(
        with_after,
        out_shape=[jax.ShapeDtypeStruct(shape, kind) for shape, kind in outs],
        in_specs=[VMEM] * count + [ANY] * len(after),
        out_specs=[VMEM] * len(outs),
        compiler_params=params(20),
    )(*args, *after)


def run_rows(phase, features, cotangent, after):
    count = features.shape[0]
    wide = 2 * C

    def body(phase_ref, features_ref, cotangent_ref, _, *refs):
        late_ref, beside_ref, value_ref = refs[2:]
        for side, ref in enumerate((features_ref, cotangent_ref)):
            for part in range(2):
                value_ref[part] = ref[:, :, part * 128 : (part + 1) * 128].astype(F32)
            quarters = [
                value_ref[part, :, pl.ds(column, HALF, stride=2), :]
                for column in range(2)
                for part in range(2)
            ]
            rows = jnp.concatenate(quarters, axis=-1).astype(BF16)
            refs[side][...] = rows
            at = slice(side * wide, (side + 1) * wide)
            late_ref[:, :, at] = rows[8:]

            @pl.when(phase_ref[0] == 0)
            def _(rows=rows, at=at):
                beside_ref[:, :, at] = rows[16:]

            @pl.when(phase_ref[0] != 0)
            def _(rows=rows, at=at):
                beside_ref[:, :, at] = rows[:8]

    shapes = [(count, HALF, wide)] * 2 + [(16, HALF, 2 * wide), (8, HALF, 2 * wide)]
    return pl.pallas_call(
        body,
        out_shape=[jax.ShapeDtypeStruct(shape, BF16) for shape in shapes],
        in_specs=[SMEM, VMEM, VMEM, ANY],
        out_specs=[VMEM] * 4,
        scratch_shapes=[pltpu.VMEM((2, count, SIDE, 128), F32)],
        compiler_params=params(12),
        name="rows",
    )(phase, features, cotangent, after)


def run_image(phase, rows, late, beside):
    def body(phase_ref, *refs):
        late_ref, beside_ref = refs[2:4]
        kind = phase_ref[0]
        for side in range(2):
            rows_ref, out_ref = refs[side], refs[4 + side]
            at = slice(side * 2 * C, (side + 1) * 2 * C)

            @pl.when(kind == 0)
            def _(rows_ref=rows_ref, out_ref=out_ref, at=at):
                out_ref[:16] = late_ref[:, :, at]
                out_ref[16:] = rows_ref[:16]

            @pl.when(kind == 1)
            def _(rows_ref=rows_ref, out_ref=out_ref, at=at):
                out_ref[:8] = beside_ref[:, :, at]
                out_ref[8:] = rows_ref[...]

            @pl.when(kind == 2)
            def _(rows_ref=rows_ref, out_ref=out_ref, at=at):
                out_ref[:24] = rows_ref[...]
                out_ref[24:] = beside_ref[:, :, at]

            @pl.when(kind == 3)
            def _(out_ref=out_ref):
                out_ref[...] = jnp.zeros_like(out_ref)

    return pl.pallas_call(
        body,
        out_shape=[jax.ShapeDtypeStruct((SIDE, HALF, 2 * C), BF16)] * 2,
        in_specs=[SMEM] + [VMEM] * 4,
        out_specs=[VMEM] * 2,
        compiler_params=params(12),
        name="image",
    )(phase, *rows, late, beside)


def run_start(section, image, kernels, turned):
    def body(section_ref, image_ref, own_ref, other_ref, out_ref, left_ref, right_ref, kernel_ref):
        where = section_ref[0]

        @pl.when((where >= 2) if turned else (where < 2))
        def _():
            choose(kernel_ref, where == (3 if turned else 0), own_ref, other_ref)
            field = image_ref[...].astype(F32)
            field = conv_in_kernel(field, kernel_ref, left_ref, right_ref, turned=turned)
            out_ref[...] = field.astype(out_ref.dtype)

    return pl.pallas_call(
        body,
        out_shape=jax.ShapeDtypeStruct((SIDE, HALF, 2 * C), F32 if turned else BF16),
        in_specs=[SMEM] + [VMEM] * 3,
        out_specs=VMEM,
        scratch_shapes=TAPS + KERNEL,
        compiler_params=params(16),
        name="start_turned" if turned else "start",
    )(section, image, *kernels)


def run_piece(blocks, weight):
    share, depth = weight.shape[0] // N_SEQ, weight.shape[1]

    def body(index_ref, weight_ref, out_ref):
        out_ref[...] = weight_ref[...]

    return pl.pallas_call(
        body,
        grid_spec=pltpu.PrefetchScalarGridSpec(
            num_scalar_prefetch=1,
            grid=(2,),
            in_specs=[pl.BlockSpec((share, depth), lambda i, index: (index[i], 0))],
            out_specs=pl.BlockSpec((share, depth), lambda i, index: (i, 0)),
        ),
        out_shape=jax.ShapeDtypeStruct((2 * share, depth), weight.dtype),
        compiler_params=params(58),
    )(blocks, weight)


def gather_partner(piece, kernel, images, before):
    rows, depth = piece.shape
    half, part = depth // 2, depth // 4

    def split(piece_ref, kernel_ref, first_ref, second_ref, again_ref):
        first_ref[...] = piece_ref[:, :half]
        second_ref[...] = piece_ref[:, half:]
        again_ref[...] = kernel_ref[...]

    outs = [((rows, half), BF16)] * 2 + [(kernel.shape, BF16)]
    first, second, again = call(split, outs, (piece, kernel), before)
    got = [flip(first, m) for m in (X1, X1 ^ X3, X3)] + [flip(second, m) for m in (Y1, Y1 ^ Y3, Y3)]
    kernels = (kernel, partner(again))
    image, cotangent = images()
    cotangent = hop(cotangent)

    def stack(*refs):
        for side in range(2):
            for far in range(4):
                source = refs[side] if far == 0 else refs[2 + 3 * side + far - 1]
                refs[8 + side][far * rows : (far + 1) * rows] = source[...]

    wide = call(stack, [((4 * rows, half), BF16)] * 2, (first, second, *got), (image,))
    rings = ((Y1, Y3), (X1, X3))
    near = [flip(value, ring[0]) for value, ring in zip(wide, rings)]
    far = [flip(value, ring[1]) for value, ring in zip(wide, rings)]
    section = lax.axis_index("section").reshape(1)
    skip_field = run_start(section, image, kernels, turned=False)
    skip_recv = hop(skip_field)

    def cut(*refs):
        for side in range(2):
            refs[4 + 2 * side][...] = refs[side][:, :part]
            refs[5 + 2 * side][...] = refs[2 + side][:, part:]

    outs = [((4 * rows, part), BF16)] * 4
    parts = call(cut, outs, (*far, *near), (skip_field, cotangent))
    low = [flip(parts[2 * side], ring[0]) for side, ring in enumerate(rings)]
    high = [flip(parts[2 * side + 1], ring[1]) for side, ring in enumerate(rings)]

    def join(*refs):
        out_ref = refs[10]
        for side in range(2):
            base = side * half
            mine, one, three = refs[side], refs[2 + side], refs[4 + side]
            for outer in range(4):
                sources = {0: [mine], 1: [one], 3: [three], 2: [refs[6 + side], refs[8 + side]]}[outer]
                for j, source in enumerate(sources):
                    count = source.shape[1]
                    at = slice(base + j * count, base + (j + 1) * count)
                    for inner in range(4):
                        block = source[inner * rows : (inner + 1) * rows]
                        x, y = (inner, outer) if side == 0 else (outer, inner)
                        start = (4 * x + y) * rows
                        out_ref[start : start + rows, at] = block

    args = (*wide, *near, *far, *low, *high)
    held = call(join, [((16 * rows, depth), BF16)], args, (skip_recv,))[0]
    return held, kernels, skip_field, skip_recv, cotangent


def run_forward(section, blocks, skip, own, near, far, codes, kernels):
    width, depth = own.shape
    cols = width // CHUNKS

    def body(
        section_ref, index_ref, skip_ref, own_ref, near_ref, far_ref, one_ref, two_ref, cos_ref,
        sin_ref, own_kernel_ref, other_kernel_ref, tokens_out, act_out, lift_out, field_ref, sum_ref,
        left_ref, right_ref, kernel_ref, both_ref, sems, tokens_ref,
        act_ref, lift_ref, out_sems,
    ):
        parity = section_ref[0] % 2

        @pl.when(section_ref[0] < 2)
        def _():
            weights = Weights(index_ref, own_ref, near_ref, far_ref, both_ref, sems, parity)
            weights.start()
            choose(kernel_ref, parity == 1, own_kernel_ref, other_kernel_ref)
            patch = patchify(skip_ref[...])
            sum_ref[...] = jnp.zeros_like(sum_ref)

            def embed(chunk, rows):
                at = lanes(chunk, cols)
                code = one_ref[:, at][:, None] * cos_ref[:, at][None]
                code += two_ref[:, at][:, None] * sin_ref[:, at][None]
                value = dot_nt(patch, rows) + code.reshape(TOKENS, cols)
                value = value.astype(BF16)
                tokens_ref[:, at] = value
                value = value.astype(F32)
                sum_ref[...] += jnp.sum(value * value, axis=-1, keepdims=True)

            weights.sweep(0, embed, wait=True)
            scale = lax.rsqrt(sum_ref[...] * (1.0 / width) + NORM_EPS)
            lift_ref[...] = jnp.zeros_like(lift_ref)

            def raise_up(chunk, rows):
                at = lanes(chunk, cols)
                active = silu(tokens_ref[:, at].astype(F32) * scale).astype(BF16)
                act_ref[:, at] = active
                lift_ref[...] += dot(active, rows)

            weights.sweep(1, raise_up, wait=True)

            pairs = ((tokens_ref, tokens_out), (act_ref, act_out), (lift_ref, lift_out))
            copies = [
                pltpu.make_async_copy(source, target, out_sems.at[n])
                for n, (source, target) in enumerate(pairs)
            ]
            for copy in copies:
                copy.start()
            field = unpatchify(rounded(silu(lift_ref[...])))
            field_ref[...] = conv_in_kernel(field, kernel_ref, left_ref, right_ref).astype(BF16)
            for copy in copies:
                copy.wait()

    return pl.pallas_call(
        body,
        out_shape=[
            jax.ShapeDtypeStruct((TOKENS, width), BF16),
            jax.ShapeDtypeStruct((TOKENS, width), BF16),
            jax.ShapeDtypeStruct((TOKENS, depth), F32),
            jax.ShapeDtypeStruct((SIDE, HALF, 2 * C), BF16),
        ],
        in_specs=[SMEM, SMEM, VMEM] + [HBM] * 3 + [VMEM] * 6,
        out_specs=[HBM] * 3 + [VMEM],
        scratch_shapes=[pltpu.VMEM((TOKENS, 1), F32)]
        + TAPS
        + KERNEL
        + weight_scratch(width, depth)
        + [
            pltpu.VMEM((TOKENS, width), BF16),
            pltpu.VMEM((TOKENS, width), BF16),
            pltpu.VMEM((TOKENS, depth), F32),
            pltpu.SemaphoreType.DMA((3,)),
        ],
        compiler_params=params(58),
        name="forward_first_pair",
    )(section, blocks, skip, own, near, far, *codes, *kernels)


def run_second_pair(section, blocks, second, skip, start, own, near, far, kernels):
    width, depth = own.shape
    cols = width // CHUNKS

    def body(
        section_ref, index_ref, second_ref, skip_ref, start_ref, own_ref, near_ref, far_ref,
        own_kernel_ref, other_kernel_ref, back_ref, side_ref, patch_ref, sum_ref, left_ref,
        right_ref, kernel_ref, tokens_ref, inner_ref, lift_ref, both_ref, sems,
    ):
        parity = section_ref[0] % 2

        @pl.when(section_ref[0] >= 2)
        def _():
            weights = Weights(index_ref, own_ref, near_ref, far_ref, both_ref, sems, parity)
            weights.start()
            choose(kernel_ref, parity == 0, own_kernel_ref, other_kernel_ref)
            field = rounded(silu(second_ref[...].astype(F32)))
            field = conv_in_kernel(field, kernel_ref, left_ref, right_ref).astype(BF16)
            patch_ref[...] = patchify(field)
            sum_ref[...] = jnp.zeros_like(sum_ref)

            def embed(chunk, rows):
                value = dot_nt(patch_ref[...], rows).astype(BF16)
                tokens_ref[:, lanes(chunk, cols)] = value
                value = value.astype(F32)
                sum_ref[...] += jnp.sum(value * value, axis=-1, keepdims=True)

            weights.sweep(0, embed, wait=True)
            scale = lax.rsqrt(sum_ref[...] * (1.0 / width) + NORM_EPS)
            lift_ref[...] = patchify(skip_ref[...]).astype(F32)

            def raise_up(chunk, rows):
                at = lanes(chunk, cols)
                active = silu(tokens_ref[:, at].astype(F32) * scale).astype(BF16)
                side_ref[:, at] = active
                lift_ref[...] += dot(active, rows)

            weights.sweep(1, raise_up, wait=True)
            last_patch = (patchify(start_ref[...]) * silu_slope(lift_ref[...])).astype(BF16)

            @pl.when(parity == 1)
            def _():
                patch_ref[...] = last_patch

            sum_ref[...] = jnp.zeros_like(sum_ref)

            def descend(chunk, rows):
                at = lanes(chunk, cols)
                normal = tokens_ref[:, at].astype(F32) * scale
                inner = dot_nt(last_patch, rows) * silu_slope(normal)
                inner_ref[:, at] = inner
                sum_ref[...] += jnp.sum(inner * normal, axis=-1, keepdims=True)

            weights.sweep(1, descend)
            mean = sum_ref[...] * (1.0 / width)
            lift_ref[...] = jnp.zeros_like(lift_ref)

            def lower(chunk, rows):
                at = lanes(chunk, cols)
                normal = tokens_ref[:, at].astype(F32) * scale
                back = (scale * (inner_ref[:, at] - normal * mean)).astype(BF16)

                @pl.when(parity == 0)
                def _():
                    side_ref[:, at] = back

                lift_ref[...] += dot(back, rows)

            weights.sweep(0, lower)
            field = unpatchify(rounded(lift_ref[...]))
            field = conv_in_kernel(field, kernel_ref, left_ref, right_ref, turned=True)
            back_ref[...] = (field * silu_slope(second_ref[...].astype(F32))).astype(BF16)

    return pl.pallas_call(
        body,
        out_shape=[
            jax.ShapeDtypeStruct((SIDE, HALF, 2 * C), BF16),
            jax.ShapeDtypeStruct((TOKENS, width), BF16),
            jax.ShapeDtypeStruct((TOKENS, depth), BF16),
        ],
        in_specs=[SMEM, SMEM] + [VMEM] * 3 + [HBM] * 3 + [VMEM] * 2,
        out_specs=[VMEM] * 3,
        scratch_shapes=[pltpu.VMEM((TOKENS, 1), F32)]
        + TAPS
        + KERNEL
        + [
            pltpu.VMEM((TOKENS, width), BF16),
            pltpu.VMEM((TOKENS, width), F32),
            pltpu.VMEM((TOKENS, depth), F32),
        ]
        + weight_scratch(width, depth),
        compiler_params=params(58),
        name="second_pair",
    )(section, blocks, second, skip, start, own, near, far, *kernels)


def run_back(section, given, skip, lift, tokens, prior, patch, near, far, kernels):
    width, depth = tokens.shape[1], lift.shape[1]
    cols = width // CHUNKS

    def body(
        section_ref, given_ref, skip_ref, lift_ref, tokens_ref, prior_ref, known_ref, near_ref,
        far_ref, own_kernel_ref, other_kernel_ref, keep_ref, send_ref, patch_ref, sum_ref, left_ref,
        right_ref, kernel_ref, inner_ref, both_ref, sems,
    ):
        where = section_ref[0]
        weights = Weights(None, None, near_ref, far_ref, both_ref, sems, 1)

        @pl.when(where == 0)
        def _():
            weights.start(own=False)

        @pl.when(where >= 1)
        def _():
            keep_ref[...] = prior_ref[:, : width // 2]
            send_ref[...] = prior_ref[:, width // 2 :]

        @pl.when(where >= 2)
        def _():
            patch_ref[...] = known_ref[...]

        @pl.when(where < 2)
        def _():
            choose(kernel_ref, where == 1, own_kernel_ref, other_kernel_ref)
            field = given_ref[...].astype(F32)
            field = conv_in_kernel(field, kernel_ref, left_ref, right_ref, turned=True)
            patch_ref[...] = (patchify(field) * silu_slope(lift_ref[...])).astype(BF16)

        @pl.when(where == 0)
        def _():
            sum_ref[...] = jnp.zeros_like(sum_ref)

            @pl.loop(0, CHUNKS, unroll=UNROLL)
            def _(chunk):
                value = tokens_ref[:, lanes(chunk, cols)].astype(F32)
                sum_ref[...] += jnp.sum(value * value, axis=-1, keepdims=True)

            scale = lax.rsqrt(sum_ref[...] * (1.0 / width) + NORM_EPS)
            sum_ref[...] = jnp.zeros_like(sum_ref)

            def descend(chunk, rows):
                at = lanes(chunk, cols)
                normal = tokens_ref[:, at].astype(F32) * scale
                inner = dot_nt(patch_ref[...], rows) * silu_slope(normal)
                inner_ref[:, at] = inner
                sum_ref[...] += jnp.sum(inner * normal, axis=-1, keepdims=True)

            weights.sweep(0, descend, wait=True)
            mean = sum_ref[...] * (1.0 / width)

            for first, ref in ((0, keep_ref), (CHUNKS // 2, send_ref)):

                @pl.loop(0, CHUNKS // 2, unroll=UNROLL)
                def _(i, first=first, ref=ref):
                    at = lanes(first + i, cols)
                    normal = tokens_ref[:, at].astype(F32) * scale
                    back = scale * (inner_ref[:, at] - normal * mean)
                    ref[:, lanes(i, cols)] = back.astype(BF16)

            patch_ref[...] = patchify(skip_ref[...])

    return pl.pallas_call(
        body,
        out_shape=[
            jax.ShapeDtypeStruct((TOKENS, width // 2), BF16),
            jax.ShapeDtypeStruct((TOKENS, width // 2), BF16),
            jax.ShapeDtypeStruct((TOKENS, depth), BF16),
        ],
        in_specs=[SMEM] + [VMEM] * 6 + [HBM] * 2 + [VMEM] * 2,
        out_specs=[VMEM] * 3,
        scratch_shapes=[pltpu.VMEM((TOKENS, 1), F32)]
        + TAPS
        + KERNEL
        + [
            pltpu.VMEM((TOKENS, width), F32),
            pltpu.VMEM((1, width, depth), BF16),
            pltpu.SemaphoreType.DMA((1, CHUNKS)),
        ],
        compiler_params=params(48),
        name="back_first_pair",
    )(section, given, skip, lift, tokens, prior, patch, near, far, *kernels)


SENT = {"a": (1, 2), "b": (3, 2)}
KEPT = {"a": (0, 3), "b": (0, 1)}


def run_partial(keep, recv, patch, patch_recv):
    half, depth = keep.shape[1], patch.shape[1]
    part, block = depth // 4, half // 16

    def body(keep_ref, recv_ref, patch_ref, other_ref, *out_refs):
        tokens = jnp.concatenate([keep_ref[...], recv_ref[...]], axis=0)
        patches = jnp.concatenate([patch_ref[...], other_ref[...]], axis=0)
        for column in range(4):
            name = "ab"[column % 2]
            sent_ref, kept_ref = out_refs[column], out_refs[4 + column]
            right = patches[:, column * part : (column + 1) * part]
            for i in range(2):
                for ref, far in ((sent_ref, SENT[name][i]), (kept_ref, KEPT[name][i])):
                    if column < 2:
                        left = tokens[:, far * 4 * block : (far + 1) * 4 * block]
                    else:
                        left = jnp.concatenate(
                            [tokens[:, (4 * j + far) * block :][:, :block] for j in range(4)], axis=1
                        )
                    ref[i] = dot_tn(left, right).astype(ref.dtype)

    shape = (2, 4 * block, part)
    outs = call(body, [(shape, BF16)] * 4 + [(shape, F32)] * 4, (keep, recv, patch, patch_recv))
    return outs[:4], outs[4:]


FIRST_RINGS = ((X1, X3), (X3, X1), (Y1, Y3), (Y3, Y1))


def run_sum(partial):
    sent, kept = partial
    got = [flip(value, ring[0]) for value, ring in zip(sent, FIRST_RINGS)]
    rows, part = kept[0].shape[1:]
    block = rows // 4

    def add_once(*refs):
        kept_refs, got_refs, sent_refs, out_refs = refs[:4], refs[4:8], refs[8:12], refs[12:]
        for kept_ref, got_ref, sent_ref, out_ref in zip(kept_refs, got_refs, sent_refs, out_refs):
            total = kept_ref[...] + got_ref[...].astype(F32)
            out_ref[...] = total[0]
            sent_ref[...] = total[1].astype(BF16)

    shape = (rows, part)
    outs = call(add_once, [(shape, BF16)] * 4 + [(shape, F32)] * 4, (*kept, *got))
    got = [flip(value, ring[1]) for value, ring in zip(outs[:4], FIRST_RINGS)]

    def add_twice(*refs):
        kept_refs, got_refs, out_refs = refs[:4], refs[4:8], refs[8:]
        for half in range(2):
            a, b = 2 * half, 2 * half + 1
            total = [kept_refs[i][...] + got_refs[i][...].astype(F32) for i in (a, b)]
            total = jnp.concatenate(total, axis=1)
            for far in range(4):
                ref = out_refs[4 * half + far]
                ref[...] = total[far * block : (far + 1) * block].astype(ref.dtype)

    shape = (block, 2 * part)
    kinds = [F32, BF16, BF16, BF16] * 2
    outs = call(add_twice, [(shape, kind) for kind in kinds], (*outs[4:], *got))
    got = [flip(v, m) for v, m in zip(outs[1:4], (Y1, Y1 ^ Y3, Y3))]
    got += [flip(v, m) for v, m in zip(outs[5:8], (X1, X1 ^ X3, X3))]

    def add_last(*refs):
        for half in range(2):
            total = refs[half][...]
            for ref in refs[2 + 3 * half : 5 + 3 * half]:
                total += ref[...].astype(F32)
            at = slice(half * 2 * part, (half + 1) * 2 * part)
            refs[8][:, at] = total[: block // 2]
            refs[9][:, at] = total[block // 2 :].astype(BF16)

    shape = (block // 2, 4 * part)
    mine, away = call(add_last, [(shape, F32), (shape, BF16)], (outs[0], outs[4], *got))
    return mine + flip(away, ZH).astype(F32)


def on_device(features, conv_kernels, patch_weights, positions, out_cotangent):
    weight = patch_weights[0]
    width, depth = weight.shape
    kernel = conv_kernels[0].reshape(9 * C, C)
    section = lax.axis_index("section")
    place = lax.axis_index(SEQ)
    first_pair = section < 2

    order = jnp.arange(N_SEQ, dtype=jnp.int32)
    away = ((order & 1) << 5) | (((order >> 3) & 3) << 3) | (((order >> 1) & 3) << 1) | (order >> 5)
    blocks = away ^ place

    here, phase = section.reshape(1), (place % 4).reshape(1)
    piece = run_piece(blocks, weight)
    *rows, late, beside = run_rows(phase, features, out_cotangent, piece)
    piece = partner(piece)
    late, beside = beside_swap(late), flip(beside, CORE)

    image_id = jnp.minimum(3 * (place // 4) + place % 4, positions.shape[0] - 1)
    begin = positions[image_id]
    half = width // 2
    feature = (blocks[:, None] * (width // N_SEQ) + jnp.arange(width // N_SEQ)[None, :]).reshape(-1)
    rates = jnp.exp((feature % half).astype(F32) * (-math.log(10000.0) / half))
    is_sin = (feature < half)[None, :]
    steps = jnp.arange(HALF, dtype=jnp.int32)
    row_angle = (begin + HALF * steps).astype(F32)[:, None] * rates[None, :]
    col_angle = steps.astype(F32)[:, None] * rates[None, :]
    row_sin, row_cos = jnp.sin(row_angle), jnp.cos(row_angle)
    row_one = jnp.where(is_sin, row_sin, row_cos)
    row_two = jnp.where(is_sin, row_cos, -row_sin)
    col_cos, col_sin = jnp.cos(col_angle), jnp.sin(col_angle)

    codes = (row_one, row_two, col_cos, col_sin)

    near, kernels, skip_field, skip_recv, cotangent = gather_partner(
        piece, kernel, lambda: run_image(phase, rows, late, beside), codes
    )
    far = flip(near, CORE)
    start = run_start(here, cotangent, kernels, turned=True)

    tokens, active, first_lift, second_field = run_forward(
        here, blocks, skip_field, weight, near, far, codes, kernels
    )
    second_back, side, patch = run_second_pair(
        here, blocks, hop(second_field), skip_recv, start, weight, near, far, kernels
    )
    prior = jnp.where(first_pair, active, side)
    keep, send, patch = run_back(
        here, hop(second_back), skip_field, first_lift, tokens, prior, patch, near, far,
        kernels,
    )

    summed = run_sum(run_partial(keep, flip(send, CORE), patch, flip(patch, CORE)))
    tokens_in_all = positions.shape[0] * HALF * HALF
    return (summed * (1.0 / math.sqrt(tokens_in_all)))[None]


def solution(mesh):
    in_specs = (
        P("seq", None, None),
        P("section", None, None, None, None),
        P("section", None, None),
        P(),
        P("seq", None, None),
    )
    out_specs = P("section", "seq", None)
    return jax.shard_map(
        on_device, mesh=mesh, in_specs=in_specs, out_specs=out_specs, check_vma=False
    )
```

```python
import math

import jax
import jax.numpy as jnp
from jax import lax
from jax.experimental import pallas as pl
from jax.experimental.pallas import tpu as pltpu
from jax.sharding import PartitionSpec as P

NORM_EPS = 1e-05
BF16 = jnp.bfloat16
F32 = jnp.float32
SIDE = 32
HALF = SIDE // 2
C = 256
N_SEQ = 64
SEQ = "seq"

X1, X3, Y1, Y3, CORE, ZH = (1 << 3, 3 << 3, 1 << 1, 3 << 1, 1, 1 << 5)


def flip(value, mask):
    return lax.ppermute(value, SEQ, [(i, i ^ mask) for i in range(N_SEQ)])


def partner(value):
    return lax.ppermute(value, "section", [(0, 1), (1, 0), (2, 3), (3, 2)])


HOPS = [(1 * N_SEQ + q, 2 * N_SEQ + q) for q in range(N_SEQ)]
HOPS += [(q, 3 * N_SEQ + (q ^ ZH)) for q in range(N_SEQ)]
HOPS += [(j, i) for i, j in HOPS]


def hop(value):
    return lax.ppermute(value, ("section", SEQ), HOPS)


def beside_swap(value):
    pairs = [((2 * k - 1) % N_SEQ, 2 * k) for k in range(N_SEQ // 2)]
    return lax.ppermute(value, SEQ, pairs + [(j, i) for i, j in pairs])


def dot(left, right):
    return jnp.dot(left, right, preferred_element_type=F32)


def dot_nt(left, right):
    return lax.dot_general(left, right, (((1,), (1,)), ((), ())), preferred_element_type=F32)


def dot_tn(left, right):
    return lax.dot_general(left, right, (((0,), (0,)), ((), ())), preferred_element_type=F32)


def patchify(field):
    pairs = field.reshape(HALF, 2, HALF, 2 * C)
    return jnp.concatenate([pairs[:, 0], pairs[:, 1]], axis=-1).reshape(HALF * HALF, 4 * C)


def unpatchify(tokens):
    pairs = tokens.reshape(HALF, HALF, 4 * C)
    return jnp.stack([pairs[..., : 2 * C], pairs[..., 2 * C :]], axis=1).reshape(SIDE, HALF, 2 * C)


def silu(value):
    half = 0.5 * value
    return half + half * jnp.tanh(half)


def silu_slope(value):
    half = 0.5 * value
    t = jnp.tanh(half)
    return (0.5 + 0.5 * t) * (1.0 + half * (1.0 - t))


CHUNKS = 4
UNROLL = 4
VMEM = pl.BlockSpec(memory_space=pltpu.VMEM)
SMEM = pl.BlockSpec(memory_space=pltpu.SMEM)
ANY = pl.BlockSpec(memory_space=pl.ANY)
HBM = pl.BlockSpec(memory_space=pltpu.HBM)


def conv_in_kernel(field, kernel_ref, left_ref, right_ref, turned=False):
    even, odd = field[..., :C], field[..., C:]
    column = lax.broadcasted_iota(jnp.int32, (SIDE, HALF, C), 1)
    before = jnp.where(column == 0, 0.0, pltpu.roll(odd, 1, 1))
    after = jnp.where(column == HALF - 1, 0.0, pltpu.roll(even, HALF - 1, 1))
    middle = field.astype(BF16)
    left_ref[1 : SIDE + 1, :, C:] = middle
    left_ref[1 : SIDE + 1, :, :C] = before.astype(BF16)
    right_ref[1 : SIDE + 1, :, : 2 * C] = middle
    right_ref[1 : SIDE + 1, :, 2 * C :] = after.astype(BF16)
    out = []
    for ref in (left_ref, right_ref):
        edge = jnp.zeros((HALF, 3 * C), BF16)
        ref[0] = edge
        ref[SIDE + 1] = edge
        total = None
        for row in range(3):
            taps = ref[row : row + SIDE].reshape(SIDE * HALF, 3 * C)
            if turned:
                for column in range(3):
                    tap = (2 - row) * 3 + 2 - column
                    weight = kernel_ref[tap * C : (tap + 1) * C]
                    term = dot_nt(taps[:, column * C : (column + 1) * C], weight)
                    total = term if total is None else total + term
            else:
                term = dot(taps, kernel_ref[row * 3 * C : (row + 1) * 3 * C])
                total = term if total is None else total + term
        out.append(total.reshape(SIDE, HALF, C))
    return jnp.concatenate(out, axis=-1)


def choose(to_ref, mine, own_ref, other_ref):
    @pl.when(mine)
    def _():
        to_ref[...] = own_ref[...]

    @pl.when(jnp.logical_not(mine))
    def _():
        to_ref[...] = other_ref[...]


def rounded(value):
    return value.astype(BF16).astype(F32)


class Weights:
    def __init__(self, index_ref, own_ref, near_ref, far_ref, both_ref, sems, parity):
        self.args = (index_ref, own_ref, near_ref, far_ref, both_ref, sems, parity)
        self.rows = both_ref.shape[1] // CHUNKS
        self.share = both_ref.shape[1] // N_SEQ

    def start(self, own=True):
        index_ref, own_ref, near_ref, far_ref, both_ref, sems, parity = self.args
        per = N_SEQ // CHUNKS
        for block in range(N_SEQ if own else 0):
            source = pl.multiple_of(index_ref[block] * self.share, self.share)
            pltpu.make_async_copy(
                own_ref.at[pl.ds(source, self.share)],
                both_ref.at[parity, pl.ds(block * self.share, self.share)],
                sems.at[parity, block // per],
            ).start()
        for chunk in range(CHUNKS):
            source = near_ref if chunk < CHUNKS // 2 else far_ref
            pltpu.make_async_copy(
                source.at[pl.ds(chunk % (CHUNKS // 2) * self.rows, self.rows)],
                both_ref.at[1 - parity, pl.ds(chunk * self.rows, self.rows)],
                sems.at[1 - parity, chunk],
            ).start()

    def sweep(self, slot, step, wait=False):
        _, _, near_ref, _, both_ref, sems, _ = self.args

        @pl.loop(0, CHUNKS, unroll=UNROLL)
        def _(chunk):
            rows = pl.ds(pl.multiple_of(chunk * self.rows, self.rows), self.rows)
            if wait:
                pltpu.make_async_copy(
                    near_ref.at[pl.ds(0, self.rows)], both_ref.at[slot, rows], sems.at[slot, chunk]
                ).wait()
            step(chunk, both_ref[slot, rows])


def weight_scratch(width, depth):
    return [pltpu.VMEM((2, width, depth), BF16), pltpu.SemaphoreType.DMA((2, CHUNKS))]


def lanes(chunk, count):
    return pl.ds(pl.multiple_of(chunk * count, count), count)


TAPS = [pltpu.VMEM((SIDE + 2, HALF, 3 * C), BF16)] * 2
TOKENS = HALF * HALF
KERNEL = [pltpu.VMEM((9 * C, C), BF16)]


def params(mib):
    return pltpu.CompilerParams(vmem_limit_bytes=mib * 1024 * 1024)


def call(body, outs, args, after=()):
    count = len(args)

    def with_after(*refs):
        body(*refs[:count], *refs[count + len(after) :])

    return pl.pallas_call(
        with_after,
        out_shape=[jax.ShapeDtypeStruct(shape, kind) for shape, kind in outs],
        in_specs=[VMEM] * count + [ANY] * len(after),
        out_specs=[VMEM] * len(outs),
        compiler_params=params(20),
    )(*args, *after)


def run_rows(phase, features, cotangent, after):
    count = features.shape[0]
    wide = 2 * C

    def body(phase_ref, features_ref, cotangent_ref, _, *refs):
        late_ref, beside_ref, value_ref = refs[2:]
        for side, ref in enumerate((features_ref, cotangent_ref)):
            for part in range(2):
                value_ref[part] = ref[:, :, part * 128 : (part + 1) * 128].astype(F32)
            quarters = [
                value_ref[part, :, pl.ds(column, HALF, stride=2), :]
                for column in range(2)
                for part in range(2)
            ]
            rows = jnp.concatenate(quarters, axis=-1).astype(BF16)
            refs[side][...] = rows
            at = slice(side * wide, (side + 1) * wide)
            late_ref[:, :, at] = rows[8:]

            @pl.when(phase_ref[0] == 0)
            def _(rows=rows, at=at):
                beside_ref[:, :, at] = rows[16:]

            @pl.when(phase_ref[0] != 0)
            def _(rows=rows, at=at):
                beside_ref[:, :, at] = rows[:8]

    shapes = [(count, HALF, wide)] * 2 + [(16, HALF, 2 * wide), (8, HALF, 2 * wide)]
    return pl.pallas_call(
        body,
        out_shape=[jax.ShapeDtypeStruct(shape, BF16) for shape in shapes],
        in_specs=[SMEM, VMEM, VMEM, ANY],
        out_specs=[VMEM] * 4,
        scratch_shapes=[pltpu.VMEM((2, count, SIDE, 128), F32)],
        compiler_params=params(12),
        name="rows",
    )(phase, features, cotangent, after)


def run_image(phase, rows, late, beside):
    def body(phase_ref, *refs):
        late_ref, beside_ref = refs[2:4]
        kind = phase_ref[0]
        for side in range(2):
            rows_ref, out_ref = refs[side], refs[4 + side]
            at = slice(side * 2 * C, (side + 1) * 2 * C)

            @pl.when(kind == 0)
            def _(rows_ref=rows_ref, out_ref=out_ref, at=at):
                out_ref[:16] = late_ref[:, :, at]
                out_ref[16:] = rows_ref[:16]

            @pl.when(kind == 1)
            def _(rows_ref=rows_ref, out_ref=out_ref, at=at):
                out_ref[:8] = beside_ref[:, :, at]
                out_ref[8:] = rows_ref[...]

            @pl.when(kind == 2)
            def _(rows_ref=rows_ref, out_ref=out_ref, at=at):
                out_ref[:24] = rows_ref[...]
                out_ref[24:] = beside_ref[:, :, at]

            @pl.when(kind == 3)
            def _(out_ref=out_ref):
                out_ref[...] = jnp.zeros_like(out_ref)

    return pl.pallas_call(
        body,
        out_shape=[jax.ShapeDtypeStruct((SIDE, HALF, 2 * C), BF16)] * 2,
        in_specs=[SMEM] + [VMEM] * 4,
        out_specs=[VMEM] * 2,
        compiler_params=params(12),
        name="image",
    )(phase, *rows, late, beside)


def run_start(section, image, kernels, turned):
    def body(section_ref, image_ref, own_ref, other_ref, out_ref, left_ref, right_ref, kernel_ref):
        where = section_ref[0]

        @pl.when((where >= 2) if turned else (where < 2))
        def _():
            choose(kernel_ref, where == (3 if turned else 0), own_ref, other_ref)
            field = image_ref[...].astype(F32)
            field = conv_in_kernel(field, kernel_ref, left_ref, right_ref, turned=turned)
            out_ref[...] = field.astype(out_ref.dtype)

    return pl.pallas_call(
        body,
        out_shape=jax.ShapeDtypeStruct((SIDE, HALF, 2 * C), F32 if turned else BF16),
        in_specs=[SMEM] + [VMEM] * 3,
        out_specs=VMEM,
        scratch_shapes=TAPS + KERNEL,
        compiler_params=params(16),
        name="start_turned" if turned else "start",
    )(section, image, *kernels)


def run_piece(blocks, weight):
    share, depth = weight.shape[0] // N_SEQ, weight.shape[1]

    def body(index_ref, weight_ref, out_ref):
        out_ref[...] = weight_ref[...]

    return pl.pallas_call(
        body,
        grid_spec=pltpu.PrefetchScalarGridSpec(
            num_scalar_prefetch=1,
            grid=(2,),
            in_specs=[pl.BlockSpec((share, depth), lambda i, index: (index[i], 0))],
            out_specs=pl.BlockSpec((share, depth), lambda i, index: (i, 0)),
        ),
        out_shape=jax.ShapeDtypeStruct((2 * share, depth), weight.dtype),
        compiler_params=params(58),
    )(blocks, weight)


def gather_partner(piece, kernel, images, before):
    rows, depth = piece.shape
    half, part = depth // 2, depth // 4

    def split(piece_ref, kernel_ref, first_ref, second_ref, again_ref):
        first_ref[...] = piece_ref[:, :half]
        second_ref[...] = piece_ref[:, half:]
        again_ref[...] = kernel_ref[...]

    outs = [((rows, half), BF16)] * 2 + [(kernel.shape, BF16)]
    first, second, again = call(split, outs, (piece, kernel), before)
    got = [flip(first, m) for m in (X1, X1 ^ X3, X3)] + [flip(second, m) for m in (Y1, Y1 ^ Y3, Y3)]
    kernels = (kernel, partner(again))
    image, cotangent = images()
    cotangent = hop(cotangent)

    def stack(*refs):
        for side in range(2):
            for far in range(4):
                source = refs[side] if far == 0 else refs[2 + 3 * side + far - 1]
                refs[8 + side][far * rows : (far + 1) * rows] = source[...]

    wide = call(stack, [((4 * rows, half), BF16)] * 2, (first, second, *got), (image,))
    rings = ((Y1, Y3), (X1, X3))
    near = [flip(value, ring[0]) for value, ring in zip(wide, rings)]
    far = [flip(value, ring[1]) for value, ring in zip(wide, rings)]
    section = lax.axis_index("section").reshape(1)
    skip_field = run_start(section, image, kernels, turned=False)
    skip_recv = hop(skip_field)

    def cut(*refs):
        for side in range(2):
            refs[4 + 2 * side][...] = refs[side][:, :part]
            refs[5 + 2 * side][...] = refs[2 + side][:, part:]

    outs = [((4 * rows, part), BF16)] * 4
    parts = call(cut, outs, (*far, *near), (skip_field, cotangent))
    low = [flip(parts[2 * side], ring[0]) for side, ring in enumerate(rings)]
    high = [flip(parts[2 * side + 1], ring[1]) for side, ring in enumerate(rings)]

    def join(*refs):
        out_ref = refs[10]
        for side in range(2):
            base = side * half
            mine, one, three = refs[side], refs[2 + side], refs[4 + side]
            for outer in range(4):
                sources = {0: [mine], 1: [one], 3: [three], 2: [refs[6 + side], refs[8 + side]]}[outer]
                for j, source in enumerate(sources):
                    count = source.shape[1]
                    at = slice(base + j * count, base + (j + 1) * count)
                    for inner in range(4):
                        block = source[inner * rows : (inner + 1) * rows]
                        x, y = (inner, outer) if side == 0 else (outer, inner)
                        start = (4 * x + y) * rows
                        out_ref[start : start + rows, at] = block

    args = (*wide, *near, *far, *low, *high)
    held = call(join, [((16 * rows, depth), BF16)], args, (skip_recv,))[0]
    return held, kernels, skip_field, skip_recv, cotangent


def run_forward(section, blocks, skip, own, near, far, codes, kernels):
    width, depth = own.shape
    cols = width // CHUNKS

    def body(
        section_ref, index_ref, skip_ref, own_ref, near_ref, far_ref, one_ref, two_ref, cos_ref,
        sin_ref, own_kernel_ref, other_kernel_ref, tokens_out, act_out, lift_out, field_ref, sum_ref,
        left_ref, right_ref, kernel_ref, both_ref, sems, tokens_ref,
        act_ref, lift_ref, out_sems,
    ):
        parity = section_ref[0] % 2

        @pl.when(section_ref[0] < 2)
        def _():
            weights = Weights(index_ref, own_ref, near_ref, far_ref, both_ref, sems, parity)
            weights.start()
            choose(kernel_ref, parity == 1, own_kernel_ref, other_kernel_ref)
            patch = patchify(skip_ref[...])
            sum_ref[...] = jnp.zeros_like(sum_ref)

            def embed(chunk, rows):
                at = lanes(chunk, cols)
                code = one_ref[:, at][:, None] * cos_ref[:, at][None]
                code += two_ref[:, at][:, None] * sin_ref[:, at][None]
                value = dot_nt(patch, rows) + code.reshape(TOKENS, cols)
                value = value.astype(BF16)
                tokens_ref[:, at] = value
                value = value.astype(F32)
                sum_ref[...] += jnp.sum(value * value, axis=-1, keepdims=True)

            weights.sweep(0, embed, wait=True)
            scale = lax.rsqrt(sum_ref[...] * (1.0 / width) + NORM_EPS)
            lift_ref[...] = jnp.zeros_like(lift_ref)

            def raise_up(chunk, rows):
                at = lanes(chunk, cols)
                active = silu(tokens_ref[:, at].astype(F32) * scale).astype(BF16)
                act_ref[:, at] = active
                lift_ref[...] += dot(active, rows)

            weights.sweep(1, raise_up, wait=True)

            pairs = ((tokens_ref, tokens_out), (act_ref, act_out), (lift_ref, lift_out))
            copies = [
                pltpu.make_async_copy(source, target, out_sems.at[n])
                for n, (source, target) in enumerate(pairs)
            ]
            for copy in copies:
                copy.start()
            field = unpatchify(rounded(silu(lift_ref[...])))
            field_ref[...] = conv_in_kernel(field, kernel_ref, left_ref, right_ref).astype(BF16)
            for copy in copies:
                copy.wait()

    return pl.pallas_call(
        body,
        out_shape=[
            jax.ShapeDtypeStruct((TOKENS, width), BF16),
            jax.ShapeDtypeStruct((TOKENS, width), BF16),
            jax.ShapeDtypeStruct((TOKENS, depth), F32),
            jax.ShapeDtypeStruct((SIDE, HALF, 2 * C), BF16),
        ],
        in_specs=[SMEM, SMEM, VMEM] + [HBM] * 3 + [VMEM] * 6,
        out_specs=[HBM] * 3 + [VMEM],
        scratch_shapes=[pltpu.VMEM((TOKENS, 1), F32)]
        + TAPS
        + KERNEL
        + weight_scratch(width, depth)
        + [
            pltpu.VMEM((TOKENS, width), BF16),
            pltpu.VMEM((TOKENS, width), BF16),
            pltpu.VMEM((TOKENS, depth), F32),
            pltpu.SemaphoreType.DMA((3,)),
        ],
        compiler_params=params(34),
        name="forward_first_pair",
    )(section, blocks, skip, own, near, far, *codes, *kernels)


def run_second_pair(section, blocks, second, skip, start, own, near, far, kernels):
    width, depth = own.shape
    cols = width // CHUNKS

    def body(
        section_ref, index_ref, second_ref, skip_ref, start_ref, own_ref, near_ref, far_ref,
        own_kernel_ref, other_kernel_ref, back_ref, side_ref, patch_ref, sum_ref, left_ref,
        right_ref, kernel_ref, tokens_ref, inner_ref, lift_ref, both_ref, sems,
    ):
        parity = section_ref[0] % 2

        @pl.when(section_ref[0] >= 2)
        def _():
            weights = Weights(index_ref, own_ref, near_ref, far_ref, both_ref, sems, parity)
            weights.start()
            choose(kernel_ref, parity == 0, own_kernel_ref, other_kernel_ref)
            field = rounded(silu(second_ref[...].astype(F32)))
            field = conv_in_kernel(field, kernel_ref, left_ref, right_ref).astype(BF16)
            patch_ref[...] = patchify(field)
            sum_ref[...] = jnp.zeros_like(sum_ref)

            def embed(chunk, rows):
                value = dot_nt(patch_ref[...], rows).astype(BF16)
                tokens_ref[:, lanes(chunk, cols)] = value
                value = value.astype(F32)
                sum_ref[...] += jnp.sum(value * value, axis=-1, keepdims=True)

            weights.sweep(0, embed, wait=True)
            scale = lax.rsqrt(sum_ref[...] * (1.0 / width) + NORM_EPS)
            lift_ref[...] = patchify(skip_ref[...]).astype(F32)

            def raise_up(chunk, rows):
                at = lanes(chunk, cols)
                active = silu(tokens_ref[:, at].astype(F32) * scale).astype(BF16)
                side_ref[:, at] = active
                lift_ref[...] += dot(active, rows)

            weights.sweep(1, raise_up, wait=True)
            last_patch = (patchify(start_ref[...]) * silu_slope(lift_ref[...])).astype(BF16)

            @pl.when(parity == 1)
            def _():
                patch_ref[...] = last_patch

            sum_ref[...] = jnp.zeros_like(sum_ref)

            def descend(chunk, rows):
                at = lanes(chunk, cols)
                normal = tokens_ref[:, at].astype(F32) * scale
                inner = dot_nt(last_patch, rows) * silu_slope(normal)
                inner_ref[:, at] = inner
                sum_ref[...] += jnp.sum(inner * normal, axis=-1, keepdims=True)

            weights.sweep(1, descend)
            mean = sum_ref[...] * (1.0 / width)
            lift_ref[...] = jnp.zeros_like(lift_ref)

            def lower(chunk, rows):
                at = lanes(chunk, cols)
                normal = tokens_ref[:, at].astype(F32) * scale
                back = (scale * (inner_ref[:, at] - normal * mean)).astype(BF16)

                @pl.when(parity == 0)
                def _():
                    side_ref[:, at] = back

                lift_ref[...] += dot(back, rows)

            weights.sweep(0, lower)
            field = unpatchify(rounded(lift_ref[...]))
            field = conv_in_kernel(field, kernel_ref, left_ref, right_ref, turned=True)
            back_ref[...] = (field * silu_slope(second_ref[...].astype(F32))).astype(BF16)

    return pl.pallas_call(
        body,
        out_shape=[
            jax.ShapeDtypeStruct((SIDE, HALF, 2 * C), BF16),
            jax.ShapeDtypeStruct((TOKENS, width), BF16),
            jax.ShapeDtypeStruct((TOKENS, depth), BF16),
        ],
        in_specs=[SMEM, SMEM] + [VMEM] * 3 + [HBM] * 3 + [VMEM] * 2,
        out_specs=[VMEM] * 3,
        scratch_shapes=[pltpu.VMEM((TOKENS, 1), F32)]
        + TAPS
        + KERNEL
        + [
            pltpu.VMEM((TOKENS, width), BF16),
            pltpu.VMEM((TOKENS, width), F32),
            pltpu.VMEM((TOKENS, depth), F32),
        ]
        + weight_scratch(width, depth),
        compiler_params=params(38),
        name="second_pair",
    )(section, blocks, second, skip, start, own, near, far, *kernels)


def run_back(section, given, skip, lift, tokens, prior, patch, near, far, kernels):
    width, depth = tokens.shape[1], lift.shape[1]
    cols = width // CHUNKS

    def body(
        section_ref, given_ref, skip_ref, lift_ref, tokens_ref, prior_ref, known_ref, near_ref,
        far_ref, own_kernel_ref, other_kernel_ref, keep_ref, send_ref, patch_ref, sum_ref, left_ref,
        right_ref, kernel_ref, inner_ref, both_ref, sems,
    ):
        where = section_ref[0]
        weights = Weights(None, None, near_ref, far_ref, both_ref, sems, 1)

        @pl.when(where == 0)
        def _():
            weights.start(own=False)

        @pl.when(where >= 1)
        def _():
            keep_ref[...] = prior_ref[:, : width // 2]
            send_ref[...] = prior_ref[:, width // 2 :]

        @pl.when(where >= 2)
        def _():
            patch_ref[...] = known_ref[...]

        @pl.when(where < 2)
        def _():
            choose(kernel_ref, where == 1, own_kernel_ref, other_kernel_ref)
            field = given_ref[...].astype(F32)
            field = conv_in_kernel(field, kernel_ref, left_ref, right_ref, turned=True)
            patch_ref[...] = (patchify(field) * silu_slope(lift_ref[...])).astype(BF16)

        @pl.when(where == 0)
        def _():
            sum_ref[...] = jnp.zeros_like(sum_ref)

            @pl.loop(0, CHUNKS, unroll=UNROLL)
            def _(chunk):
                value = tokens_ref[:, lanes(chunk, cols)].astype(F32)
                sum_ref[...] += jnp.sum(value * value, axis=-1, keepdims=True)

            scale = lax.rsqrt(sum_ref[...] * (1.0 / width) + NORM_EPS)
            sum_ref[...] = jnp.zeros_like(sum_ref)

            def descend(chunk, rows):
                at = lanes(chunk, cols)
                normal = tokens_ref[:, at].astype(F32) * scale
                inner = dot_nt(patch_ref[...], rows) * silu_slope(normal)
                inner_ref[:, at] = inner
                sum_ref[...] += jnp.sum(inner * normal, axis=-1, keepdims=True)

            weights.sweep(0, descend, wait=True)
            mean = sum_ref[...] * (1.0 / width)

            for first, ref in ((0, keep_ref), (CHUNKS // 2, send_ref)):

                @pl.loop(0, CHUNKS // 2, unroll=UNROLL)
                def _(i, first=first, ref=ref):
                    at = lanes(first + i, cols)
                    normal = tokens_ref[:, at].astype(F32) * scale
                    back = scale * (inner_ref[:, at] - normal * mean)
                    ref[:, lanes(i, cols)] = back.astype(BF16)

            patch_ref[...] = patchify(skip_ref[...])

    return pl.pallas_call(
        body,
        out_shape=[
            jax.ShapeDtypeStruct((TOKENS, width // 2), BF16),
            jax.ShapeDtypeStruct((TOKENS, width // 2), BF16),
            jax.ShapeDtypeStruct((TOKENS, depth), BF16),
        ],
        in_specs=[SMEM] + [VMEM] * 6 + [HBM] * 2 + [VMEM] * 2,
        out_specs=[VMEM] * 3,
        scratch_shapes=[pltpu.VMEM((TOKENS, 1), F32)]
        + TAPS
        + KERNEL
        + [
            pltpu.VMEM((TOKENS, width), F32),
            pltpu.VMEM((1, width, depth), BF16),
            pltpu.SemaphoreType.DMA((1, CHUNKS)),
        ],
        compiler_params=params(30),
        name="back_first_pair",
    )(section, given, skip, lift, tokens, prior, patch, near, far, *kernels)


SENT = {"a": (1, 2), "b": (3, 2)}
KEPT = {"a": (0, 3), "b": (0, 1)}


def run_partial(keep, recv, patch, patch_recv):
    half, depth = keep.shape[1], patch.shape[1]
    part, block = depth // 4, half // 16

    def body(keep_ref, recv_ref, patch_ref, other_ref, *out_refs):
        tokens = jnp.concatenate([keep_ref[...], recv_ref[...]], axis=0)
        patches = jnp.concatenate([patch_ref[...], other_ref[...]], axis=0)
        for column in range(4):
            name = "ab"[column % 2]
            sent_ref, kept_ref = out_refs[column], out_refs[4 + column]
            right = patches[:, column * part : (column + 1) * part]
            for i in range(2):
                for ref, far in ((sent_ref, SENT[name][i]), (kept_ref, KEPT[name][i])):
                    if column < 2:
                        left = tokens[:, far * 4 * block : (far + 1) * 4 * block]
                    else:
                        left = jnp.concatenate(
                            [tokens[:, (4 * j + far) * block :][:, :block] for j in range(4)], axis=1
                        )
                    ref[i] = dot_tn(left, right).astype(ref.dtype)

    shape = (2, 4 * block, part)
    outs = call(body, [(shape, BF16)] * 4 + [(shape, F32)] * 4, (keep, recv, patch, patch_recv))
    return outs[:4], outs[4:]


FIRST_RINGS = ((X1, X3), (X3, X1), (Y1, Y3), (Y3, Y1))


def run_sum(partial):
    sent, kept = partial
    got = [flip(value, ring[0]) for value, ring in zip(sent, FIRST_RINGS)]
    rows, part = kept[0].shape[1:]
    block = rows // 4

    def add_once(*refs):
        kept_refs, got_refs, sent_refs, out_refs = refs[:4], refs[4:8], refs[8:12], refs[12:]
        for kept_ref, got_ref, sent_ref, out_ref in zip(kept_refs, got_refs, sent_refs, out_refs):
            total = kept_ref[...] + got_ref[...].astype(F32)
            out_ref[...] = total[0]
            sent_ref[...] = total[1].astype(BF16)

    shape = (rows, part)
    outs = call(add_once, [(shape, BF16)] * 4 + [(shape, F32)] * 4, (*kept, *got))
    got = [flip(value, ring[1]) for value, ring in zip(outs[:4], FIRST_RINGS)]

    def add_twice(*refs):
        kept_refs, got_refs, out_refs = refs[:4], refs[4:8], refs[8:]
        for half in range(2):
            a, b = 2 * half, 2 * half + 1
            total = [kept_refs[i][...] + got_refs[i][...].astype(F32) for i in (a, b)]
            total = jnp.concatenate(total, axis=1)
            for far in range(4):
                ref = out_refs[4 * half + far]
                ref[...] = total[far * block : (far + 1) * block].astype(ref.dtype)

    shape = (block, 2 * part)
    kinds = [F32, BF16, BF16, BF16] * 2
    outs = call(add_twice, [(shape, kind) for kind in kinds], (*outs[4:], *got))
    got = [flip(v, m) for v, m in zip(outs[1:4], (Y1, Y1 ^ Y3, Y3))]
    got += [flip(v, m) for v, m in zip(outs[5:8], (X1, X1 ^ X3, X3))]

    def add_last(*refs):
        for half in range(2):
            total = refs[half][...]
            for ref in refs[2 + 3 * half : 5 + 3 * half]:
                total += ref[...].astype(F32)
            at = slice(half * 2 * part, (half + 1) * 2 * part)
            refs[8][:, at] = total[: block // 2]
            refs[9][:, at] = total[block // 2 :].astype(BF16)

    shape = (block // 2, 4 * part)
    mine, away = call(add_last, [(shape, F32), (shape, BF16)], (outs[0], outs[4], *got))
    return mine + flip(away, ZH).astype(F32)


def on_device(features, conv_kernels, patch_weights, positions, out_cotangent):
    weight = patch_weights[0]
    width, depth = weight.shape
    kernel = conv_kernels[0].reshape(9 * C, C)
    section = lax.axis_index("section")
    place = lax.axis_index(SEQ)
    first_pair = section < 2

    order = jnp.arange(N_SEQ, dtype=jnp.int32)
    away = ((order & 1) << 5) | (((order >> 3) & 3) << 3) | (((order >> 1) & 3) << 1) | (order >> 5)
    blocks = away ^ place

    here, phase = section.reshape(1), (place % 4).reshape(1)
    piece = run_piece(blocks, weight)
    *rows, late, beside = run_rows(phase, features, out_cotangent, piece)
    piece = partner(piece)
    late, beside = beside_swap(late), flip(beside, CORE)

    image_id = jnp.minimum(3 * (place // 4) + place % 4, positions.shape[0] - 1)
    begin = positions[image_id]
    half = width // 2
    feature = (blocks[:, None] * (width // N_SEQ) + jnp.arange(width // N_SEQ)[None, :]).reshape(-1)
    rates = jnp.exp((feature % half).astype(F32) * (-math.log(10000.0) / half))
    is_sin = (feature < half)[None, :]
    steps = jnp.arange(HALF, dtype=jnp.int32)
    row_angle = (begin + HALF * steps).astype(F32)[:, None] * rates[None, :]
    col_angle = steps.astype(F32)[:, None] * rates[None, :]
    row_sin, row_cos = jnp.sin(row_angle), jnp.cos(row_angle)
    row_one = jnp.where(is_sin, row_sin, row_cos)
    row_two = jnp.where(is_sin, row_cos, -row_sin)
    col_cos, col_sin = jnp.cos(col_angle), jnp.sin(col_angle)

    codes = (row_one, row_two, col_cos, col_sin)

    near, kernels, skip_field, skip_recv, cotangent = gather_partner(
        piece, kernel, lambda: run_image(phase, rows, late, beside), (late, beside, *codes)
    )
    far = flip(near, CORE)
    start = run_start(here, cotangent, kernels, turned=True)

    tokens, active, first_lift, second_field = run_forward(
        here, blocks, skip_field, weight, near, far, codes, kernels
    )
    second_back, side, patch = run_second_pair(
        here, blocks, hop(second_field), skip_recv, start, weight, near, far, kernels
    )
    prior = jnp.where(first_pair, active, side)
    keep, send, patch = run_back(
        here, hop(second_back), skip_field, first_lift, tokens, prior, patch, near, far,
        kernels,
    )

    summed = run_sum(run_partial(keep, flip(send, CORE), patch, flip(patch, CORE)))
    tokens_in_all = positions.shape[0] * HALF * HALF
    return (summed * (1.0 / math.sqrt(tokens_in_all)))[None]


def solution(mesh):
    in_specs = (
        P("seq", None, None),
        P("section", None, None, None, None),
        P("section", None, None),
        P(),
        P("seq", None, None),
    )
    out_specs = P("section", "seq", None)
    return jax.shard_map(
        on_device, mesh=mesh, in_specs=in_specs, out_specs=out_specs, check_vma=False
    )
```

```python
import math

import jax
import jax.numpy as jnp
from jax import lax
from jax.experimental import pallas as pl
from jax.experimental.pallas import tpu as pltpu
from jax.sharding import PartitionSpec as P

NORM_EPS = 1e-05
BF16 = jnp.bfloat16
F32 = jnp.float32
SIDE = 32
HALF = SIDE // 2
C = 256
N_SEQ = 64
SEQ = "seq"

X1, X3, Y1, Y3, CORE, ZH = (1 << 3, 3 << 3, 1 << 1, 3 << 1, 1, 1 << 5)


def flip(value, mask):
    return lax.ppermute(value, SEQ, [(i, i ^ mask) for i in range(N_SEQ)])


def partner(value):
    return lax.ppermute(value, "section", [(0, 1), (1, 0), (2, 3), (3, 2)])


HOPS = [(1 * N_SEQ + q, 2 * N_SEQ + q) for q in range(N_SEQ)]
HOPS += [(q, 3 * N_SEQ + (q ^ ZH)) for q in range(N_SEQ)]
HOPS += [(j, i) for i, j in HOPS]


def hop(value):
    return lax.ppermute(value, ("section", SEQ), HOPS)


def beside_swap(value):
    pairs = [((2 * k - 1) % N_SEQ, 2 * k) for k in range(N_SEQ // 2)]
    return lax.ppermute(value, SEQ, pairs + [(j, i) for i, j in pairs])


def dot(left, right):
    return jnp.dot(left, right, preferred_element_type=F32)


def dot_nt(left, right):
    return lax.dot_general(left, right, (((1,), (1,)), ((), ())), preferred_element_type=F32)


def dot_tn(left, right):
    return lax.dot_general(left, right, (((0,), (0,)), ((), ())), preferred_element_type=F32)


def patchify(field):
    pairs = field.reshape(HALF, 2, HALF, 2 * C)
    return jnp.concatenate([pairs[:, 0], pairs[:, 1]], axis=-1).reshape(HALF * HALF, 4 * C)


def unpatchify(tokens):
    pairs = tokens.reshape(HALF, HALF, 4 * C)
    return jnp.stack([pairs[..., : 2 * C], pairs[..., 2 * C :]], axis=1).reshape(SIDE, HALF, 2 * C)


def silu(value):
    half = 0.5 * value
    return half + half * jnp.tanh(half)


def silu_slope(value):
    half = 0.5 * value
    t = jnp.tanh(half)
    return (0.5 + 0.5 * t) * (1.0 + half * (1.0 - t))


CHUNKS = 4
UNROLL = 4
VMEM = pl.BlockSpec(memory_space=pltpu.VMEM)
SMEM = pl.BlockSpec(memory_space=pltpu.SMEM)
ANY = pl.BlockSpec(memory_space=pl.ANY)
HBM = pl.BlockSpec(memory_space=pltpu.HBM)


def conv_in_kernel(field, kernel_ref, left_ref, right_ref, turned=False):
    even, odd = field[..., :C], field[..., C:]
    column = lax.broadcasted_iota(jnp.int32, (SIDE, HALF, C), 1)
    before = jnp.where(column == 0, 0.0, pltpu.roll(odd, 1, 1))
    after = jnp.where(column == HALF - 1, 0.0, pltpu.roll(even, HALF - 1, 1))
    middle = field.astype(BF16)
    left_ref[1 : SIDE + 1, :, C:] = middle
    left_ref[1 : SIDE + 1, :, :C] = before.astype(BF16)
    right_ref[1 : SIDE + 1, :, : 2 * C] = middle
    right_ref[1 : SIDE + 1, :, 2 * C :] = after.astype(BF16)
    out = []
    for ref in (left_ref, right_ref):
        edge = jnp.zeros((HALF, 3 * C), BF16)
        ref[0] = edge
        ref[SIDE + 1] = edge
        total = None
        for row in range(3):
            taps = ref[row : row + SIDE].reshape(SIDE * HALF, 3 * C)
            if turned:
                for column in range(3):
                    tap = (2 - row) * 3 + 2 - column
                    weight = kernel_ref[tap * C : (tap + 1) * C]
                    term = dot_nt(taps[:, column * C : (column + 1) * C], weight)
                    total = term if total is None else total + term
            else:
                term = dot(taps, kernel_ref[row * 3 * C : (row + 1) * 3 * C])
                total = term if total is None else total + term
        out.append(total.reshape(SIDE, HALF, C))
    return jnp.concatenate(out, axis=-1)


def choose(to_ref, mine, own_ref, other_ref):
    @pl.when(mine)
    def _():
        to_ref[...] = own_ref[...]

    @pl.when(jnp.logical_not(mine))
    def _():
        to_ref[...] = other_ref[...]


def rounded(value):
    return value.astype(BF16).astype(F32)


class Weights:
    def __init__(self, index_ref, own_ref, near_ref, far_ref, both_ref, sems, parity):
        self.args = (index_ref, own_ref, near_ref, far_ref, both_ref, sems, parity)
        self.rows = both_ref.shape[1] // CHUNKS
        self.share = both_ref.shape[1] // N_SEQ

    def start(self, own=True):
        index_ref, own_ref, near_ref, far_ref, both_ref, sems, parity = self.args
        per = N_SEQ // CHUNKS
        for block in range(N_SEQ if own else 0):
            source = pl.multiple_of(index_ref[block] * self.share, self.share)
            pltpu.make_async_copy(
                own_ref.at[pl.ds(source, self.share)],
                both_ref.at[parity, pl.ds(block * self.share, self.share)],
                sems.at[parity, block // per],
            ).start()
        for chunk in range(CHUNKS):
            source = near_ref if chunk < CHUNKS // 2 else far_ref
            pltpu.make_async_copy(
                source.at[pl.ds(chunk % (CHUNKS // 2) * self.rows, self.rows)],
                both_ref.at[1 - parity, pl.ds(chunk * self.rows, self.rows)],
                sems.at[1 - parity, chunk],
            ).start()

    def sweep(self, slot, step, wait=False):
        _, _, near_ref, _, both_ref, sems, _ = self.args

        @pl.loop(0, CHUNKS, unroll=UNROLL)
        def _(chunk):
            rows = pl.ds(pl.multiple_of(chunk * self.rows, self.rows), self.rows)
            if wait:
                pltpu.make_async_copy(
                    near_ref.at[pl.ds(0, self.rows)], both_ref.at[slot, rows], sems.at[slot, chunk]
                ).wait()
            step(chunk, both_ref[slot, rows])


def weight_scratch(width, depth):
    return [pltpu.VMEM((2, width, depth), BF16), pltpu.SemaphoreType.DMA((2, CHUNKS))]


def lanes(chunk, count):
    return pl.ds(pl.multiple_of(chunk * count, count), count)


TAPS = [pltpu.VMEM((SIDE + 2, HALF, 3 * C), BF16)] * 2
TOKENS = HALF * HALF
KERNEL = [pltpu.VMEM((9 * C, C), BF16)]


def params(mib):
    return pltpu.CompilerParams(vmem_limit_bytes=mib * 1024 * 1024)


def call(body, outs, args, after=()):
    count = len(args)

    def with_after(*refs):
        body(*refs[:count], *refs[count + len(after) :])

    return pl.pallas_call(
        with_after,
        out_shape=[jax.ShapeDtypeStruct(shape, kind) for shape, kind in outs],
        in_specs=[VMEM] * count + [ANY] * len(after),
        out_specs=[VMEM] * len(outs),
        compiler_params=params(20),
    )(*args, *after)


def run_rows(section, phase, features, cotangent, after):
    count = features.shape[0]
    wide = 2 * C

    def body(section_ref, phase_ref, features_ref, cotangent_ref, _, rows_ref, late_ref, beside_ref, value_ref):
        for part in range(2):
            at = slice(part * 128, (part + 1) * 128)

            @pl.when(section_ref[0] < 2)
            def _(part=part, at=at):
                value_ref[part] = features_ref[:, :, at].astype(F32)

            @pl.when(section_ref[0] >= 2)
            def _(part=part, at=at):
                value_ref[part] = cotangent_ref[:, :, at].astype(F32)

        quarters = [
            value_ref[part, :, pl.ds(column, HALF, stride=2), :]
            for column in range(2)
            for part in range(2)
        ]
        rows = jnp.concatenate(quarters, axis=-1).astype(BF16)
        rows_ref[...] = rows
        late_ref[...] = rows[8:]

        @pl.when(phase_ref[0] == 0)
        def _():
            beside_ref[...] = rows[16:]

        @pl.when(phase_ref[0] != 0)
        def _():
            beside_ref[...] = rows[:8]

    shapes = [(count, HALF, wide), (16, HALF, wide), (8, HALF, wide)]
    return pl.pallas_call(
        body,
        out_shape=[jax.ShapeDtypeStruct(shape, BF16) for shape in shapes],
        in_specs=[SMEM, SMEM, VMEM, VMEM, ANY],
        out_specs=[VMEM] * 3,
        scratch_shapes=[pltpu.VMEM((2, count, SIDE, 128), F32)],
        compiler_params=params(12),
        name="rows",
    )(section, phase, features, cotangent, after)


def run_image(phase, rows, late, beside):
    def body(phase_ref, rows_ref, late_ref, beside_ref, out_ref):
        kind = phase_ref[0]

        @pl.when(kind == 0)
        def _():
            out_ref[:16] = late_ref[...]
            out_ref[16:] = rows_ref[:16]

        @pl.when(kind == 1)
        def _():
            out_ref[:8] = beside_ref[...]
            out_ref[8:] = rows_ref[...]

        @pl.when(kind == 2)
        def _():
            out_ref[:24] = rows_ref[...]
            out_ref[24:] = beside_ref[...]

        @pl.when(kind == 3)
        def _():
            out_ref[...] = jnp.zeros_like(out_ref)

    return pl.pallas_call(
        body,
        out_shape=jax.ShapeDtypeStruct((SIDE, HALF, 2 * C), BF16),
        in_specs=[SMEM] + [VMEM] * 3,
        out_specs=VMEM,
        compiler_params=params(12),
        name="image",
    )(phase, rows, late, beside)


def run_start(section, image, kernels, turned):
    def body(section_ref, image_ref, own_ref, other_ref, out_ref, left_ref, right_ref, kernel_ref):
        where = section_ref[0]

        @pl.when((where >= 2) if turned else (where < 2))
        def _():
            choose(kernel_ref, where == (3 if turned else 0), own_ref, other_ref)
            field = image_ref[...].astype(F32)
            field = conv_in_kernel(field, kernel_ref, left_ref, right_ref, turned=turned)
            out_ref[...] = field.astype(out_ref.dtype)

    return pl.pallas_call(
        body,
        out_shape=jax.ShapeDtypeStruct((SIDE, HALF, 2 * C), F32 if turned else BF16),
        in_specs=[SMEM] + [VMEM] * 3,
        out_specs=VMEM,
        scratch_shapes=TAPS + KERNEL,
        compiler_params=params(16),
        name="start_turned" if turned else "start",
    )(section, image, *kernels)


def run_piece(blocks, weight):
    share, depth = weight.shape[0] // N_SEQ, weight.shape[1]

    def body(index_ref, weight_ref, out_ref):
        out_ref[...] = weight_ref[...]

    return pl.pallas_call(
        body,
        grid_spec=pltpu.PrefetchScalarGridSpec(
            num_scalar_prefetch=1,
            grid=(2,),
            in_specs=[pl.BlockSpec((share, depth), lambda i, index: (index[i], 0))],
            out_specs=pl.BlockSpec((share, depth), lambda i, index: (i, 0)),
        ),
        out_shape=jax.ShapeDtypeStruct((2 * share, depth), weight.dtype),
        compiler_params=params(58),
    )(blocks, weight)


def gather_partner(piece, kernel, before, meanwhile):
    rows, depth = piece.shape
    half, part = depth // 2, depth // 4

    def split(piece_ref, kernel_ref, first_ref, second_ref, again_ref):
        first_ref[...] = piece_ref[:, :half]
        second_ref[...] = piece_ref[:, half:]
        again_ref[...] = kernel_ref[...]

    outs = [((rows, half), BF16)] * 2 + [(kernel.shape, BF16)]
    first, second, again = call(split, outs, (piece, kernel), before)
    got = [flip(first, m) for m in (X1, X1 ^ X3, X3)] + [flip(second, m) for m in (Y1, Y1 ^ Y3, Y3)]
    kernels = (kernel, partner(again))

    def stack(*refs):
        for side in range(2):
            for far in range(4):
                source = refs[side] if far == 0 else refs[2 + 3 * side + far - 1]
                refs[8 + side][far * rows : (far + 1) * rows] = source[...]

    wide = call(stack, [((4 * rows, half), BF16)] * 2, (first, second, *got))
    rings = ((Y1, Y3), (X1, X3))
    near = [flip(value, ring[0]) for value, ring in zip(wide, rings)]
    far = [flip(value, ring[1]) for value, ring in zip(wide, rings)]
    skip_field, start = meanwhile(wide[0], kernels)

    def cut(*refs):
        for side in range(2):
            refs[4 + 2 * side][...] = refs[side][:, :part]
            refs[5 + 2 * side][...] = refs[2 + side][:, part:]

    outs = [((4 * rows, part), BF16)] * 4
    parts = call(cut, outs, (*far, *near))
    low = [flip(parts[2 * side], ring[0]) for side, ring in enumerate(rings)]
    high = [flip(parts[2 * side + 1], ring[1]) for side, ring in enumerate(rings)]

    def join(*refs):
        out_ref = refs[10]
        for side in range(2):
            base = side * half
            mine, one, three = refs[side], refs[2 + side], refs[4 + side]
            for outer in range(4):
                sources = {0: [mine], 1: [one], 3: [three], 2: [refs[6 + side], refs[8 + side]]}[outer]
                for j, source in enumerate(sources):
                    count = source.shape[1]
                    at = slice(base + j * count, base + (j + 1) * count)
                    for inner in range(4):
                        block = source[inner * rows : (inner + 1) * rows]
                        x, y = (inner, outer) if side == 0 else (outer, inner)
                        start = (4 * x + y) * rows
                        out_ref[start : start + rows, at] = block

    args = (*wide, *near, *far, *low, *high)
    held = call(join, [((16 * rows, depth), BF16)], args, (skip_field,))[0]
    return held, kernels, skip_field, start


def run_forward(section, blocks, skip, own, near, far, codes, kernels):
    width, depth = own.shape
    cols = width // CHUNKS

    def body(
        section_ref, index_ref, skip_ref, own_ref, near_ref, far_ref, one_ref, two_ref, cos_ref,
        sin_ref, own_kernel_ref, other_kernel_ref, tokens_out, act_out, lift_out, field_ref, sum_ref,
        left_ref, right_ref, kernel_ref, both_ref, sems, tokens_ref,
        act_ref, lift_ref, out_sems,
    ):
        parity = section_ref[0] % 2

        @pl.when(section_ref[0] < 2)
        def _():
            weights = Weights(index_ref, own_ref, near_ref, far_ref, both_ref, sems, parity)
            weights.start()
            choose(kernel_ref, parity == 1, own_kernel_ref, other_kernel_ref)
            patch = patchify(skip_ref[...])
            sum_ref[...] = jnp.zeros_like(sum_ref)

            def embed(chunk, rows):
                at = lanes(chunk, cols)
                code = one_ref[:, at][:, None] * cos_ref[:, at][None]
                code += two_ref[:, at][:, None] * sin_ref[:, at][None]
                value = dot_nt(patch, rows) + code.reshape(TOKENS, cols)
                value = value.astype(BF16)
                tokens_ref[:, at] = value
                value = value.astype(F32)
                sum_ref[...] += jnp.sum(value * value, axis=-1, keepdims=True)

            weights.sweep(0, embed, wait=True)
            scale = lax.rsqrt(sum_ref[...] * (1.0 / width) + NORM_EPS)
            lift_ref[...] = jnp.zeros_like(lift_ref)

            def raise_up(chunk, rows):
                at = lanes(chunk, cols)
                active = silu(tokens_ref[:, at].astype(F32) * scale).astype(BF16)
                act_ref[:, at] = active
                lift_ref[...] += dot(active, rows)

            weights.sweep(1, raise_up, wait=True)

            pairs = ((tokens_ref, tokens_out), (act_ref, act_out), (lift_ref, lift_out))
            copies = [
                pltpu.make_async_copy(source, target, out_sems.at[n])
                for n, (source, target) in enumerate(pairs)
            ]
            for copy in copies:
                copy.start()
            field = unpatchify(rounded(silu(lift_ref[...])))
            field_ref[...] = conv_in_kernel(field, kernel_ref, left_ref, right_ref).astype(BF16)
            for copy in copies:
                copy.wait()

    return pl.pallas_call(
        body,
        out_shape=[
            jax.ShapeDtypeStruct((TOKENS, width), BF16),
            jax.ShapeDtypeStruct((TOKENS, width), BF16),
            jax.ShapeDtypeStruct((TOKENS, depth), F32),
            jax.ShapeDtypeStruct((SIDE, HALF, 2 * C), BF16),
        ],
        in_specs=[SMEM, SMEM, VMEM] + [HBM] * 3 + [VMEM] * 6,
        out_specs=[HBM] * 3 + [VMEM],
        scratch_shapes=[pltpu.VMEM((TOKENS, 1), F32)]
        + TAPS
        + KERNEL
        + weight_scratch(width, depth)
        + [
            pltpu.VMEM((TOKENS, width), BF16),
            pltpu.VMEM((TOKENS, width), BF16),
            pltpu.VMEM((TOKENS, depth), F32),
            pltpu.SemaphoreType.DMA((3,)),
        ],
        compiler_params=params(56),
        name="forward_first_pair",
    )(section, blocks, skip, own, near, far, *codes, *kernels)


def run_second_pair(section, blocks, second, skip, start, own, near, far, kernels):
    width, depth = own.shape
    cols = width // CHUNKS

    def body(
        section_ref, index_ref, second_ref, skip_ref, start_ref, own_ref, near_ref, far_ref,
        own_kernel_ref, other_kernel_ref, back_ref, side_ref, patch_ref, sum_ref, left_ref,
        right_ref, kernel_ref, tokens_ref, inner_ref, lift_ref, both_ref, sems,
    ):
        parity = section_ref[0] % 2

        @pl.when(section_ref[0] >= 2)
        def _():
            weights = Weights(index_ref, own_ref, near_ref, far_ref, both_ref, sems, parity)
            weights.start()
            choose(kernel_ref, parity == 0, own_kernel_ref, other_kernel_ref)
            field = rounded(silu(second_ref[...].astype(F32)))
            field = conv_in_kernel(field, kernel_ref, left_ref, right_ref).astype(BF16)
            patch_ref[...] = patchify(field)
            sum_ref[...] = jnp.zeros_like(sum_ref)

            def embed(chunk, rows):
                value = dot_nt(patch_ref[...], rows).astype(BF16)
                tokens_ref[:, lanes(chunk, cols)] = value
                value = value.astype(F32)
                sum_ref[...] += jnp.sum(value * value, axis=-1, keepdims=True)

            weights.sweep(0, embed, wait=True)
            scale = lax.rsqrt(sum_ref[...] * (1.0 / width) + NORM_EPS)
            lift_ref[...] = patchify(skip_ref[...]).astype(F32)

            def raise_up(chunk, rows):
                at = lanes(chunk, cols)
                active = silu(tokens_ref[:, at].astype(F32) * scale).astype(BF16)
                side_ref[:, at] = active
                lift_ref[...] += dot(active, rows)

            weights.sweep(1, raise_up, wait=True)
            last_patch = (patchify(start_ref[...]) * silu_slope(lift_ref[...])).astype(BF16)

            @pl.when(parity == 1)
            def _():
                patch_ref[...] = last_patch

            sum_ref[...] = jnp.zeros_like(sum_ref)

            def descend(chunk, rows):
                at = lanes(chunk, cols)
                normal = tokens_ref[:, at].astype(F32) * scale
                inner = dot_nt(last_patch, rows) * silu_slope(normal)
                inner_ref[:, at] = inner
                sum_ref[...] += jnp.sum(inner * normal, axis=-1, keepdims=True)

            weights.sweep(1, descend)
            mean = sum_ref[...] * (1.0 / width)
            lift_ref[...] = jnp.zeros_like(lift_ref)

            def lower(chunk, rows):
                at = lanes(chunk, cols)
                normal = tokens_ref[:, at].astype(F32) * scale
                back = (scale * (inner_ref[:, at] - normal * mean)).astype(BF16)

                @pl.when(parity == 0)
                def _():
                    side_ref[:, at] = back

                lift_ref[...] += dot(back, rows)

            weights.sweep(0, lower)
            field = unpatchify(rounded(lift_ref[...]))
            field = conv_in_kernel(field, kernel_ref, left_ref, right_ref, turned=True)
            back_ref[...] = (field * silu_slope(second_ref[...].astype(F32))).astype(BF16)

    return pl.pallas_call(
        body,
        out_shape=[
            jax.ShapeDtypeStruct((SIDE, HALF, 2 * C), BF16),
            jax.ShapeDtypeStruct((TOKENS, width), BF16),
            jax.ShapeDtypeStruct((TOKENS, depth), BF16),
        ],
        in_specs=[SMEM, SMEM] + [VMEM] * 3 + [HBM] * 3 + [VMEM] * 2,
        out_specs=[VMEM] * 3,
        scratch_shapes=[pltpu.VMEM((TOKENS, 1), F32)]
        + TAPS
        + KERNEL
        + [
            pltpu.VMEM((TOKENS, width), BF16),
            pltpu.VMEM((TOKENS, width), F32),
            pltpu.VMEM((TOKENS, depth), F32),
        ]
        + weight_scratch(width, depth),
        compiler_params=params(53),
        name="second_pair",
    )(section, blocks, second, skip, start, own, near, far, *kernels)


def run_back(section, given, skip, lift, tokens, prior, patch, near, far, kernels):
    width, depth = tokens.shape[1], lift.shape[1]
    cols = width // CHUNKS

    def body(
        section_ref, given_ref, skip_ref, lift_ref, tokens_ref, prior_ref, known_ref, near_ref,
        far_ref, own_kernel_ref, other_kernel_ref, keep_ref, send_ref, patch_ref, sum_ref, left_ref,
        right_ref, kernel_ref, inner_ref, both_ref, sems,
    ):
        where = section_ref[0]
        weights = Weights(None, None, near_ref, far_ref, both_ref, sems, 1)

        @pl.when(where == 0)
        def _():
            weights.start(own=False)

        @pl.when(where >= 1)
        def _():
            keep_ref[...] = prior_ref[:, : width // 2]
            send_ref[...] = prior_ref[:, width // 2 :]

        @pl.when(where >= 2)
        def _():
            patch_ref[...] = known_ref[...]

        @pl.when(where < 2)
        def _():
            choose(kernel_ref, where == 1, own_kernel_ref, other_kernel_ref)
            field = given_ref[...].astype(F32)
            field = conv_in_kernel(field, kernel_ref, left_ref, right_ref, turned=True)
            patch_ref[...] = (patchify(field) * silu_slope(lift_ref[...])).astype(BF16)

        @pl.when(where == 0)
        def _():
            sum_ref[...] = jnp.zeros_like(sum_ref)

            @pl.loop(0, CHUNKS, unroll=UNROLL)
            def _(chunk):
                value = tokens_ref[:, lanes(chunk, cols)].astype(F32)
                sum_ref[...] += jnp.sum(value * value, axis=-1, keepdims=True)

            scale = lax.rsqrt(sum_ref[...] * (1.0 / width) + NORM_EPS)
            sum_ref[...] = jnp.zeros_like(sum_ref)

            def descend(chunk, rows):
                at = lanes(chunk, cols)
                normal = tokens_ref[:, at].astype(F32) * scale
                inner = dot_nt(patch_ref[...], rows) * silu_slope(normal)
                inner_ref[:, at] = inner
                sum_ref[...] += jnp.sum(inner * normal, axis=-1, keepdims=True)

            weights.sweep(0, descend, wait=True)
            mean = sum_ref[...] * (1.0 / width)

            for first, ref in ((0, keep_ref), (CHUNKS // 2, send_ref)):

                @pl.loop(0, CHUNKS // 2, unroll=UNROLL)
                def _(i, first=first, ref=ref):
                    at = lanes(first + i, cols)
                    normal = tokens_ref[:, at].astype(F32) * scale
                    back = scale * (inner_ref[:, at] - normal * mean)
                    ref[:, lanes(i, cols)] = back.astype(BF16)

            patch_ref[...] = patchify(skip_ref[...])

    return pl.pallas_call(
        body,
        out_shape=[
            jax.ShapeDtypeStruct((TOKENS, width // 2), BF16),
            jax.ShapeDtypeStruct((TOKENS, width // 2), BF16),
            jax.ShapeDtypeStruct((TOKENS, depth), BF16),
        ],
        in_specs=[SMEM] + [VMEM] * 6 + [HBM] * 2 + [VMEM] * 2,
        out_specs=[VMEM] * 3,
        scratch_shapes=[pltpu.VMEM((TOKENS, 1), F32)]
        + TAPS
        + KERNEL
        + [
            pltpu.VMEM((TOKENS, width), F32),
            pltpu.VMEM((1, width, depth), BF16),
            pltpu.SemaphoreType.DMA((1, CHUNKS)),
        ],
        compiler_params=params(30),
        name="back_first_pair",
    )(section, given, skip, lift, tokens, prior, patch, near, far, *kernels)


SENT = {"a": (1, 2), "b": (3, 2)}
KEPT = {"a": (0, 3), "b": (0, 1)}


def run_partial(keep, recv, patch, patch_recv):
    half, depth = keep.shape[1], patch.shape[1]
    part, block = depth // 4, half // 16

    def body(keep_ref, recv_ref, patch_ref, other_ref, *out_refs):
        tokens = jnp.concatenate([keep_ref[...], recv_ref[...]], axis=0)
        patches = jnp.concatenate([patch_ref[...], other_ref[...]], axis=0)
        for column in range(4):
            name = "ab"[column % 2]
            sent_ref, kept_ref = out_refs[column], out_refs[4 + column]
            right = patches[:, column * part : (column + 1) * part]
            for i in range(2):
                for ref, far in ((sent_ref, SENT[name][i]), (kept_ref, KEPT[name][i])):
                    if column < 2:
                        left = tokens[:, far * 4 * block : (far + 1) * 4 * block]
                    else:
                        left = jnp.concatenate(
                            [tokens[:, (4 * j + far) * block :][:, :block] for j in range(4)], axis=1
                        )
                    ref[i] = dot_tn(left, right).astype(ref.dtype)

    shape = (2, 4 * block, part)
    outs = call(body, [(shape, BF16)] * 4 + [(shape, F32)] * 4, (keep, recv, patch, patch_recv))
    return outs[:4], outs[4:]


FIRST_RINGS = ((X1, X3), (X3, X1), (Y1, Y3), (Y3, Y1))


def run_sum(partial):
    sent, kept = partial
    got = [flip(value, ring[0]) for value, ring in zip(sent, FIRST_RINGS)]
    rows, part = kept[0].shape[1:]
    block = rows // 4

    def add_once(*refs):
        kept_refs, got_refs, sent_refs, out_refs = refs[:4], refs[4:8], refs[8:12], refs[12:]
        for kept_ref, got_ref, sent_ref, out_ref in zip(kept_refs, got_refs, sent_refs, out_refs):
            total = kept_ref[...] + got_ref[...].astype(F32)
            out_ref[...] = total[0]
            sent_ref[...] = total[1].astype(BF16)

    shape = (rows, part)
    outs = call(add_once, [(shape, BF16)] * 4 + [(shape, F32)] * 4, (*kept, *got))
    got = [flip(value, ring[1]) for value, ring in zip(outs[:4], FIRST_RINGS)]

    def add_twice(*refs):
        kept_refs, got_refs, out_refs = refs[:4], refs[4:8], refs[8:]
        for half in range(2):
            a, b = 2 * half, 2 * half + 1
            total = [kept_refs[i][...] + got_refs[i][...].astype(F32) for i in (a, b)]
            total = jnp.concatenate(total, axis=1)
            for far in range(4):
                ref = out_refs[4 * half + far]
                ref[...] = total[far * block : (far + 1) * block].astype(ref.dtype)

    shape = (block, 2 * part)
    kinds = [F32, BF16, BF16, BF16] * 2
    outs = call(add_twice, [(shape, kind) for kind in kinds], (*outs[4:], *got))
    got = [flip(v, m) for v, m in zip(outs[1:4], (Y1, Y1 ^ Y3, Y3))]
    got += [flip(v, m) for v, m in zip(outs[5:8], (X1, X1 ^ X3, X3))]

    def add_last(*refs):
        for half in range(2):
            total = refs[half][...]
            for ref in refs[2 + 3 * half : 5 + 3 * half]:
                total += ref[...].astype(F32)
            at = slice(half * 2 * part, (half + 1) * 2 * part)
            refs[8][:, at] = total[: block // 2]
            refs[9][:, at] = total[block // 2 :].astype(BF16)

    shape = (block // 2, 4 * part)
    mine, away = call(add_last, [(shape, F32), (shape, BF16)], (outs[0], outs[4], *got))
    return mine + flip(away, ZH).astype(F32)


def on_device(features, conv_kernels, patch_weights, positions, out_cotangent):
    weight = patch_weights[0]
    width, depth = weight.shape
    kernel = conv_kernels[0].reshape(9 * C, C)
    section = lax.axis_index("section")
    place = lax.axis_index(SEQ)
    first_pair = section < 2

    order = jnp.arange(N_SEQ, dtype=jnp.int32)
    away = ((order & 1) << 5) | (((order >> 3) & 3) << 3) | (((order >> 1) & 3) << 1) | (order >> 5)
    blocks = away ^ place

    here, phase = section.reshape(1), (place % 4).reshape(1)
    piece = partner(run_piece(blocks, weight))
    across = hop(out_cotangent)

    image_id = jnp.minimum(3 * (place // 4) + place % 4, positions.shape[0] - 1)
    begin = positions[image_id]
    half = width // 2
    feature = (blocks[:, None] * (width // N_SEQ) + jnp.arange(width // N_SEQ)[None, :]).reshape(-1)
    rates = jnp.exp((feature % half).astype(F32) * (-math.log(10000.0) / half))
    is_sin = (feature < half)[None, :]
    steps = jnp.arange(HALF, dtype=jnp.int32)
    row_angle = (begin + HALF * steps).astype(F32)[:, None] * rates[None, :]
    col_angle = steps.astype(F32)[:, None] * rates[None, :]
    row_sin, row_cos = jnp.sin(row_angle), jnp.cos(row_angle)
    row_one = jnp.where(is_sin, row_sin, row_cos)
    row_two = jnp.where(is_sin, row_cos, -row_sin)
    col_cos, col_sin = jnp.cos(col_angle), jnp.sin(col_angle)

    codes = (row_one, row_two, col_cos, col_sin)

    def first_convolutions(after, kernels):
        rows, late, beside = run_rows(here, phase, features, across, after)
        image = run_image(phase, rows, beside_swap(late), flip(beside, CORE))
        return [run_start(here, image, kernels, turned=turned) for turned in (False, True)]

    near, kernels, skip_field, start = gather_partner(piece, kernel, codes, first_convolutions)
    far = flip(near, CORE)
    skip_recv = hop(skip_field)

    tokens, active, first_lift, second_field = run_forward(
        here, blocks, skip_field, weight, near, far, codes, kernels
    )
    second_back, side, patch = run_second_pair(
        here, blocks, hop(second_field), skip_recv, start, weight, near, far, kernels
    )
    prior = jnp.where(first_pair, active, side)
    keep, send, patch = run_back(
        here, hop(second_back), skip_field, first_lift, tokens, prior, patch, near, far,
        kernels,
    )

    summed = run_sum(run_partial(keep, flip(send, CORE), patch, flip(patch, CORE)))
    tokens_in_all = positions.shape[0] * HALF * HALF
    return (summed * (1.0 / math.sqrt(tokens_in_all)))[None]


def solution(mesh):
    in_specs = (
        P("seq", None, None),
        P("section", None, None, None, None),
        P("section", None, None),
        P(),
        P("seq", None, None),
    )
    out_specs = P("section", "seq", None)
    return jax.shard_map(
        on_device, mesh=mesh, in_specs=in_specs, out_specs=out_specs, check_vma=False
    )
```

```python
import math

import jax
import jax.numpy as jnp
from jax import lax
from jax.experimental import pallas as pl
from jax.experimental.pallas import tpu as pltpu
from jax.sharding import PartitionSpec as P

NORM_EPS = 1e-05
BF16 = jnp.bfloat16
F32 = jnp.float32
SIDE = 32
HALF = SIDE // 2
C = 256
N_SEQ = 64
SEQ = "seq"

X1, X3, Y1, Y3, CORE, ZH = (1 << 3, 3 << 3, 1 << 1, 3 << 1, 1, 1 << 5)


def flip(value, mask):
    return lax.ppermute(value, SEQ, [(i, i ^ mask) for i in range(N_SEQ)])


def partner(value):
    return lax.ppermute(value, "section", [(0, 1), (1, 0), (2, 3), (3, 2)])


HOPS = [(1 * N_SEQ + q, 2 * N_SEQ + q) for q in range(N_SEQ)]
HOPS += [(q, 3 * N_SEQ + (q ^ ZH)) for q in range(N_SEQ)]
HOPS += [(j, i) for i, j in HOPS]


def hop(value):
    return lax.ppermute(value, ("section", SEQ), HOPS)


def beside_swap(value):
    pairs = [((2 * k - 1) % N_SEQ, 2 * k) for k in range(N_SEQ // 2)]
    return lax.ppermute(value, SEQ, pairs + [(j, i) for i, j in pairs])


def dot(left, right):
    return jnp.dot(left, right, preferred_element_type=F32)


def dot_nt(left, right):
    return lax.dot_general(left, right, (((1,), (1,)), ((), ())), preferred_element_type=F32)


def dot_tn(left, right):
    return lax.dot_general(left, right, (((0,), (0,)), ((), ())), preferred_element_type=F32)


def patchify(field):
    pairs = field.reshape(HALF, 2, HALF, 2 * C)
    return jnp.concatenate([pairs[:, 0], pairs[:, 1]], axis=-1).reshape(HALF * HALF, 4 * C)


def unpatchify(tokens):
    pairs = tokens.reshape(HALF, HALF, 4 * C)
    return jnp.stack([pairs[..., : 2 * C], pairs[..., 2 * C :]], axis=1).reshape(SIDE, HALF, 2 * C)


def silu(value):
    half = 0.5 * value
    return half + half * jnp.tanh(half)


def silu_slope(value):
    half = 0.5 * value
    t = jnp.tanh(half)
    return (0.5 + 0.5 * t) * (1.0 + half * (1.0 - t))


CHUNKS = 4
UNROLL = 4
VMEM = pl.BlockSpec(memory_space=pltpu.VMEM)
SMEM = pl.BlockSpec(memory_space=pltpu.SMEM)
ANY = pl.BlockSpec(memory_space=pl.ANY)
HBM = pl.BlockSpec(memory_space=pltpu.HBM)


def conv_in_kernel(field, kernel_ref, left_ref, right_ref, turned=False):
    even, odd = field[..., :C], field[..., C:]
    column = lax.broadcasted_iota(jnp.int32, (SIDE, HALF, C), 1)
    before = jnp.where(column == 0, 0.0, pltpu.roll(odd, 1, 1))
    after = jnp.where(column == HALF - 1, 0.0, pltpu.roll(even, HALF - 1, 1))
    middle = field.astype(BF16)
    left_ref[1 : SIDE + 1, :, C:] = middle
    left_ref[1 : SIDE + 1, :, :C] = before.astype(BF16)
    right_ref[1 : SIDE + 1, :, : 2 * C] = middle
    right_ref[1 : SIDE + 1, :, 2 * C :] = after.astype(BF16)
    out = []
    for ref in (left_ref, right_ref):
        edge = jnp.zeros((HALF, 3 * C), BF16)
        ref[0] = edge
        ref[SIDE + 1] = edge
        total = None
        for row in range(3):
            taps = ref[row : row + SIDE].reshape(SIDE * HALF, 3 * C)
            if turned:
                for column in range(3):
                    tap = (2 - row) * 3 + 2 - column
                    weight = kernel_ref[tap * C : (tap + 1) * C]
                    term = dot_nt(taps[:, column * C : (column + 1) * C], weight)
                    total = term if total is None else total + term
            else:
                term = dot(taps, kernel_ref[row * 3 * C : (row + 1) * 3 * C])
                total = term if total is None else total + term
        out.append(total.reshape(SIDE, HALF, C))
    return jnp.concatenate(out, axis=-1)


def choose(to_ref, mine, core, own_ref, near_ref, rest_ref):
    half = near_ref.shape[0]

    @pl.when(mine)
    def _():
        to_ref[...] = own_ref[...]

    @pl.when(jnp.logical_not(mine))
    def _():
        to_ref[pl.ds(pl.multiple_of(core * half, half), half)] = near_ref[...]
        to_ref[pl.ds(pl.multiple_of((1 - core) * half, half), half)] = rest_ref[...]


def rounded(value):
    return value.astype(BF16).astype(F32)


class Weights:
    def __init__(self, index_ref, own_ref, near_ref, far_ref, both_ref, sems, parity):
        self.args = (index_ref, own_ref, near_ref, far_ref, both_ref, sems, parity)
        self.rows = both_ref.shape[1] // CHUNKS
        self.share = both_ref.shape[1] // N_SEQ

    def start(self, own=True):
        index_ref, own_ref, near_ref, far_ref, both_ref, sems, parity = self.args
        per = N_SEQ // CHUNKS
        for block in range(N_SEQ if own else 0):
            source = pl.multiple_of(index_ref[block] * self.share, self.share)
            pltpu.make_async_copy(
                own_ref.at[pl.ds(source, self.share)],
                both_ref.at[parity, pl.ds(block * self.share, self.share)],
                sems.at[parity, block // per],
            ).start()
        for chunk in range(CHUNKS):
            source = near_ref if chunk < CHUNKS // 2 else far_ref
            pltpu.make_async_copy(
                source.at[pl.ds(chunk % (CHUNKS // 2) * self.rows, self.rows)],
                both_ref.at[1 - parity, pl.ds(chunk * self.rows, self.rows)],
                sems.at[1 - parity, chunk],
            ).start()

    def sweep(self, slot, step, wait=False):
        _, _, near_ref, _, both_ref, sems, _ = self.args

        @pl.loop(0, CHUNKS, unroll=UNROLL)
        def _(chunk):
            rows = pl.ds(pl.multiple_of(chunk * self.rows, self.rows), self.rows)
            if wait:
                pltpu.make_async_copy(
                    near_ref.at[pl.ds(0, self.rows)], both_ref.at[slot, rows], sems.at[slot, chunk]
                ).wait()
            step(chunk, both_ref[slot, rows])


def weight_scratch(width, depth):
    return [pltpu.VMEM((2, width, depth), BF16), pltpu.SemaphoreType.DMA((2, CHUNKS))]


def lanes(chunk, count):
    return pl.ds(pl.multiple_of(chunk * count, count), count)


TAPS = [pltpu.VMEM((SIDE + 2, HALF, 3 * C), BF16)] * 2
TOKENS = HALF * HALF
KERNEL = [pltpu.VMEM((9 * C, C), BF16)]


def params(mib):
    return pltpu.CompilerParams(vmem_limit_bytes=mib * 1024 * 1024)


def call(body, outs, args, after=(), scalars=()):
    count = len(scalars) + len(args)

    def with_after(*refs):
        body(*refs[:count], *refs[count + len(after) :])

    return pl.pallas_call(
        with_after,
        out_shape=[jax.ShapeDtypeStruct(shape, kind) for shape, kind in outs],
        in_specs=[SMEM] * len(scalars) + [VMEM] * len(args) + [ANY] * len(after),
        out_specs=[VMEM] * len(outs),
        compiler_params=params(20),
    )(*scalars, *args, *after)


def run_rows(section, phase, features, cotangent, after):
    count = features.shape[0]
    wide = 2 * C

    def body(section_ref, phase_ref, features_ref, cotangent_ref, _, rows_ref, late_ref, beside_ref, value_ref):
        for part in range(2):
            at = slice(part * 128, (part + 1) * 128)

            @pl.when(section_ref[0] < 2)
            def _(part=part, at=at):
                value_ref[part] = features_ref[:, :, at].astype(F32)

            @pl.when(section_ref[0] >= 2)
            def _(part=part, at=at):
                value_ref[part] = cotangent_ref[:, :, at].astype(F32)

        quarters = [
            value_ref[part, :, pl.ds(column, HALF, stride=2), :]
            for column in range(2)
            for part in range(2)
        ]
        rows = jnp.concatenate(quarters, axis=-1).astype(BF16)
        rows_ref[...] = rows
        late_ref[...] = rows[8:]

        @pl.when(phase_ref[0] == 0)
        def _():
            beside_ref[...] = rows[16:]

        @pl.when(phase_ref[0] != 0)
        def _():
            beside_ref[...] = rows[:8]

    shapes = [(count, HALF, wide), (16, HALF, wide), (8, HALF, wide)]
    return pl.pallas_call(
        body,
        out_shape=[jax.ShapeDtypeStruct(shape, BF16) for shape in shapes],
        in_specs=[SMEM, SMEM, VMEM, VMEM, ANY],
        out_specs=[VMEM] * 3,
        scratch_shapes=[pltpu.VMEM((2, count, SIDE, 128), F32)],
        compiler_params=params(12),
        name="rows",
    )(section, phase, features, cotangent, after)


def run_image(phase, rows, late, beside):
    def body(phase_ref, rows_ref, late_ref, beside_ref, out_ref):
        kind = phase_ref[0]

        @pl.when(kind == 0)
        def _():
            out_ref[:16] = late_ref[...]
            out_ref[16:] = rows_ref[:16]

        @pl.when(kind == 1)
        def _():
            out_ref[:8] = beside_ref[...]
            out_ref[8:] = rows_ref[...]

        @pl.when(kind == 2)
        def _():
            out_ref[:24] = rows_ref[...]
            out_ref[24:] = beside_ref[...]

        @pl.when(kind == 3)
        def _():
            out_ref[...] = jnp.zeros_like(out_ref)

    return pl.pallas_call(
        body,
        out_shape=jax.ShapeDtypeStruct((SIDE, HALF, 2 * C), BF16),
        in_specs=[SMEM] + [VMEM] * 3,
        out_specs=VMEM,
        compiler_params=params(12),
        name="image",
    )(phase, rows, late, beside)


def run_start(section, image, kernels, turned):
    def body(section_ref, image_ref, own_ref, near_ref, rest_ref, out_ref, left_ref, right_ref, kernel_ref):
        where = section_ref[0]

        @pl.when((where >= 2) if turned else (where < 2))
        def _():
            choose(kernel_ref, where == (3 if turned else 0), section_ref[1], own_ref, near_ref, rest_ref)
            field = image_ref[...].astype(F32)
            field = conv_in_kernel(field, kernel_ref, left_ref, right_ref, turned=turned)
            out_ref[...] = field.astype(out_ref.dtype)

    return pl.pallas_call(
        body,
        out_shape=jax.ShapeDtypeStruct((SIDE, HALF, 2 * C), F32 if turned else BF16),
        in_specs=[SMEM] + [VMEM] * 4,
        out_specs=VMEM,
        scratch_shapes=TAPS + KERNEL,
        compiler_params=params(16),
        name="start_turned" if turned else "start",
    )(section, image, *kernels)


def run_piece(blocks, weight):
    share, depth = weight.shape[0] // N_SEQ, weight.shape[1]

    def body(index_ref, weight_ref, out_ref):
        out_ref[...] = weight_ref[...]

    return pl.pallas_call(
        body,
        grid_spec=pltpu.PrefetchScalarGridSpec(
            num_scalar_prefetch=1,
            grid=(2,),
            in_specs=[pl.BlockSpec((share, depth), lambda i, index: (index[i], 0))],
            out_specs=pl.BlockSpec((share, depth), lambda i, index: (i, 0)),
        ),
        out_shape=jax.ShapeDtypeStruct((2 * share, depth), weight.dtype),
        compiler_params=params(58),
    )(blocks, weight)


def gather_partner(here, piece, kernel, before, across, meanwhile):
    rows, depth = piece.shape
    half, part = depth // 2, depth // 4

    kernel_rows = kernel.shape[0] // 2

    def split(here_ref, piece_ref, kernel_ref, first_ref, second_ref, part_ref):
        first_ref[...] = piece_ref[:, :half]
        second_ref[...] = piece_ref[:, half:]
        start = pl.multiple_of(here_ref[1] * kernel_rows, kernel_rows)
        part_ref[...] = kernel_ref[pl.ds(start, kernel_rows)]

    outs = [((rows, half), BF16)] * 2 + [((kernel_rows, kernel.shape[1]), BF16)]
    first, second, kernel_part = call(split, outs, (piece, kernel), before, (here,))
    got = [flip(first, m) for m in (X1, X1 ^ X3, X3)] + [flip(second, m) for m in (Y1, Y1 ^ Y3, Y3)]
    kernel_part = partner(kernel_part)

    def stack(*refs):
        for side in range(2):
            for far in range(4):
                source = refs[side] if far == 0 else refs[2 + 3 * side + far - 1]
                refs[8 + side][far * rows : (far + 1) * rows] = source[...]

    wide = call(stack, [((4 * rows, half), BF16)] * 2, (first, second, *got), (kernel_part, across))
    kernels = (kernel, kernel_part, flip(kernel_part, CORE))
    rings = ((Y1, Y3), (X1, X3))
    near = [flip(value, ring[0]) for value, ring in zip(wide, rings)]
    far = [flip(value, ring[1]) for value, ring in zip(wide, rings)]
    skip_field, start = meanwhile(wide[0], kernels)

    def cut(*refs):
        for side in range(2):
            refs[4 + 2 * side][...] = refs[side][:, :part]
            refs[5 + 2 * side][...] = refs[2 + side][:, part:]

    outs = [((4 * rows, part), BF16)] * 4
    parts = call(cut, outs, (*far, *near))
    low = [flip(parts[2 * side], ring[0]) for side, ring in enumerate(rings)]
    high = [flip(parts[2 * side + 1], ring[1]) for side, ring in enumerate(rings)]

    def join(*refs):
        out_ref = refs[10]
        for side in range(2):
            base = side * half
            mine, one, three = refs[side], refs[2 + side], refs[4 + side]
            for outer in range(4):
                sources = {0: [mine], 1: [one], 3: [three], 2: [refs[6 + side], refs[8 + side]]}[outer]
                for j, source in enumerate(sources):
                    count = source.shape[1]
                    at = slice(base + j * count, base + (j + 1) * count)
                    for inner in range(4):
                        block = source[inner * rows : (inner + 1) * rows]
                        x, y = (inner, outer) if side == 0 else (outer, inner)
                        start = (4 * x + y) * rows
                        out_ref[start : start + rows, at] = block

    args = (*wide, *near, *far, *low, *high)
    held = call(join, [((16 * rows, depth), BF16)], args, (skip_field,))[0]
    return held, kernels, skip_field, start


def run_forward(section, blocks, skip, own, near, far, codes, kernels):
    width, depth = own.shape
    cols = width // CHUNKS

    def body(
        section_ref, index_ref, skip_ref, own_ref, near_ref, far_ref, one_ref, two_ref, cos_ref,
        sin_ref, own_kernel_ref, near_kernel_ref, rest_kernel_ref, tokens_out, act_out, lift_out, field_ref, sum_ref,
        left_ref, right_ref, kernel_ref, both_ref, sems, tokens_ref,
        act_ref, lift_ref, out_sems,
    ):
        parity = section_ref[0] % 2

        @pl.when(section_ref[0] < 2)
        def _():
            weights = Weights(index_ref, own_ref, near_ref, far_ref, both_ref, sems, parity)
            weights.start()
            choose(kernel_ref, parity == 1, section_ref[1], own_kernel_ref, near_kernel_ref, rest_kernel_ref)
            patch = patchify(skip_ref[...])
            sum_ref[...] = jnp.zeros_like(sum_ref)

            def embed(chunk, rows):
                at = lanes(chunk, cols)
                code = one_ref[:, at][:, None] * cos_ref[:, at][None]
                code += two_ref[:, at][:, None] * sin_ref[:, at][None]
                value = dot_nt(patch, rows) + code.reshape(TOKENS, cols)
                value = value.astype(BF16)
                tokens_ref[:, at] = value
                value = value.astype(F32)
                sum_ref[...] += jnp.sum(value * value, axis=-1, keepdims=True)

            weights.sweep(0, embed, wait=True)
            scale = lax.rsqrt(sum_ref[...] * (1.0 / width) + NORM_EPS)
            lift_ref[...] = jnp.zeros_like(lift_ref)

            def raise_up(chunk, rows):
                at = lanes(chunk, cols)
                active = silu(tokens_ref[:, at].astype(F32) * scale).astype(BF16)
                act_ref[:, at] = active
                lift_ref[...] += dot(active, rows)

            weights.sweep(1, raise_up, wait=True)

            pairs = ((tokens_ref, tokens_out), (act_ref, act_out), (lift_ref, lift_out))
            copies = [
                pltpu.make_async_copy(source, target, out_sems.at[n])
                for n, (source, target) in enumerate(pairs)
            ]
            for copy in copies:
                copy.start()
            field = unpatchify(rounded(silu(lift_ref[...])))
            field_ref[...] = conv_in_kernel(field, kernel_ref, left_ref, right_ref).astype(BF16)
            for copy in copies:
                copy.wait()

    return pl.pallas_call(
        body,
        out_shape=[
            jax.ShapeDtypeStruct((TOKENS, width), BF16),
            jax.ShapeDtypeStruct((TOKENS, width), BF16),
            jax.ShapeDtypeStruct((TOKENS, depth), F32),
            jax.ShapeDtypeStruct((SIDE, HALF, 2 * C), BF16),
        ],
        in_specs=[SMEM, SMEM, VMEM] + [HBM] * 3 + [VMEM] * 7,
        out_specs=[HBM] * 3 + [VMEM],
        scratch_shapes=[pltpu.VMEM((TOKENS, 1), F32)]
        + TAPS
        + KERNEL
        + weight_scratch(width, depth)
        + [
            pltpu.VMEM((TOKENS, width), BF16),
            pltpu.VMEM((TOKENS, width), BF16),
            pltpu.VMEM((TOKENS, depth), F32),
            pltpu.SemaphoreType.DMA((3,)),
        ],
        compiler_params=params(56),
        name="forward_first_pair",
    )(section, blocks, skip, own, near, far, *codes, *kernels)


def run_second_pair(section, blocks, second, skip, start, own, near, far, kernels):
    width, depth = own.shape
    cols = width // CHUNKS

    def body(
        section_ref, index_ref, second_ref, skip_ref, start_ref, own_ref, near_ref, far_ref,
        own_kernel_ref, near_kernel_ref, rest_kernel_ref, back_ref, side_ref, patch_ref, sum_ref, left_ref,
        right_ref, kernel_ref, tokens_ref, inner_ref, lift_ref, both_ref, sems,
    ):
        parity = section_ref[0] % 2

        @pl.when(section_ref[0] >= 2)
        def _():
            weights = Weights(index_ref, own_ref, near_ref, far_ref, both_ref, sems, parity)
            weights.start()
            choose(kernel_ref, parity == 0, section_ref[1], own_kernel_ref, near_kernel_ref, rest_kernel_ref)
            field = rounded(silu(second_ref[...].astype(F32)))
            field = conv_in_kernel(field, kernel_ref, left_ref, right_ref).astype(BF16)
            patch_ref[...] = patchify(field)
            sum_ref[...] = jnp.zeros_like(sum_ref)

            def embed(chunk, rows):
                value = dot_nt(patch_ref[...], rows).astype(BF16)
                tokens_ref[:, lanes(chunk, cols)] = value
                value = value.astype(F32)
                sum_ref[...] += jnp.sum(value * value, axis=-1, keepdims=True)

            weights.sweep(0, embed, wait=True)
            scale = lax.rsqrt(sum_ref[...] * (1.0 / width) + NORM_EPS)
            lift_ref[...] = patchify(skip_ref[...]).astype(F32)

            def raise_up(chunk, rows):
                at = lanes(chunk, cols)
                active = silu(tokens_ref[:, at].astype(F32) * scale).astype(BF16)
                side_ref[:, at] = active
                lift_ref[...] += dot(active, rows)

            weights.sweep(1, raise_up, wait=True)
            last_patch = (patchify(start_ref[...]) * silu_slope(lift_ref[...])).astype(BF16)

            @pl.when(parity == 1)
            def _():
                patch_ref[...] = last_patch

            sum_ref[...] = jnp.zeros_like(sum_ref)

            def descend(chunk, rows):
                at = lanes(chunk, cols)
                normal = tokens_ref[:, at].astype(F32) * scale
                inner = dot_nt(last_patch, rows) * silu_slope(normal)
                inner_ref[:, at] = inner
                sum_ref[...] += jnp.sum(inner * normal, axis=-1, keepdims=True)

            weights.sweep(1, descend)
            mean = sum_ref[...] * (1.0 / width)
            lift_ref[...] = jnp.zeros_like(lift_ref)

            def lower(chunk, rows):
                at = lanes(chunk, cols)
                normal = tokens_ref[:, at].astype(F32) * scale
                back = (scale * (inner_ref[:, at] - normal * mean)).astype(BF16)

                @pl.when(parity == 0)
                def _():
                    side_ref[:, at] = back

                lift_ref[...] += dot(back, rows)

            weights.sweep(0, lower)
            field = unpatchify(rounded(lift_ref[...]))
            field = conv_in_kernel(field, kernel_ref, left_ref, right_ref, turned=True)
            back_ref[...] = (field * silu_slope(second_ref[...].astype(F32))).astype(BF16)

    return pl.pallas_call(
        body,
        out_shape=[
            jax.ShapeDtypeStruct((SIDE, HALF, 2 * C), BF16),
            jax.ShapeDtypeStruct((TOKENS, width), BF16),
            jax.ShapeDtypeStruct((TOKENS, depth), BF16),
        ],
        in_specs=[SMEM, SMEM] + [VMEM] * 3 + [HBM] * 3 + [VMEM] * 3,
        out_specs=[VMEM] * 3,
        scratch_shapes=[pltpu.VMEM((TOKENS, 1), F32)]
        + TAPS
        + KERNEL
        + [
            pltpu.VMEM((TOKENS, width), BF16),
            pltpu.VMEM((TOKENS, width), F32),
            pltpu.VMEM((TOKENS, depth), F32),
        ]
        + weight_scratch(width, depth),
        compiler_params=params(38),
        name="second_pair",
    )(section, blocks, second, skip, start, own, near, far, *kernels)


def run_back(section, given, skip, lift, tokens, prior, patch, near, far, kernels):
    width, depth = tokens.shape[1], lift.shape[1]
    cols = width // CHUNKS

    def body(
        section_ref, given_ref, skip_ref, lift_ref, tokens_ref, prior_ref, known_ref, near_ref,
        far_ref, own_kernel_ref, near_kernel_ref, rest_kernel_ref, keep_ref, send_ref, patch_ref, sum_ref, left_ref,
        right_ref, kernel_ref, inner_ref, both_ref, sems,
    ):
        where = section_ref[0]
        weights = Weights(None, None, near_ref, far_ref, both_ref, sems, 1)

        @pl.when(where == 0)
        def _():
            weights.start(own=False)

        @pl.when(where >= 1)
        def _():
            keep_ref[...] = prior_ref[:, : width // 2]
            send_ref[...] = prior_ref[:, width // 2 :]

        @pl.when(where >= 2)
        def _():
            patch_ref[...] = known_ref[...]

        @pl.when(where < 2)
        def _():
            choose(kernel_ref, where == 1, section_ref[1], own_kernel_ref, near_kernel_ref, rest_kernel_ref)
            field = given_ref[...].astype(F32)
            field = conv_in_kernel(field, kernel_ref, left_ref, right_ref, turned=True)
            patch_ref[...] = (patchify(field) * silu_slope(lift_ref[...])).astype(BF16)

        @pl.when(where == 0)
        def _():
            sum_ref[...] = jnp.zeros_like(sum_ref)

            @pl.loop(0, CHUNKS, unroll=UNROLL)
            def _(chunk):
                value = tokens_ref[:, lanes(chunk, cols)].astype(F32)
                sum_ref[...] += jnp.sum(value * value, axis=-1, keepdims=True)

            scale = lax.rsqrt(sum_ref[...] * (1.0 / width) + NORM_EPS)
            sum_ref[...] = jnp.zeros_like(sum_ref)

            def descend(chunk, rows):
                at = lanes(chunk, cols)
                normal = tokens_ref[:, at].astype(F32) * scale
                inner = dot_nt(patch_ref[...], rows) * silu_slope(normal)
                inner_ref[:, at] = inner
                sum_ref[...] += jnp.sum(inner * normal, axis=-1, keepdims=True)

            weights.sweep(0, descend, wait=True)
            mean = sum_ref[...] * (1.0 / width)

            for first, ref in ((0, keep_ref), (CHUNKS // 2, send_ref)):

                @pl.loop(0, CHUNKS // 2, unroll=UNROLL)
                def _(i, first=first, ref=ref):
                    at = lanes(first + i, cols)
                    normal = tokens_ref[:, at].astype(F32) * scale
                    back = scale * (inner_ref[:, at] - normal * mean)
                    ref[:, lanes(i, cols)] = back.astype(BF16)

            patch_ref[...] = patchify(skip_ref[...])

    return pl.pallas_call(
        body,
        out_shape=[
            jax.ShapeDtypeStruct((TOKENS, width // 2), BF16),
            jax.ShapeDtypeStruct((TOKENS, width // 2), BF16),
            jax.ShapeDtypeStruct((TOKENS, depth), BF16),
        ],
        in_specs=[SMEM] + [VMEM] * 6 + [HBM] * 2 + [VMEM] * 3,
        out_specs=[VMEM] * 3,
        scratch_shapes=[pltpu.VMEM((TOKENS, 1), F32)]
        + TAPS
        + KERNEL
        + [
            pltpu.VMEM((TOKENS, width), F32),
            pltpu.VMEM((1, width, depth), BF16),
            pltpu.SemaphoreType.DMA((1, CHUNKS)),
        ],
        compiler_params=params(30),
        name="back_first_pair",
    )(section, given, skip, lift, tokens, prior, patch, near, far, *kernels)


SENT = {"a": (1, 2), "b": (3, 2)}
KEPT = {"a": (0, 3), "b": (0, 1)}


def run_partial(keep, recv, patch, patch_recv):
    half, depth = keep.shape[1], patch.shape[1]
    part, block = depth // 4, half // 16

    def body(keep_ref, recv_ref, patch_ref, other_ref, *out_refs):
        tokens = jnp.concatenate([keep_ref[...], recv_ref[...]], axis=0)
        patches = jnp.concatenate([patch_ref[...], other_ref[...]], axis=0)
        for column in range(4):
            name = "ab"[column % 2]
            sent_ref, kept_ref = out_refs[column], out_refs[4 + column]
            right = patches[:, column * part : (column + 1) * part]
            for i in range(2):
                for ref, far in ((sent_ref, SENT[name][i]), (kept_ref, KEPT[name][i])):
                    if column < 2:
                        left = tokens[:, far * 4 * block : (far + 1) * 4 * block]
                    else:
                        left = jnp.concatenate(
                            [tokens[:, (4 * j + far) * block :][:, :block] for j in range(4)], axis=1
                        )
                    ref[i] = dot_tn(left, right).astype(ref.dtype)

    shape = (2, 4 * block, part)
    outs = call(body, [(shape, BF16)] * 4 + [(shape, F32)] * 4, (keep, recv, patch, patch_recv))
    return outs[:4], outs[4:]


FIRST_RINGS = ((X1, X3), (X3, X1), (Y1, Y3), (Y3, Y1))


def run_sum(partial):
    sent, kept = partial
    got = [flip(value, ring[0]) for value, ring in zip(sent, FIRST_RINGS)]
    rows, part = kept[0].shape[1:]
    block = rows // 4

    def add_once(*refs):
        kept_refs, got_refs, sent_refs, out_refs = refs[:4], refs[4:8], refs[8:12], refs[12:]
        for kept_ref, got_ref, sent_ref, out_ref in zip(kept_refs, got_refs, sent_refs, out_refs):
            total = kept_ref[...] + got_ref[...].astype(F32)
            out_ref[...] = total[0]
            sent_ref[...] = total[1].astype(BF16)

    shape = (rows, part)
    outs = call(add_once, [(shape, BF16)] * 4 + [(shape, F32)] * 4, (*kept, *got))
    got = [flip(value, ring[1]) for value, ring in zip(outs[:4], FIRST_RINGS)]

    def add_twice(*refs):
        kept_refs, got_refs, out_refs = refs[:4], refs[4:8], refs[8:]
        for half in range(2):
            a, b = 2 * half, 2 * half + 1
            total = [kept_refs[i][...] + got_refs[i][...].astype(F32) for i in (a, b)]
            total = jnp.concatenate(total, axis=1)
            for far in range(4):
                ref = out_refs[4 * half + far]
                ref[...] = total[far * block : (far + 1) * block].astype(ref.dtype)

    shape = (block, 2 * part)
    kinds = [F32, BF16, BF16, BF16] * 2
    outs = call(add_twice, [(shape, kind) for kind in kinds], (*outs[4:], *got))
    got = [flip(v, m) for v, m in zip(outs[1:4], (Y1, Y1 ^ Y3, Y3))]
    got += [flip(v, m) for v, m in zip(outs[5:8], (X1, X1 ^ X3, X3))]

    def add_last(*refs):
        for half in range(2):
            total = refs[half][...]
            for ref in refs[2 + 3 * half : 5 + 3 * half]:
                total += ref[...].astype(F32)
            at = slice(half * 2 * part, (half + 1) * 2 * part)
            refs[8][:, at] = total[: block // 2]
            refs[9][:, at] = total[block // 2 :].astype(BF16)

    shape = (block // 2, 4 * part)
    mine, away = call(add_last, [(shape, F32), (shape, BF16)], (outs[0], outs[4], *got))
    return mine + flip(away, ZH).astype(F32)


def on_device(features, conv_kernels, patch_weights, positions, out_cotangent):
    weight = patch_weights[0]
    width, depth = weight.shape
    kernel = conv_kernels[0].reshape(9 * C, C)
    section = lax.axis_index("section")
    place = lax.axis_index(SEQ)
    first_pair = section < 2

    order = jnp.arange(N_SEQ, dtype=jnp.int32)
    away = ((order & 1) << 5) | (((order >> 3) & 3) << 3) | (((order >> 1) & 3) << 1) | (order >> 5)
    blocks = away ^ place

    here, phase = jnp.stack([section, place % 2]), (place % 4).reshape(1)
    piece = partner(run_piece(blocks, weight))
    across = hop(out_cotangent)

    image_id = jnp.minimum(3 * (place // 4) + place % 4, positions.shape[0] - 1)
    begin = positions[image_id]
    half = width // 2
    feature = (blocks[:, None] * (width // N_SEQ) + jnp.arange(width // N_SEQ)[None, :]).reshape(-1)
    rates = jnp.exp((feature % half).astype(F32) * (-math.log(10000.0) / half))
    is_sin = (feature < half)[None, :]
    steps = jnp.arange(HALF, dtype=jnp.int32)
    row_angle = (begin + HALF * steps).astype(F32)[:, None] * rates[None, :]
    col_angle = steps.astype(F32)[:, None] * rates[None, :]
    row_sin, row_cos = jnp.sin(row_angle), jnp.cos(row_angle)
    row_one = jnp.where(is_sin, row_sin, row_cos)
    row_two = jnp.where(is_sin, row_cos, -row_sin)
    col_cos, col_sin = jnp.cos(col_angle), jnp.sin(col_angle)

    codes = (row_one, row_two, col_cos, col_sin)

    def first_convolutions(after, kernels):
        rows, late, beside = run_rows(here, phase, features, across, after)
        image = run_image(phase, rows, beside_swap(late), flip(beside, CORE))
        return [run_start(here, image, kernels, turned=turned) for turned in (False, True)]

    near, kernels, skip_field, start = gather_partner(
        here, piece, kernel, codes, across, first_convolutions
    )
    far = flip(near, CORE)
    skip_recv = hop(skip_field)

    tokens, active, first_lift, second_field = run_forward(
        here, blocks, skip_field, weight, near, far, codes, kernels
    )
    second_back, side, patch = run_second_pair(
        here, blocks, hop(second_field), skip_recv, start, weight, near, far, kernels
    )
    prior = jnp.where(first_pair, active, side)
    keep, send, patch = run_back(
        here, hop(second_back), skip_field, first_lift, tokens, prior, patch, near, far,
        kernels,
    )

    summed = run_sum(run_partial(keep, flip(send, CORE), patch, flip(patch, CORE)))
    tokens_in_all = positions.shape[0] * HALF * HALF
    return (summed * (1.0 / math.sqrt(tokens_in_all)))[None]


def solution(mesh):
    in_specs = (
        P("seq", None, None),
        P("section", None, None, None, None),
        P("section", None, None),
        P(),
        P("seq", None, None),
    )
    out_specs = P("section", "seq", None)
    return jax.shard_map(
        on_device, mesh=mesh, in_specs=in_specs, out_specs=out_specs, check_vma=False
    )
```

```python
import math

import jax
import jax.numpy as jnp
from jax import lax
from jax.experimental import pallas as pl
from jax.experimental.pallas import tpu as pltpu
from jax.sharding import PartitionSpec as P

NORM_EPS = 1e-05
BF16 = jnp.bfloat16
F32 = jnp.float32
SIDE = 32
HALF = SIDE // 2
C = 256
N_SEQ = 64
SEQ = "seq"

X1, X3, Y1, Y3, CORE, ZH = (1 << 3, 3 << 3, 1 << 1, 3 << 1, 1, 1 << 5)


def flip(value, mask):
    return lax.ppermute(value, SEQ, [(i, i ^ mask) for i in range(N_SEQ)])


def partner(value):
    return lax.ppermute(value, "section", [(0, 1), (1, 0), (2, 3), (3, 2)])


HOPS = [(1 * N_SEQ + q, 2 * N_SEQ + q) for q in range(N_SEQ)]
HOPS += [(q, 3 * N_SEQ + (q ^ ZH)) for q in range(N_SEQ)]
HOPS += [(j, i) for i, j in HOPS]


def hop(value):
    return lax.ppermute(value, ("section", SEQ), HOPS)


def beside_swap(value):
    pairs = [((2 * k - 1) % N_SEQ, 2 * k) for k in range(N_SEQ // 2)]
    return lax.ppermute(value, SEQ, pairs + [(j, i) for i, j in pairs])


def dot(left, right):
    return jnp.dot(left, right, preferred_element_type=F32)


def dot_nt(left, right):
    return lax.dot_general(left, right, (((1,), (1,)), ((), ())), preferred_element_type=F32)


def dot_tn(left, right):
    return lax.dot_general(left, right, (((0,), (0,)), ((), ())), preferred_element_type=F32)


def patchify(field):
    pairs = field.reshape(HALF, 2, HALF, 2 * C)
    return jnp.concatenate([pairs[:, 0], pairs[:, 1]], axis=-1).reshape(HALF * HALF, 4 * C)


def unpatchify(tokens):
    pairs = tokens.reshape(HALF, HALF, 4 * C)
    return jnp.stack([pairs[..., : 2 * C], pairs[..., 2 * C :]], axis=1).reshape(SIDE, HALF, 2 * C)


def silu(value):
    half = 0.5 * value
    return half + half * jnp.tanh(half)


def silu_slope(value):
    half = 0.5 * value
    t = jnp.tanh(half)
    return (0.5 + 0.5 * t) * (1.0 + half * (1.0 - t))


CHUNKS = 4
UNROLL = 4
VMEM = pl.BlockSpec(memory_space=pltpu.VMEM)
SMEM = pl.BlockSpec(memory_space=pltpu.SMEM)
ANY = pl.BlockSpec(memory_space=pl.ANY)
HBM = pl.BlockSpec(memory_space=pltpu.HBM)


def conv_in_kernel(field, kernel_ref, left_ref, right_ref, turned=False):
    even, odd = field[..., :C], field[..., C:]
    column = lax.broadcasted_iota(jnp.int32, (SIDE, HALF, C), 1)
    before = jnp.where(column == 0, 0.0, pltpu.roll(odd, 1, 1))
    after = jnp.where(column == HALF - 1, 0.0, pltpu.roll(even, HALF - 1, 1))
    middle = field.astype(BF16)
    left_ref[1 : SIDE + 1, :, C:] = middle
    left_ref[1 : SIDE + 1, :, :C] = before.astype(BF16)
    right_ref[1 : SIDE + 1, :, : 2 * C] = middle
    right_ref[1 : SIDE + 1, :, 2 * C :] = after.astype(BF16)
    out = []
    for ref in (left_ref, right_ref):
        edge = jnp.zeros((HALF, 3 * C), BF16)
        ref[0] = edge
        ref[SIDE + 1] = edge
        total = None
        for row in range(3):
            taps = ref[row : row + SIDE].reshape(SIDE * HALF, 3 * C)
            if turned:
                for column in range(3):
                    tap = (2 - row) * 3 + 2 - column
                    weight = kernel_ref[tap * C : (tap + 1) * C]
                    term = dot_nt(taps[:, column * C : (column + 1) * C], weight)
                    total = term if total is None else total + term
            else:
                term = dot(taps, kernel_ref[row * 3 * C : (row + 1) * 3 * C])
                total = term if total is None else total + term
        out.append(total.reshape(SIDE, HALF, C))
    return jnp.concatenate(out, axis=-1)


def choose(to_ref, mine, core, own_ref, near_ref, rest_ref):
    half = near_ref.shape[0]

    @pl.when(mine)
    def _():
        to_ref[...] = own_ref[...]

    @pl.when(jnp.logical_not(mine))
    def _():
        to_ref[pl.ds(pl.multiple_of(core * half, half), half)] = near_ref[...]
        to_ref[pl.ds(pl.multiple_of((1 - core) * half, half), half)] = rest_ref[...]


def rounded(value):
    return value.astype(BF16).astype(F32)


class Weights:
    def __init__(self, index_ref, own_ref, near_ref, far_ref, both_ref, sems, parity):
        self.args = (index_ref, own_ref, near_ref, far_ref, both_ref, sems, parity)
        self.rows = both_ref.shape[1] // CHUNKS
        self.share = both_ref.shape[1] // N_SEQ

    def start(self, own=True):
        index_ref, own_ref, near_ref, far_ref, both_ref, sems, parity = self.args
        per = N_SEQ // CHUNKS
        for block in range(N_SEQ if own else 0):
            source = pl.multiple_of(index_ref[block] * self.share, self.share)
            pltpu.make_async_copy(
                own_ref.at[pl.ds(source, self.share)],
                both_ref.at[parity, pl.ds(block * self.share, self.share)],
                sems.at[parity, block // per],
            ).start()
        for chunk in range(CHUNKS):
            source = near_ref if chunk < CHUNKS // 2 else far_ref
            pltpu.make_async_copy(
                source.at[pl.ds(chunk % (CHUNKS // 2) * self.rows, self.rows)],
                both_ref.at[1 - parity, pl.ds(chunk * self.rows, self.rows)],
                sems.at[1 - parity, chunk],
            ).start()

    def sweep(self, slot, step, wait=False):
        _, _, near_ref, _, both_ref, sems, _ = self.args

        @pl.loop(0, CHUNKS, unroll=UNROLL)
        def _(chunk):
            rows = pl.ds(pl.multiple_of(chunk * self.rows, self.rows), self.rows)
            if wait:
                pltpu.make_async_copy(
                    near_ref.at[pl.ds(0, self.rows)], both_ref.at[slot, rows], sems.at[slot, chunk]
                ).wait()
            step(chunk, both_ref[slot, rows])


def weight_scratch(width, depth):
    return [pltpu.VMEM((2, width, depth), BF16), pltpu.SemaphoreType.DMA((2, CHUNKS))]


def lanes(chunk, count):
    return pl.ds(pl.multiple_of(chunk * count, count), count)


TAPS = [pltpu.VMEM((SIDE + 2, HALF, 3 * C), BF16)] * 2
TOKENS = HALF * HALF
KERNEL = [pltpu.VMEM((9 * C, C), BF16)]


def params(mib):
    return pltpu.CompilerParams(vmem_limit_bytes=mib * 1024 * 1024)


def call(body, outs, args, after=(), scalars=()):
    count = len(scalars) + len(args)

    def with_after(*refs):
        body(*refs[:count], *refs[count + len(after) :])

    return pl.pallas_call(
        with_after,
        out_shape=[jax.ShapeDtypeStruct(shape, kind) for shape, kind in outs],
        in_specs=[SMEM] * len(scalars) + [VMEM] * len(args) + [ANY] * len(after),
        out_specs=[VMEM] * len(outs),
        compiler_params=params(20),
    )(*scalars, *args, *after)


def run_rows(section, phase, features, cotangent, after):
    count = features.shape[0]
    wide = 2 * C

    def body(section_ref, phase_ref, features_ref, cotangent_ref, _, rows_ref, late_ref, beside_ref, value_ref):
        for part in range(2):
            at = slice(part * 128, (part + 1) * 128)

            @pl.when(section_ref[0] < 2)
            def _(part=part, at=at):
                value_ref[part] = features_ref[:, :, at].astype(F32)

            @pl.when(section_ref[0] >= 2)
            def _(part=part, at=at):
                value_ref[part] = cotangent_ref[:, :, at].astype(F32)

        quarters = [
            value_ref[part, :, pl.ds(column, HALF, stride=2), :]
            for column in range(2)
            for part in range(2)
        ]
        rows = jnp.concatenate(quarters, axis=-1).astype(BF16)
        rows_ref[...] = rows
        late_ref[...] = rows[8:]

        @pl.when(phase_ref[0] == 0)
        def _():
            beside_ref[...] = rows[16:]

        @pl.when(phase_ref[0] != 0)
        def _():
            beside_ref[...] = rows[:8]

    shapes = [(count, HALF, wide), (16, HALF, wide), (8, HALF, wide)]
    return pl.pallas_call(
        body,
        out_shape=[jax.ShapeDtypeStruct(shape, BF16) for shape in shapes],
        in_specs=[SMEM, SMEM, VMEM, VMEM, ANY],
        out_specs=[VMEM] * 3,
        scratch_shapes=[pltpu.VMEM((2, count, SIDE, 128), F32)],
        compiler_params=params(12),
        name="rows",
    )(section, phase, features, cotangent, after)


def run_image(phase, rows, late, beside):
    def body(phase_ref, rows_ref, late_ref, beside_ref, out_ref):
        kind = phase_ref[0]

        @pl.when(kind == 0)
        def _():
            out_ref[:16] = late_ref[...]
            out_ref[16:] = rows_ref[:16]

        @pl.when(kind == 1)
        def _():
            out_ref[:8] = beside_ref[...]
            out_ref[8:] = rows_ref[...]

        @pl.when(kind == 2)
        def _():
            out_ref[:24] = rows_ref[...]
            out_ref[24:] = beside_ref[...]

        @pl.when(kind == 3)
        def _():
            out_ref[...] = jnp.zeros_like(out_ref)

    return pl.pallas_call(
        body,
        out_shape=jax.ShapeDtypeStruct((SIDE, HALF, 2 * C), BF16),
        in_specs=[SMEM] + [VMEM] * 3,
        out_specs=VMEM,
        compiler_params=params(12),
        name="image",
    )(phase, rows, late, beside)


def run_start(section, image, kernels, turned):
    def body(section_ref, image_ref, own_ref, near_ref, rest_ref, out_ref, left_ref, right_ref, kernel_ref):
        where = section_ref[0]

        @pl.when((where >= 2) if turned else (where < 2))
        def _():
            choose(kernel_ref, where == (3 if turned else 0), section_ref[1], own_ref, near_ref, rest_ref)
            field = image_ref[...].astype(F32)
            field = conv_in_kernel(field, kernel_ref, left_ref, right_ref, turned=turned)
            out_ref[...] = field.astype(out_ref.dtype)

    return pl.pallas_call(
        body,
        out_shape=jax.ShapeDtypeStruct((SIDE, HALF, 2 * C), F32 if turned else BF16),
        in_specs=[SMEM] + [VMEM] * 4,
        out_specs=VMEM,
        scratch_shapes=TAPS + KERNEL,
        compiler_params=params(16),
        name="start_turned" if turned else "start",
    )(section, image, *kernels)


def run_piece(blocks, weight):
    share, depth = weight.shape[0] // N_SEQ, weight.shape[1]

    def body(index_ref, weight_ref, out_ref):
        out_ref[...] = weight_ref[...]

    return pl.pallas_call(
        body,
        grid_spec=pltpu.PrefetchScalarGridSpec(
            num_scalar_prefetch=1,
            grid=(2,),
            in_specs=[pl.BlockSpec((share, depth), lambda i, index: (index[i], 0))],
            out_specs=pl.BlockSpec((share, depth), lambda i, index: (i, 0)),
        ),
        out_shape=jax.ShapeDtypeStruct((2 * share, depth), weight.dtype),
        compiler_params=params(58),
    )(blocks, weight)


def gather_partner(here, piece, kernel, before, across, meanwhile):
    rows, depth = piece.shape
    half, part = depth // 2, depth // 4

    kernel_rows = kernel.shape[0] // 2

    def split(here_ref, piece_ref, kernel_ref, first_ref, second_ref, part_ref):
        first_ref[...] = piece_ref[:, :half]
        second_ref[...] = piece_ref[:, half:]
        start = pl.multiple_of(here_ref[1] * kernel_rows, kernel_rows)
        part_ref[...] = kernel_ref[pl.ds(start, kernel_rows)]

    outs = [((rows, half), BF16)] * 2 + [((kernel_rows, kernel.shape[1]), BF16)]
    first, second, kernel_part = call(split, outs, (piece, kernel), before, (here,))
    got = [flip(first, m) for m in (X1, X1 ^ X3, X3)] + [flip(second, m) for m in (Y1, Y1 ^ Y3, Y3)]
    kernel_part = partner(kernel_part)

    def stack(*refs):
        for side in range(2):
            for far in range(4):
                source = refs[side] if far == 0 else refs[2 + 3 * side + far - 1]
                refs[8 + side][far * rows : (far + 1) * rows] = source[...]

    wide = call(stack, [((4 * rows, half), BF16)] * 2, (first, second, *got), (kernel_part, across))
    kernels = (kernel, kernel_part, flip(kernel_part, CORE))
    rings = ((Y1, Y3), (X1, X3))
    near = [flip(value, ring[0]) for value, ring in zip(wide, rings)]
    far = [flip(value, ring[1]) for value, ring in zip(wide, rings)]
    skip_field, start = meanwhile(wide[0], kernels)

    def cut(*refs):
        for side in range(2):
            refs[4 + 2 * side][...] = refs[side][:, :part]
            refs[5 + 2 * side][...] = refs[2 + side][:, part:]

    outs = [((4 * rows, part), BF16)] * 4
    parts = call(cut, outs, (*far, *near))
    low = [flip(parts[2 * side], ring[0]) for side, ring in enumerate(rings)]
    high = [flip(parts[2 * side + 1], ring[1]) for side, ring in enumerate(rings)]

    def join(*refs):
        out_ref = refs[10]
        for side in range(2):
            base = side * half
            mine, one, three = refs[side], refs[2 + side], refs[4 + side]
            for outer in range(4):
                sources = {0: [mine], 1: [one], 3: [three], 2: [refs[6 + side], refs[8 + side]]}[outer]
                for j, source in enumerate(sources):
                    count = source.shape[1]
                    at = slice(base + j * count, base + (j + 1) * count)
                    for inner in range(4):
                        block = source[inner * rows : (inner + 1) * rows]
                        x, y = (inner, outer) if side == 0 else (outer, inner)
                        start = (4 * x + y) * rows
                        out_ref[start : start + rows, at] = block

    args = (*wide, *near, *far, *low, *high)
    held = call(join, [((16 * rows, depth), BF16)], args, (skip_field,))[0]
    return held, kernels, skip_field, start


def run_forward(section, blocks, skip, own, near, far, codes, kernels):
    width, depth = own.shape
    cols = width // CHUNKS

    def body(
        section_ref, index_ref, skip_ref, own_ref, near_ref, far_ref, one_ref, two_ref, cos_ref,
        sin_ref, own_kernel_ref, near_kernel_ref, rest_kernel_ref, tokens_out, act_out, lift_out, field_ref, sum_ref,
        left_ref, right_ref, kernel_ref, both_ref, sems, tokens_ref,
        act_ref, lift_ref, out_sems,
    ):
        parity = section_ref[0] % 2

        @pl.when(section_ref[0] < 2)
        def _():
            weights = Weights(index_ref, own_ref, near_ref, far_ref, both_ref, sems, parity)
            weights.start()
            choose(kernel_ref, parity == 1, section_ref[1], own_kernel_ref, near_kernel_ref, rest_kernel_ref)
            patch = patchify(skip_ref[...])
            sum_ref[...] = jnp.zeros_like(sum_ref)

            def embed(chunk, rows):
                at = lanes(chunk, cols)
                code = one_ref[:, at][:, None] * cos_ref[:, at][None]
                code += two_ref[:, at][:, None] * sin_ref[:, at][None]
                value = dot_nt(patch, rows) + code.reshape(TOKENS, cols)
                value = value.astype(BF16)
                tokens_ref[:, at] = value
                value = value.astype(F32)
                sum_ref[...] += jnp.sum(value * value, axis=-1, keepdims=True)

            weights.sweep(0, embed, wait=True)
            scale = lax.rsqrt(sum_ref[...] * (1.0 / width) + NORM_EPS)
            lift_ref[...] = jnp.zeros_like(lift_ref)

            def raise_up(chunk, rows):
                at = lanes(chunk, cols)
                active = silu(tokens_ref[:, at].astype(F32) * scale).astype(BF16)
                act_ref[:, at] = active
                lift_ref[...] += dot(active, rows)

            weights.sweep(1, raise_up, wait=True)

            pairs = ((tokens_ref, tokens_out), (act_ref, act_out), (lift_ref, lift_out))
            copies = [
                pltpu.make_async_copy(source, target, out_sems.at[n])
                for n, (source, target) in enumerate(pairs)
            ]
            for copy in copies:
                copy.start()
            field = unpatchify(rounded(silu(lift_ref[...])))
            field_ref[...] = conv_in_kernel(field, kernel_ref, left_ref, right_ref).astype(BF16)
            for copy in copies:
                copy.wait()

    return pl.pallas_call(
        body,
        out_shape=[
            jax.ShapeDtypeStruct((TOKENS, width), BF16),
            jax.ShapeDtypeStruct((TOKENS, width), BF16),
            jax.ShapeDtypeStruct((TOKENS, depth), F32),
            jax.ShapeDtypeStruct((SIDE, HALF, 2 * C), BF16),
        ],
        in_specs=[SMEM, SMEM, VMEM] + [ANY] * 3 + [VMEM] * 7,
        out_specs=[HBM] * 3 + [VMEM],
        scratch_shapes=[pltpu.VMEM((TOKENS, 1), F32)]
        + TAPS
        + KERNEL
        + weight_scratch(width, depth)
        + [
            pltpu.VMEM((TOKENS, width), BF16),
            pltpu.VMEM((TOKENS, width), BF16),
            pltpu.VMEM((TOKENS, depth), F32),
            pltpu.SemaphoreType.DMA((3,)),
        ],
        compiler_params=params(34),
        name="forward_first_pair",
    )(section, blocks, skip, own, near, far, *codes, *kernels)


def run_second_pair(section, blocks, second, skip, start, own, near, far, kernels):
    width, depth = own.shape
    cols = width // CHUNKS

    def body(
        section_ref, index_ref, second_ref, skip_ref, start_ref, own_ref, near_ref, far_ref,
        own_kernel_ref, near_kernel_ref, rest_kernel_ref, back_ref, side_ref, patch_ref, sum_ref, left_ref,
        right_ref, kernel_ref, tokens_ref, inner_ref, lift_ref, both_ref, sems,
    ):
        parity = section_ref[0] % 2

        @pl.when(section_ref[0] >= 2)
        def _():
            weights = Weights(index_ref, own_ref, near_ref, far_ref, both_ref, sems, parity)
            weights.start()
            choose(kernel_ref, parity == 0, section_ref[1], own_kernel_ref, near_kernel_ref, rest_kernel_ref)
            field = rounded(silu(second_ref[...].astype(F32)))
            field = conv_in_kernel(field, kernel_ref, left_ref, right_ref).astype(BF16)
            patch_ref[...] = patchify(field)
            sum_ref[...] = jnp.zeros_like(sum_ref)

            def embed(chunk, rows):
                value = dot_nt(patch_ref[...], rows).astype(BF16)
                tokens_ref[:, lanes(chunk, cols)] = value
                value = value.astype(F32)
                sum_ref[...] += jnp.sum(value * value, axis=-1, keepdims=True)

            weights.sweep(0, embed, wait=True)
            scale = lax.rsqrt(sum_ref[...] * (1.0 / width) + NORM_EPS)
            lift_ref[...] = patchify(skip_ref[...]).astype(F32)

            def raise_up(chunk, rows):
                at = lanes(chunk, cols)
                active = silu(tokens_ref[:, at].astype(F32) * scale).astype(BF16)
                side_ref[:, at] = active
                lift_ref[...] += dot(active, rows)

            weights.sweep(1, raise_up, wait=True)
            last_patch = (patchify(start_ref[...]) * silu_slope(lift_ref[...])).astype(BF16)

            @pl.when(parity == 1)
            def _():
                patch_ref[...] = last_patch

            sum_ref[...] = jnp.zeros_like(sum_ref)

            def descend(chunk, rows):
                at = lanes(chunk, cols)
                normal = tokens_ref[:, at].astype(F32) * scale
                inner = dot_nt(last_patch, rows) * silu_slope(normal)
                inner_ref[:, at] = inner
                sum_ref[...] += jnp.sum(inner * normal, axis=-1, keepdims=True)

            weights.sweep(1, descend)
            mean = sum_ref[...] * (1.0 / width)
            lift_ref[...] = jnp.zeros_like(lift_ref)

            def lower(chunk, rows):
                at = lanes(chunk, cols)
                normal = tokens_ref[:, at].astype(F32) * scale
                back = (scale * (inner_ref[:, at] - normal * mean)).astype(BF16)

                @pl.when(parity == 0)
                def _():
                    side_ref[:, at] = back

                lift_ref[...] += dot(back, rows)

            weights.sweep(0, lower)
            field = unpatchify(rounded(lift_ref[...]))
            field = conv_in_kernel(field, kernel_ref, left_ref, right_ref, turned=True)
            back_ref[...] = (field * silu_slope(second_ref[...].astype(F32))).astype(BF16)

    return pl.pallas_call(
        body,
        out_shape=[
            jax.ShapeDtypeStruct((SIDE, HALF, 2 * C), BF16),
            jax.ShapeDtypeStruct((TOKENS, width), BF16),
            jax.ShapeDtypeStruct((TOKENS, depth), BF16),
        ],
        in_specs=[SMEM, SMEM] + [VMEM] * 3 + [ANY] * 3 + [VMEM] * 3,
        out_specs=[VMEM] * 3,
        scratch_shapes=[pltpu.VMEM((TOKENS, 1), F32)]
        + TAPS
        + KERNEL
        + [
            pltpu.VMEM((TOKENS, width), BF16),
            pltpu.VMEM((TOKENS, width), F32),
            pltpu.VMEM((TOKENS, depth), F32),
        ]
        + weight_scratch(width, depth),
        compiler_params=params(38),
        name="second_pair",
    )(section, blocks, second, skip, start, own, near, far, *kernels)


def run_back(section, given, skip, lift, tokens, prior, patch, near, far, kernels):
    width, depth = tokens.shape[1], lift.shape[1]
    cols = width // CHUNKS

    def body(
        section_ref, given_ref, skip_ref, lift_ref, tokens_ref, prior_ref, known_ref, near_ref,
        far_ref, own_kernel_ref, near_kernel_ref, rest_kernel_ref, keep_ref, send_ref, patch_ref, sum_ref, left_ref,
        right_ref, kernel_ref, inner_ref, both_ref, sems,
    ):
        where = section_ref[0]
        weights = Weights(None, None, near_ref, far_ref, both_ref, sems, 1)

        @pl.when(where == 0)
        def _():
            weights.start(own=False)

        @pl.when(where >= 1)
        def _():
            keep_ref[...] = prior_ref[:, : width // 2]
            send_ref[...] = prior_ref[:, width // 2 :]

        @pl.when(where >= 2)
        def _():
            patch_ref[...] = known_ref[...]

        @pl.when(where < 2)
        def _():
            choose(kernel_ref, where == 1, section_ref[1], own_kernel_ref, near_kernel_ref, rest_kernel_ref)
            field = given_ref[...].astype(F32)
            field = conv_in_kernel(field, kernel_ref, left_ref, right_ref, turned=True)
            patch_ref[...] = (patchify(field) * silu_slope(lift_ref[...])).astype(BF16)

        @pl.when(where == 0)
        def _():
            sum_ref[...] = jnp.zeros_like(sum_ref)

            @pl.loop(0, CHUNKS, unroll=UNROLL)
            def _(chunk):
                value = tokens_ref[:, lanes(chunk, cols)].astype(F32)
                sum_ref[...] += jnp.sum(value * value, axis=-1, keepdims=True)

            scale = lax.rsqrt(sum_ref[...] * (1.0 / width) + NORM_EPS)
            sum_ref[...] = jnp.zeros_like(sum_ref)

            def descend(chunk, rows):
                at = lanes(chunk, cols)
                normal = tokens_ref[:, at].astype(F32) * scale
                inner = dot_nt(patch_ref[...], rows) * silu_slope(normal)
                inner_ref[:, at] = inner
                sum_ref[...] += jnp.sum(inner * normal, axis=-1, keepdims=True)

            weights.sweep(0, descend, wait=True)
            mean = sum_ref[...] * (1.0 / width)

            for first, ref in ((0, keep_ref), (CHUNKS // 2, send_ref)):

                @pl.loop(0, CHUNKS // 2, unroll=UNROLL)
                def _(i, first=first, ref=ref):
                    at = lanes(first + i, cols)
                    normal = tokens_ref[:, at].astype(F32) * scale
                    back = scale * (inner_ref[:, at] - normal * mean)
                    ref[:, lanes(i, cols)] = back.astype(BF16)

            patch_ref[...] = patchify(skip_ref[...])

    return pl.pallas_call(
        body,
        out_shape=[
            jax.ShapeDtypeStruct((TOKENS, width // 2), BF16),
            jax.ShapeDtypeStruct((TOKENS, width // 2), BF16),
            jax.ShapeDtypeStruct((TOKENS, depth), BF16),
        ],
        in_specs=[SMEM] + [VMEM] * 6 + [ANY] * 2 + [VMEM] * 3,
        out_specs=[VMEM] * 3,
        scratch_shapes=[pltpu.VMEM((TOKENS, 1), F32)]
        + TAPS
        + KERNEL
        + [
            pltpu.VMEM((TOKENS, width), F32),
            pltpu.VMEM((1, width, depth), BF16),
            pltpu.SemaphoreType.DMA((1, CHUNKS)),
        ],
        compiler_params=params(30),
        name="back_first_pair",
    )(section, given, skip, lift, tokens, prior, patch, near, far, *kernels)


SENT = {"a": (1, 2), "b": (3, 2)}
KEPT = {"a": (0, 3), "b": (0, 1)}


def run_partial(keep, recv, patch, patch_recv):
    half, depth = keep.shape[1], patch.shape[1]
    part, block = depth // 4, half // 16

    def body(keep_ref, recv_ref, patch_ref, other_ref, *out_refs):
        tokens = jnp.concatenate([keep_ref[...], recv_ref[...]], axis=0)
        patches = jnp.concatenate([patch_ref[...], other_ref[...]], axis=0)
        for column in range(4):
            name = "ab"[column % 2]
            sent_ref, kept_ref = out_refs[column], out_refs[4 + column]
            right = patches[:, column * part : (column + 1) * part]
            for i in range(2):
                for ref, far in ((sent_ref, SENT[name][i]), (kept_ref, KEPT[name][i])):
                    if column < 2:
                        left = tokens[:, far * 4 * block : (far + 1) * 4 * block]
                    else:
                        left = jnp.concatenate(
                            [tokens[:, (4 * j + far) * block :][:, :block] for j in range(4)], axis=1
                        )
                    ref[i] = dot_tn(left, right).astype(ref.dtype)

    shape = (2, 4 * block, part)
    outs = call(body, [(shape, BF16)] * 4 + [(shape, F32)] * 4, (keep, recv, patch, patch_recv))
    return outs[:4], outs[4:]


FIRST_RINGS = ((X1, X3), (X3, X1), (Y1, Y3), (Y3, Y1))


def run_sum(partial):
    sent, kept = partial
    got = [flip(value, ring[0]) for value, ring in zip(sent, FIRST_RINGS)]
    rows, part = kept[0].shape[1:]
    block = rows // 4

    def add_once(*refs):
        kept_refs, got_refs, sent_refs, out_refs = refs[:4], refs[4:8], refs[8:12], refs[12:]
        for kept_ref, got_ref, sent_ref, out_ref in zip(kept_refs, got_refs, sent_refs, out_refs):
            total = kept_ref[...] + got_ref[...].astype(F32)
            out_ref[...] = total[0]
            sent_ref[...] = total[1].astype(BF16)

    shape = (rows, part)
    outs = call(add_once, [(shape, BF16)] * 4 + [(shape, F32)] * 4, (*kept, *got))
    got = [flip(value, ring[1]) for value, ring in zip(outs[:4], FIRST_RINGS)]

    def add_twice(*refs):
        kept_refs, got_refs, out_refs = refs[:4], refs[4:8], refs[8:]
        for half in range(2):
            a, b = 2 * half, 2 * half + 1
            total = [kept_refs[i][...] + got_refs[i][...].astype(F32) for i in (a, b)]
            total = jnp.concatenate(total, axis=1)
            for far in range(4):
                ref = out_refs[4 * half + far]
                ref[...] = total[far * block : (far + 1) * block].astype(ref.dtype)

    shape = (block, 2 * part)
    kinds = [F32, BF16, BF16, BF16] * 2
    outs = call(add_twice, [(shape, kind) for kind in kinds], (*outs[4:], *got))
    got = [flip(v, m) for v, m in zip(outs[1:4], (Y1, Y1 ^ Y3, Y3))]
    got += [flip(v, m) for v, m in zip(outs[5:8], (X1, X1 ^ X3, X3))]

    def add_last(*refs):
        for half in range(2):
            total = refs[half][...]
            for ref in refs[2 + 3 * half : 5 + 3 * half]:
                total += ref[...].astype(F32)
            at = slice(half * 2 * part, (half + 1) * 2 * part)
            refs[8][:, at] = total[: block // 2]
            refs[9][:, at] = total[block // 2 :].astype(BF16)

    shape = (block // 2, 4 * part)
    mine, away = call(add_last, [(shape, F32), (shape, BF16)], (outs[0], outs[4], *got))
    return mine + flip(away, ZH).astype(F32)


def on_device(features, conv_kernels, patch_weights, positions, out_cotangent):
    weight = patch_weights[0]
    width, depth = weight.shape
    kernel = conv_kernels[0].reshape(9 * C, C)
    section = lax.axis_index("section")
    place = lax.axis_index(SEQ)
    first_pair = section < 2

    order = jnp.arange(N_SEQ, dtype=jnp.int32)
    away = ((order & 1) << 5) | (((order >> 3) & 3) << 3) | (((order >> 1) & 3) << 1) | (order >> 5)
    blocks = away ^ place

    here, phase = jnp.stack([section, place % 2]), (place % 4).reshape(1)
    piece = partner(run_piece(blocks, weight))
    across = hop(out_cotangent)

    image_id = jnp.minimum(3 * (place // 4) + place % 4, positions.shape[0] - 1)
    begin = positions[image_id]
    half = width // 2
    feature = (blocks[:, None] * (width // N_SEQ) + jnp.arange(width // N_SEQ)[None, :]).reshape(-1)
    rates = jnp.exp((feature % half).astype(F32) * (-math.log(10000.0) / half))
    is_sin = (feature < half)[None, :]
    steps = jnp.arange(HALF, dtype=jnp.int32)
    row_angle = (begin + HALF * steps).astype(F32)[:, None] * rates[None, :]
    col_angle = steps.astype(F32)[:, None] * rates[None, :]
    row_sin, row_cos = jnp.sin(row_angle), jnp.cos(row_angle)
    row_one = jnp.where(is_sin, row_sin, row_cos)
    row_two = jnp.where(is_sin, row_cos, -row_sin)
    col_cos, col_sin = jnp.cos(col_angle), jnp.sin(col_angle)

    codes = (row_one, row_two, col_cos, col_sin)

    def first_convolutions(after, kernels):
        rows, late, beside = run_rows(here, phase, features, across, after)
        image = run_image(phase, rows, beside_swap(late), flip(beside, CORE))
        return [run_start(here, image, kernels, turned=turned) for turned in (False, True)]

    near, kernels, skip_field, start = gather_partner(
        here, piece, kernel, codes, across, first_convolutions
    )
    far = flip(near, CORE)
    skip_recv = hop(skip_field)

    tokens, active, first_lift, second_field = run_forward(
        here, blocks, skip_field, weight, near, far, codes, kernels
    )
    second_back, side, patch = run_second_pair(
        here, blocks, hop(second_field), skip_recv, start, weight, near, far, kernels
    )
    prior = jnp.where(first_pair, active, side)
    keep, send, patch = run_back(
        here, hop(second_back), skip_field, first_lift, tokens, prior, patch, near, far,
        kernels,
    )

    summed = run_sum(run_partial(keep, flip(send, CORE), patch, flip(patch, CORE)))
    tokens_in_all = positions.shape[0] * HALF * HALF
    return (summed * (1.0 / math.sqrt(tokens_in_all)))[None]


def solution(mesh):
    in_specs = (
        P("seq", None, None),
        P("section", None, None, None, None),
        P("section", None, None),
        P(),
        P("seq", None, None),
    )
    out_specs = P("section", "seq", None)
    return jax.shard_map(
        on_device, mesh=mesh, in_specs=in_specs, out_specs=out_specs, check_vma=False
    )
```
